32 devices in a mesh: heads: 8 (over y, x, core), keys: 4 (over z).
Axes of the slice: x: 2, y: 2, z: 4, core: 2. Of those that a mesh axis runs over, the one named last changes fastest.
Arguments:
- main_query: bfloat16 [128, 128, 576], P(None, 'heads'), may hold values from -5 to 5
- latent_keys: bfloat16 [8192, 576], P('keys'), may hold values from -16 to 16
- index_query: bfloat16 [128, 64, 128], P('heads'), may hold values from -1 to 1
- index_keys: bfloat16 [8192, 128], P('keys'), may hold values from -20 to 20
- index_weight: float32 [128, 64], P('heads'), may hold values from -0.15 to 1
- query_pos: int32 [128], replicated, may hold values from 1024 to 8191, as said below
- kl_weight: float32 [128], P('heads'), may hold values from 2 to 16
Outputs:
- index_query_grad: float32 [128, 64, 128], P('heads')
- index_key_grad: float32 [8192, 128], P('keys')
- index_weight_grad: float32 [128, 64], P('heads')
The draws below stay inside these ranges and needn't reach their ends.
Inputs may be any that keep to these rules, and one draw needn't show every extreme that they name: Query q sees the keys at positions 0 to query_pos[q]; some query sees all 8192 keys and some sees exactly the first 1025.
All inputs are finite; a program needn't handle non-finite values.
Results may differ from the reference program's by a relative error of at most 0.005.
Values sent between devices are 32-bit elements; how exact they have to be, the bound alone decides.
No kernel may reach another device: no remote copies, remote signals or barrier semaphores. Data moves between devices by JAX's collectives and lax.ppermute only.
A program may use at most 128 MiB of HBM per device.

```python
import math
import jax
import jax.numpy as jnp
from jax import lax

H = 128
D = 576
HI = 64
DI = 128
QROW_DEV = 16
Q = 128
KEYS = 8192


def row_scales(key, shape, lower, upper):
    return jnp.exp(jax.random.uniform(key, shape, jnp.float32, math.log(lower), math.log(upper)))


def draw_latent_keys(key, part):
    base_key = jax.random.fold_in(key, 101)
    scales = row_scales(jax.random.fold_in(base_key, 1), (KEYS, 1), 0.3, 3.0)
    values = jax.random.truncated_normal(jax.random.fold_in(base_key, 2), -5.0, 5.0, (KEYS, D), jnp.float32) * scales
    return values.astype(jnp.bfloat16)


def draw_main_query(key, part):
    base_key = jax.random.fold_in(key, 102)
    scales = row_scales(jax.random.fold_in(base_key, 1), (Q, H, 1), 0.03, 0.3)
    values = jax.random.truncated_normal(jax.random.fold_in(base_key, 2), -5.0, 5.0, (Q, H, D), jnp.float32) * scales
    return values.astype(jnp.bfloat16)


def draw_index_keys(key, part):
    base_key = jax.random.fold_in(key, 103)
    scales = row_scales(jax.random.fold_in(base_key, 1), (KEYS, 1), 0.4, 4.0)
    values = jax.random.truncated_normal(jax.random.fold_in(base_key, 2), -5.0, 5.0, (KEYS, DI), jnp.float32) * scales
    return values.astype(jnp.bfloat16)


def draw_index_query(key, part):
    base_key = jax.random.fold_in(key, 104)
    values = jax.random.truncated_normal(jax.random.fold_in(base_key, 2), -5.0, 5.0, (Q, HI, DI), jnp.float32) * DI ** (-0.5)
    return values.astype(jnp.bfloat16)


def draw_index_weight(key, part):
    base_key = jax.random.fold_in(key, 105)
    values = jax.random.truncated_normal(jax.random.fold_in(base_key, 2), -5.0, 5.0, (Q, HI), jnp.float32) * 0.03
    return values.astype(jnp.float32)


def draw_query_pos(key, part):
    values = jax.random.randint(jax.random.fold_in(key, 201), (Q,), KEYS // 8, KEYS)
    values = values.at[0].set(KEYS - 1)
    values = values.at[1].set(KEYS // 8)
    return values.astype(jnp.int32)


def level_of(rng, extent, split, smallest, high):
    def one(axis_at, parts):
        heights = jax.random.uniform(jax.random.fold_in(jax.random.fold_in(rng, 6), axis_at), (parts,), jnp.float32, smallest / len(split), high / len(split))
        return jnp.repeat(jnp.exp(heights), extent[axis_at] // parts).reshape((-1,) + (1,) * (len(extent) - axis_at - 1))

    level = one(*split[0])
    for cut in split[1:]:
        level = level * one(*cut)
    return level


def setup_inputs(seed: int = 0) -> dict:
    key_of = jax.random.split(jax.random.key(seed), 8)
    return {
        "main_query": draw_main_query(jax.random.fold_in(key_of[7], 71), 0),
        "latent_keys": draw_latent_keys(jax.random.fold_in(key_of[7], 71), 0),
        "index_query": draw_index_query(jax.random.fold_in(key_of[7], 71), 0),
        "index_keys": draw_index_keys(jax.random.fold_in(key_of[7], 71), 0),
        "index_weight": draw_index_weight(jax.random.fold_in(key_of[7], 71), 0),
        "query_pos": draw_query_pos(jax.random.fold_in(key_of[7], 71), 0),
        "kl_weight": jnp.clip(jnp.exp(math.log(16.0) - 2.0794415 * jax.random.uniform(key_of[6], (Q,), jnp.float32) ** level_of(key_of[6], (Q,), ((0, 8),), -0.2, 0.2)), 2.0, 16.0),
    }


softmax_scale = 192.0 ** -0.5
masked_fill = -1e30


def reference(main_query, latent_keys, index_query, index_keys, index_weight, query_pos, kl_weight):
    key_index = jnp.arange(KEYS, dtype=jnp.int32)
    visible = key_index[None, :] <= query_pos[:, None].astype(jnp.int32)
    query_total = query_pos.shape[0]

    def head_step(summed, query_head):
        scores = jnp.dot(query_head, latent_keys.T, preferred_element_type=jnp.float32) * softmax_scale
        scores = jnp.where(visible, scores, masked_fill)
        maxima = jnp.max(scores, axis=1, keepdims=True)
        weights = jnp.where(visible, jnp.exp(scores - maxima), 0.0)
        return summed + weights / jnp.sum(weights, axis=1, keepdims=True), None

    summed, _ = lax.scan(head_step, jnp.zeros((query_total, KEYS), jnp.float32), jnp.swapaxes(main_query, 0, 1))
    target = summed / H

    blocks = query_total // QROW_DEV

    def block_step(key_grad, inputs):
        query_block, weight_block, visible_block, target_block, kl_block = inputs
        logits = jnp.dot(query_block.reshape(QROW_DEV * HI, DI), index_keys.T, preferred_element_type=jnp.float32)
        logits = logits.reshape(QROW_DEV, HI, KEYS)
        active = jnp.maximum(logits, 0.0)
        iscores = jnp.einsum("qj,qjk->qk", weight_block, active, precision=lax.Precision.HIGHEST)
        iscores = jnp.where(visible_block, iscores, masked_fill)
        maxima = jnp.max(iscores, axis=1, keepdims=True)
        weights = jnp.where(visible_block, jnp.exp(iscores - maxima), 0.0)
        iprobs = weights / jnp.sum(weights, axis=1, keepdims=True)
        delta = kl_block[:, None] * (iprobs - target_block)
        weight_grad = jnp.einsum("qk,qjk->qj", delta, active, precision=lax.Precision.HIGHEST)
        slopes = jnp.where(logits > 0.0, delta[:, None, :] * weight_block[:, :, None], 0.0).astype(jnp.bfloat16)
        flattened = slopes.reshape(QROW_DEV * HI, KEYS)
        query_grad = jnp.dot(flattened, index_keys, preferred_element_type=jnp.float32).reshape(QROW_DEV, HI, DI)
        key_part = lax.dot_general(flattened, query_block.reshape(QROW_DEV * HI, DI), (((0,), (0,)), ((), ())), preferred_element_type=jnp.float32)
        return key_grad + key_part, (query_grad, weight_grad)

    inputs = (
        index_query.reshape(blocks, QROW_DEV, HI, DI),
        index_weight.reshape(blocks, QROW_DEV, HI),
        visible.reshape(blocks, QROW_DEV, KEYS),
        target.reshape(blocks, QROW_DEV, KEYS),
        kl_weight.reshape(blocks, QROW_DEV),
    )
    key_grad, (query_grad, weight_grad) = lax.scan(block_step, jnp.zeros((KEYS, DI), jnp.float32), inputs)
    return query_grad.reshape(query_total, HI, DI), key_grad, weight_grad.reshape(query_total, HI)
```

```python
import math

import jax
import jax.numpy as jnp
from jax import lax
from jax.experimental import pallas as pl
from jax.experimental.pallas import tpu as pltpu
from jax.sharding import PartitionSpec as P

H = 128

LOG2E = math.log2(math.e)
score_scale = 192.0 ** (-0.5) * LOG2E
masked_fill = -1e30
never_masked = 3e38

VMEM_LIMIT = 56 * 1024 * 1024
F32 = jnp.float32
BF16 = jnp.bfloat16


def params(**more):
    return pltpu.CompilerParams(vmem_limit_bytes=VMEM_LIMIT, **more)


def whole_spec(array):
    rank = len(array.shape)
    return pl.BlockSpec(array.shape, lambda *_: (0,) * rank)


def smem_spec():
    return pl.BlockSpec(memory_space=pltpu.SMEM)


def shape_of(dims, dtype=F32):
    return jax.ShapeDtypeStruct(dims, dtype)


def tile_of(extent, wanted):
    return wanted if extent % wanted == 0 else extent


def index_forward(place, row_pos, index_query, index_keys, index_weight, lanes):
    rows, heads, width = index_query.shape
    keys = index_keys.shape[0]
    tile = tile_of(keys, 512)

    def body(place_ref, pos_ref, query_ref, keys_ref, weight_ref, score_ref, lse_ref, wiq_ref):
        columns = weight_ref[...].T
        flat = query_ref[...].reshape(rows * heads, width)
        for row in range(rows):
            piece = query_ref[row].astype(F32) * columns[:, row : row + 1]
            wiq_ref[:, row * heads : (row + 1) * heads] = piece.T.astype(BF16)
        for at in range(0, keys, tile):
            logits = lax.dot_general(
                flat, keys_ref[at : at + tile, :], (((1,), (1,)), ((), ())), preferred_element_type=F32
            )
            index = place_ref[0] + at + lax.broadcasted_iota(jnp.int32, (1, tile), 1)
            for row in range(rows):
                active = jnp.maximum(logits[row * heads : (row + 1) * heads, :], 0.0)
                summed = jnp.sum(active * columns[:, row : row + 1], axis=0, keepdims=True)
                seen = index <= pos_ref[row]
                score_ref[row : row + 1, at : at + tile] = jnp.where(seen, summed * LOG2E, masked_fill)
        scores = score_ref[...]
        top = jnp.max(scores, axis=1, keepdims=True)
        total = jnp.sum(jnp.exp2(scores - top), axis=1, keepdims=True)
        lse_ref[...] = jnp.broadcast_to(top + jnp.log2(total), lse_ref.shape)

    operands = (place, row_pos, index_query, index_keys, index_weight)
    return pl.pallas_call(
        body,
        out_shape=(shape_of((rows, keys)), shape_of((rows, lanes)), shape_of((width, rows * heads), BF16)),
        in_specs=[smem_spec(), smem_spec()] + [whole_spec(a) for a in operands[2:]],
        out_specs=(
            pl.BlockSpec((rows, keys), lambda: (0, 0)),
            pl.BlockSpec((rows, lanes), lambda: (0, 0)),
            pl.BlockSpec((width, rows * heads), lambda: (0, 0)),
        ),
        compiler_params=params(),
        name="index_forward",
    )(*operands)


def main_scores(place, pos, query_t, keys_t, index_lse):
    head_local, feature, queries = query_t.shape
    keys = keys_t.shape[1]
    per = 256 // queries if queries < 256 and head_local % (256 // queries) == 0 else 1
    lanes = per * queries
    blocks = head_local // per
    tile = tile_of(keys, 512)
    tiles = keys // tile
    rows = index_lse.shape[0]

    def body(place_ref, pos_ref, query_ref, keys_ref, lse_ref, prob_ref, top_ref, stat_ref, key_rows, bias):
        step = pl.program_id(0)

        @pl.when(step == 0)
        def _():
            for at in range(0, keys, tile):
                key_rows[at : at + tile, :] = keys_ref[:, at : at + tile].T
            index = place_ref[0] + lax.broadcasted_iota(jnp.int32, (keys, queries), 0)
            bias[...] = jnp.where(index <= pos_ref[...], never_masked, masked_fill)
            stat_ref[blocks:, :] = lse_ref[...]

        weights = jnp.concatenate([query_ref[i] for i in range(per)], axis=1)
        tops, totals = [], []
        for t in range(tiles):
            span = slice(t * tile, (t + 1) * tile)
            scores = jnp.dot(key_rows[span, :], weights, preferred_element_type=F32)
            limit = bias[span, :]
            scores = jnp.minimum(scores, jnp.concatenate([limit] * per, axis=1))
            top = jnp.max(scores, axis=0, keepdims=True)
            prob = jnp.exp2((scores - top) * score_scale)
            tops.append(top * score_scale)
            totals.append(jnp.sum(prob, axis=0, keepdims=True))
            prob_ref[0, span, :] = prob.astype(BF16)
        best = tops[0]
        for top in tops[1:]:
            best = jnp.maximum(best, top)
        total = sum(s * jnp.exp2(top - best) for s, top in zip(totals, tops))
        for t in range(tiles):
            top_ref[0, t : t + 1, :] = tops[t]
        stat_ref[pl.ds(step, 1), :] = best + jnp.log2(total)

    return pl.pallas_call(
        body,
        grid=(blocks,),
        out_shape=(
            shape_of((blocks, keys, lanes), BF16),
            shape_of((blocks, tiles, lanes)),
            shape_of((blocks + rows, lanes)),
        ),
        in_specs=[
            smem_spec(),
            whole_spec(pos),
            pl.BlockSpec((per, feature, queries), lambda i: (i, 0, 0)),
            whole_spec(keys_t),
            whole_spec(index_lse),
        ],
        out_specs=(
            pl.BlockSpec((1, keys, lanes), lambda i: (i, 0, 0)),
            pl.BlockSpec((1, tiles, lanes), lambda i: (i, 0, 0)),
            pl.BlockSpec((blocks + rows, lanes), lambda i: (0, 0)),
        ),
        scratch_shapes=[pltpu.VMEM((keys, feature), BF16), pltpu.VMEM((keys, queries), F32)],
        compiler_params=params(),
        name="main_scores",
    )(place, pos, query_t, keys_t, index_lse)


def joined(stats):
    best = stats[0]
    for stat in stats[1:]:
        best = jnp.maximum(best, stat)
    return best + jnp.log2(sum(jnp.exp2(stat - best) for stat in stats))


def head_sum(place, probs, tops, stats, queries, row_local):
    blocks, keys, lanes = probs.shape
    tiles = tops.shape[1]
    tile = keys // tiles
    per = lanes // queries
    chips = queries // row_local // 2
    sub = tile_of(tile, 128)

    def body(place_ref, prob_ref, top_ref, *refs):
        stat_refs, (keep_ref, send_ref, summed) = refs[:-3], refs[-3:]
        step = pl.program_id(0)
        whole = joined([ref[:blocks, :] for ref in stat_refs])
        factors = [
            jnp.exp2(top_ref[b, pl.ds(step, 1), :] - whole[b : b + 1, :]) * (1.0 / H) for b in range(blocks)
        ]
        for at in range(0, tile, sub):
            total = None
            for b in range(blocks):
                part = prob_ref[b, at : at + sub, :].astype(F32) * factors[b]
                for i in range(per):
                    piece = part[:, i * queries : (i + 1) * queries]
                    total = piece if total is None else total + piece
            summed[:, at : at + sub] = total.T
        chip = place_ref[1] // 2
        core = place_ref[1] % 2
        for r in range(chips):
            first = (chip ^ r) * 2
            keep_ref[r] = summed[pl.ds(pl.multiple_of((first + core) * row_local, row_local), row_local), :]
            send_ref[r] = summed[pl.ds(pl.multiple_of((first + 1 - core) * row_local, row_local), row_local), :]

    half = shape_of((chips, row_local, keys))
    half_spec = pl.BlockSpec((chips, row_local, tile), lambda i: (0, 0, i))
    return pl.pallas_call(
        body,
        grid=(tiles,),
        out_shape=(half, half),
        in_specs=[smem_spec(), pl.BlockSpec((blocks, tile, lanes), lambda i: (0, i, 0)), whole_spec(tops)]
        + [whole_spec(s) for s in stats],
        out_specs=(half_spec, half_spec),
        scratch_shapes=[pltpu.VMEM((queries, tile), F32)],
        compiler_params=params(),
        name="head_sum",
    )(place, probs, tops, *stats)


def gradients(place, scores, stats, targets, kl, index_query, index_keys, wiq, key_devices, head_devices):
    rows, heads, width = index_query.shape
    keys = index_keys.shape[0]
    tile = tile_of(keys, 512)
    parts = len(targets)
    own = rows // key_devices
    chips = head_devices // 2
    chunk = keys // head_devices
    first_row = stats[0].shape[0] - rows

    def body(place_ref, score_ref, kl_ref, query_ref, keys_ref, wiq_ref, *refs):
        stat_refs, refs = refs[: len(stats)], refs[len(stats) :]
        target_refs, refs = refs[:parts], refs[parts:]
        query_outs, (keep_ref, send_ref, query_total, key_total) = refs[:key_devices], refs[key_devices:]
        whole = joined([ref[first_row:, :1] for ref in stat_refs])
        flat = query_ref[...].reshape(rows * heads, width)
        for at in range(0, keys, tile):
            span = slice(at, at + tile)
            target = target_refs[0][:, span]
            for ref in target_refs[1:]:
                target = target + ref[:, span]
            delta = kl_ref[...] * (jnp.exp2(score_ref[:, span] - whole) - target)
            logits = lax.dot_general(
                flat, keys_ref[span, :], (((1,), (1,)), ((), ())), preferred_element_type=F32
            ).astype(BF16)
            delta = delta.astype(BF16)
            pieces = []
            for row in range(rows):
                pieces.append(
                    jnp.where(
                        logits[row * heads : (row + 1) * heads, :] > 0,
                        jnp.broadcast_to(delta[row : row + 1, :], (heads, tile)),
                        jnp.zeros((), BF16),
                    )
                )
            slopes = jnp.concatenate(pieces, axis=0)
            part = jnp.dot(slopes, keys_ref[span, :], preferred_element_type=F32)
            if at == 0:
                query_total[...] = part
            else:
                query_total[...] += part
            key_part = jnp.dot(wiq_ref[...], slopes, preferred_element_type=F32)
            key_total[span, :] = key_part.T
        chip, core, z = place_ref[1] // 2, place_ref[1] % 2, place_ref[2]
        for r in range(chips):
            first = (chip ^ r) * 2
            keep_ref[r] = key_total[pl.ds(pl.multiple_of((first + core) * chunk, chunk), chunk), :]
            send_ref[r] = key_total[pl.ds(pl.multiple_of((first + 1 - core) * chunk, chunk), chunk), :]
        for r in range(key_devices):
            size = own * heads
            query_outs[r][...] = query_total[pl.ds(pl.multiple_of((z ^ r) * size, size), size), :]

    half = shape_of((chips, chunk, width))
    outs = tuple(shape_of((own * heads, width)) for _ in range(key_devices)) + (half, half)
    operands = (scores, kl, index_query, index_keys, wiq, *stats, *targets)
    return pl.pallas_call(
        body,
        out_shape=outs,
        in_specs=[smem_spec()] + [whole_spec(a) for a in operands],
        out_specs=tuple(whole_spec(o) for o in outs),
        scratch_shapes=[pltpu.VMEM((rows * heads, width), F32), pltpu.VMEM((keys, width), F32)],
        compiler_params=params(),
        name="gradients",
    )(place, *operands)


def finish_query(place, pieces, index_query, index_weight):
    rows, heads, width = index_query.shape
    own = rows // len(pieces)

    def body(place_ref, query_ref, weight_ref, *refs):
        piece_refs, (query_out, weight_out, columns) = refs[:-3], refs[-3:]
        z = place_ref[2]
        columns[...] = weight_ref[...].T
        weight_columns = columns[...]
        for r, ref in enumerate(piece_refs):
            first = (z ^ r) * own
            for i in range(own):
                row = first + i
                piece = ref[i * heads : (i + 1) * heads, :]
                picked = lax.broadcasted_iota(jnp.int32, (heads, rows), 1) == row
                column = jnp.sum(jnp.where(picked, weight_columns, 0.0), axis=1, keepdims=True)
                query_out[row] = piece * column
                summed = jnp.sum(piece * query_ref[row].astype(F32), axis=1, keepdims=True)
                weight_out[pl.ds(row, 1), :] = summed.T

    return pl.pallas_call(
        body,
        out_shape=(shape_of((rows, heads, width)), shape_of((rows, heads))),
        in_specs=[smem_spec(), whole_spec(index_query), whole_spec(index_weight)]
        + [whole_spec(p) for p in pieces],
        out_specs=(
            pl.BlockSpec((rows, heads, width), lambda: (0, 0, 0)),
            pl.BlockSpec((rows, heads), lambda: (0, 0)),
        ),
        scratch_shapes=[pltpu.VMEM((heads, rows), F32)],
        compiler_params=params(),
        name="finish_query",
    )(place, index_query, index_weight, *pieces)


def finish_keys(place, mine, others):
    chips = len(mine)
    chunk, width = mine[0].shape

    def body(place_ref, *refs):
        out_ref = refs[-1]
        chip, core = place_ref[1] // 2, place_ref[1] % 2
        for r in range(chips):
            first = (chip ^ r) * 2
            out_ref[pl.ds(pl.multiple_of((first + core) * chunk, chunk), chunk), :] = refs[r][...]
            out_ref[pl.ds(pl.multiple_of((first + 1 - core) * chunk, chunk), chunk), :] = refs[chips + r][...]

    out = shape_of((2 * chips * chunk, width))
    return pl.pallas_call(
        body,
        out_shape=out,
        in_specs=[smem_spec()] + [whole_spec(a) for a in (*mine, *others)],
        out_specs=whole_spec(out),
        compiler_params=params(),
        name="finish_keys",
    )(place, *mine, *others)


def shards(main_query, latent_keys, index_query, index_keys, index_weight, query_pos, kl_weight):
    queries = main_query.shape[0]
    key_local = latent_keys.shape[0]
    row_local = index_query.shape[0]
    head_devices = lax.axis_size("heads")
    key_devices = lax.axis_size("keys")
    chips = head_devices // 2
    at_head = lax.axis_index("heads")
    at_key = lax.axis_index("keys")
    place = jnp.stack([at_key * key_local, at_head, at_key]).astype(jnp.int32)
    row_pos = lax.dynamic_slice_in_dim(query_pos, at_head * row_local, row_local)

    def across(axis, count, value, bits):
        return lax.ppermute(value, axis, [(i, i ^ bits) for i in range(count)])

    def to_keys(value, bits):
        return across("keys", key_devices, value, bits)

    def to_heads(value, bits):
        return across("heads", head_devices, value, bits)

    lanes = 256 if queries < 256 else queries
    scores, index_lse, wiq = index_forward(place, row_pos, index_query, index_keys, index_weight, lanes)
    probs, tops, stat = main_scores(
        place, query_pos[None, :], main_query.transpose(1, 2, 0), latent_keys.T, index_lse
    )
    stats = [stat] + [to_keys(stat, bits) for bits in reversed(range(1, key_devices))]
    keep, send = head_sum(place, probs, tops, stats, queries, row_local)
    other = to_heads(send, 1)
    sums = [keep[r] + other[r] for r in range(chips)]
    targets = [sums[0]] + [to_heads(sums[r], 2 * r) for r in reversed(range(1, chips))]
    *query_parts, keep, send = gradients(
        place, scores, stats, targets, kl_weight[:, None], index_query, index_keys, wiq, key_devices, head_devices
    )
    other = to_heads(send, 1)
    query_own = query_parts[0]
    arrived = [to_keys(query_parts[r], r) for r in reversed(range(1, key_devices))]
    for part in arrived:
        query_own = query_own + part
    sums = [keep[r] + other[r] for r in range(chips)]
    key_own = sums[0]
    for part in [to_heads(sums[r], 2 * r) for r in reversed(range(1, chips))]:
        key_own = key_own + part
    query_pieces = [query_own] + [to_keys(query_own, r) for r in range(1, key_devices)]
    mine = [key_own] + [to_heads(key_own, 2 * r) for r in range(1, chips)]
    others = [to_heads(piece, 1) for piece in mine]
    query_grad, weight_grad = finish_query(place, query_pieces, index_query, index_weight)
    key_grad = finish_keys(place, mine, others)
    return query_grad, key_grad, weight_grad


def solution(mesh):
    placed = (
        P(None, "heads", None),
        P("keys", None),
        P("heads", None, None),
        P("keys", None),
        P("heads", None),
        P(),
        P("heads"),
    )
    return jax.shard_map(
        shards,
        mesh=mesh,
        in_specs=placed,
        out_specs=(P("heads", None, None), P("keys", None), P("heads", None)),
        check_vma=False,
    )
```

```python
import math

import jax
import jax.numpy as jnp
from jax import lax
from jax.experimental import pallas as pl
from jax.experimental.pallas import tpu as pltpu
from jax.sharding import PartitionSpec as P

H = 128

LOG2E = math.log2(math.e)
score_scale = 192.0 ** (-0.5) * LOG2E
masked_fill = -1e30

F32 = jnp.float32
BF16 = jnp.bfloat16
MIB = 1024 * 1024

vmem_spec = pl.BlockSpec(memory_space=pltpu.VMEM)
any_spec = pl.BlockSpec(memory_space=pl.ANY)


def in_vmem(array):
    return pltpu.with_memory_space_constraint(array, pltpu.VMEM)


def in_hbm(array):
    return pltpu.with_memory_space_constraint(array, pltpu.HBM)


def vmem_call(body, name, outs, operands, scratch=(), out_specs=None, limit=32 * MIB, cost=0):
    several = isinstance(outs, (tuple, list))
    if out_specs is None:
        out_specs = tuple(vmem_spec for _ in outs) if several else vmem_spec
    return pl.pallas_call(
        body,
        out_shape=outs,
        in_specs=[vmem_spec] * len(operands),
        out_specs=out_specs,
        scratch_shapes=list(scratch),
        compiler_params=pltpu.CompilerParams(vmem_limit_bytes=limit),
        cost_estimate=pl.CostEstimate(flops=cost, bytes_accessed=0, transcendentals=0),
        name=name,
    )(*[in_vmem(a) for a in operands])


def tile_of(extent, wanted):
    return wanted if extent % wanted == 0 else extent


def rows_of(ref, first, count):
    return ref[pl.ds(pl.multiple_of(first, count), count)]


def head_place():
    at = lax.axis_index("heads")
    return at // 2, at % 2


def index_forward(query_pos, index_query, index_keys, index_weight, groups, after):
    rows, heads, width = index_query.shape
    keys = index_keys.shape[0]
    tile = tile_of(keys, 256)
    own = rows // groups

    def body(pos_ref, query_ref, keys_ref, weight_ref, _, score_ref, lse_ref, wiq_ref):
        columns = weight_ref[...].T
        flat = query_ref[...].reshape(rows * heads, width)
        for row in range(rows):
            piece = query_ref[row].astype(F32) * columns[:, row : row + 1]
            wiq_ref[row // own, :, (row % own) * heads : (row % own + 1) * heads] = piece.T.astype(BF16)
        first_key = lax.axis_index("keys") * keys
        first_row = lax.axis_index("heads") * rows
        for at in range(0, keys, tile):
            logits = lax.dot_general(
                flat, keys_ref[at : at + tile, :], (((1,), (1,)), ((), ())), preferred_element_type=F32
            )
            index = first_key + at + lax.broadcasted_iota(jnp.int32, (1, tile), 1)
            for row in range(rows):
                active = jnp.maximum(logits[row * heads : (row + 1) * heads, :], 0.0)
                summed = jnp.sum(active * columns[:, row : row + 1], axis=0, keepdims=True)
                seen = index <= pos_ref[first_row + row]
                score_ref[row : row + 1, at : at + tile] = jnp.where(seen, summed * LOG2E, masked_fill)
        scores = score_ref[...]
        top = jnp.max(scores, axis=1, keepdims=True)
        total = jnp.sum(jnp.exp2(scores - top), axis=1, keepdims=True)
        lse_ref[...] = jnp.broadcast_to(top + jnp.log2(total), lse_ref.shape)

    return pl.pallas_call(
        body,
        out_shape=(
            pltpu.VMEM((rows, keys), F32),
            pltpu.VMEM((rows, 128), F32),
            pltpu.VMEM((groups, width, own * heads), BF16),
        ),
        in_specs=[pl.BlockSpec(memory_space=pltpu.SMEM)] + [vmem_spec] * 4,
        out_specs=(vmem_spec,) * 3,
        compiler_params=pltpu.CompilerParams(vmem_limit_bytes=32 * MIB),
        cost_estimate=pl.CostEstimate(flops=10**9, bytes_accessed=0, transcendentals=0),
        name="index_forward",
    )(query_pos, *[in_vmem(a) for a in (index_query, index_keys, index_weight, after)])


def main_scores(pos, query_t, keys_t):
    head_local, feature, queries = query_t.shape
    keys = keys_t.shape[1]
    per = 256 // queries if queries < 256 and head_local % (256 // queries) == 0 else 1
    lanes = per * queries
    blocks = head_local // per
    tile = tile_of(keys, 128)
    tiles = keys // tile
    mask_at = -(-feature // 128) * 128
    depth = mask_at + -(-queries // 128) * 128

    def body(pos_ref, query_ref, keys_ref, prob_ref, top_ref, stat_ref, key_rows, weights):
        step = pl.program_id(0)

        @pl.when(step == 0)
        def _():
            chunk = tile_of(keys, 512)
            for at in range(0, keys, chunk):
                key_rows[at : at + chunk, :feature] = keys_ref[:, at : at + chunk].T
            if mask_at > feature:
                key_rows[:, feature:mask_at] = jnp.zeros((keys, mask_at - feature), BF16)
                weights[feature:mask_at, :] = jnp.zeros((mask_at - feature, lanes), BF16)
            index = lax.axis_index("keys") * keys + lax.broadcasted_iota(jnp.int32, (keys, queries), 0)
            hidden = jnp.where(index <= pos_ref[...], 0.0, masked_fill).astype(BF16)
            key_rows[:, mask_at : mask_at + queries] = hidden
            at_row = lax.broadcasted_iota(jnp.int32, (depth - mask_at, lanes), 0)
            at_lane = lax.broadcasted_iota(jnp.int32, (depth - mask_at, lanes), 1)
            weights[mask_at:, :] = jnp.where(at_row == at_lane % queries, 1.0, 0.0).astype(BF16)
            if depth > mask_at + queries:
                key_rows[:, mask_at + queries :] = jnp.zeros((keys, depth - mask_at - queries), BF16)

        for i in range(per):
            weights[:feature, i * queries : (i + 1) * queries] = query_ref[i]
        tops, totals = [], []
        for t in range(tiles):
            span = slice(t * tile, (t + 1) * tile)
            scores = jnp.dot(key_rows[span, :], weights[...], preferred_element_type=F32)
            top = jnp.max(scores, axis=0, keepdims=True)
            prob = jnp.exp2((scores - top) * score_scale)
            top = top * score_scale
            tops.append(top)
            totals.append(jnp.sum(prob, axis=0, keepdims=True))
            prob_ref[step, span, :] = prob.astype(prob_ref.dtype)
            top_ref[step, t : t + 1, :] = top
        best = tops[0]
        for top in tops[1:]:
            best = jnp.maximum(best, top)
        total = sum(s * jnp.exp2(top - best) for s, top in zip(totals, tops))
        stat_ref[pl.ds(step, 1), :] = best + jnp.log2(total)

    return pl.pallas_call(
        body,
        grid=(blocks,),
        out_shape=(
            pltpu.VMEM((blocks, keys, lanes), BF16),
            pltpu.VMEM((blocks, tiles, lanes), F32),
            pltpu.VMEM((blocks, lanes), F32),
        ),
        in_specs=[
            pl.BlockSpec((1, queries), lambda i: (0, 0)),
            pl.BlockSpec((per, feature, queries), lambda i: (i, 0, 0)),
            pl.BlockSpec((feature, keys), lambda i: (0, 0)),
        ],
        out_specs=(vmem_spec,) * 3,
        scratch_shapes=[pltpu.VMEM((keys, depth), BF16), pltpu.VMEM((depth, lanes), BF16)],
        compiler_params=pltpu.CompilerParams(vmem_limit_bytes=28 * MIB),
        name="main_scores",
    )(pos, in_hbm(query_t), in_hbm(keys_t))


def joined(stats):
    best = stats[0]
    for stat in stats[1:]:
        best = jnp.maximum(best, stat)
    return best + jnp.log2(sum(jnp.exp2(stat - best) for stat in stats))


def head_sum(probs, tops, stats, queries, row_local):
    blocks, keys, lanes = probs.shape
    tiles = tops.shape[1]
    tile = keys // tiles
    per = lanes // queries
    chips = queries // row_local // 2

    def body(prob_ref, top_ref, *refs):
        stat_refs, (keep_ref, send_ref, summed) = refs[:-3], refs[-3:]
        whole = joined([ref[...] for ref in stat_refs])
        factors = [jnp.exp2(top_ref[b] - whole[b : b + 1, :]) * (1.0 / H) for b in range(blocks)]
        for t in range(tiles):
            span = slice(t * tile, (t + 1) * tile)
            total = None
            for b in range(blocks):
                part = prob_ref[b, span, :].astype(F32) * factors[b][t : t + 1, :]
                for i in range(per):
                    piece = part[:, i * queries : (i + 1) * queries]
                    total = piece if total is None else total + piece
            summed[:, span] = total.T
        chip, core = head_place()
        for r in range(chips):
            first = (chip ^ r) * 2
            keep_ref[r] = rows_of(summed, (first + core) * row_local, row_local)
            send_ref[r] = rows_of(summed, (first + 1 - core) * row_local, row_local)

    half = pltpu.VMEM((chips, row_local, keys), F32)
    return vmem_call(
        body, "head_sum", (half, half), (probs, tops, *stats), [pltpu.VMEM((queries, keys), F32)], cost=10**9
    )


def add_stacks(left, right):
    count = left.shape[0]

    def body(left_ref, right_ref, *outs):
        for r in range(count):
            outs[r][...] = left_ref[r] + right_ref[r]

    return vmem_call(
        body, "add_stacks", tuple(pltpu.VMEM(left.shape[1:], F32) for _ in range(count)), (left, right)
    )


def add_all(parts):
    def body(*refs):
        total = refs[0][...]
        for ref in refs[1:-1]:
            total = total + ref[...]
        refs[-1][...] = total

    return vmem_call(body, "add_all", pltpu.VMEM(parts[0].shape, F32), parts)


def deltas(scores, stats, targets, kl, groups):
    rows, keys = scores.shape
    own = rows // groups

    def body(score_ref, kl_ref, *refs):
        stat_refs, target_refs, out_ref = refs[: len(stats)], refs[len(stats) : -1], refs[-1]
        whole = joined([ref[:, :1] for ref in stat_refs])
        target = target_refs[0][...]
        for ref in target_refs[1:]:
            target = target + ref[...]
        delta = kl_ref[...] * (jnp.exp2(score_ref[...] - whole) - target)
        for g in range(groups):
            out_ref[g] = delta[g * own : (g + 1) * own, :]

    return vmem_call(body, "deltas", pltpu.VMEM((groups, own, keys), F32), (scores, kl, *stats, *targets))


def query_part(r, delta, index_query, index_keys):
    groups, own, keys = delta.shape
    heads, width = index_query.shape[1:]
    tile = tile_of(keys, 512)

    def body(delta_ref, query_ref, keys_ref, slope_ref, out_ref):
        group = lax.axis_index("keys") ^ r
        flat = query_ref[pl.ds(group * own, own)].reshape(own * heads, width)
        for at in range(0, keys, tile):
            span = slice(at, at + tile)
            logits = lax.dot_general(
                flat, keys_ref[span, :], (((1,), (1,)), ((), ())), preferred_element_type=F32
            ).astype(BF16)
            delta_rows = delta_ref[group, :, span]
            for row in range(own):
                line = jnp.broadcast_to(delta_rows[row : row + 1, :], (heads, tile)).astype(BF16)
                part = slice(row * heads, (row + 1) * heads)
                slope_ref[part, span] = jnp.where(logits[part, :] > 0, line, jnp.zeros((), BF16))
        out_ref[...] = jnp.dot(slope_ref[...], keys_ref[...], preferred_element_type=F32)

    outs = (pltpu.VMEM((own * heads, keys), BF16), pltpu.VMEM((own * heads, width), F32))
    return vmem_call(body, "query_part", outs, (delta, index_query, index_keys), cost=3 * 10**8)


def key_part(slopes, wiq, head_devices):
    groups, width = wiq.shape[:2]
    keys = slopes[0].shape[1]
    tile = tile_of(keys, 512)
    chips = head_devices // 2
    chunk = keys // head_devices

    def body(wiq_ref, *refs):
        slope_refs, (keep_ref, send_ref, total) = refs[:groups], refs[groups:]
        z = lax.axis_index("keys")
        for at in range(0, keys, tile):
            span = slice(at, at + tile)
            summed = None
            for r in range(groups):
                part = jnp.dot(wiq_ref[z ^ r], slope_refs[r][:, span], preferred_element_type=F32)
                summed = part if summed is None else summed + part
            total[span, :] = summed.T
        chip, core = head_place()
        for r in range(chips):
            first = (chip ^ r) * 2
            keep_ref[r] = rows_of(total, (first + core) * chunk, chunk)
            send_ref[r] = rows_of(total, (first + 1 - core) * chunk, chunk)

    half = pltpu.VMEM((chips, chunk, width), F32)
    return vmem_call(
        body, "key_part", (half, half), (wiq, *slopes), [pltpu.VMEM((keys, width), F32)], cost=10**9
    )


def own_rows(parts, index_query, index_weight):
    rows, heads, width = index_query.shape
    size = parts[0].shape[0]
    own = size // heads
    extra = -(-own // 8) * 8

    def body(query_ref, weight_ref, *refs):
        first = lax.axis_index("keys") * own
        part_refs, out_ref = refs[:-1], refs[-1]
        columns = weight_ref[...].T
        lane = lax.broadcasted_iota(jnp.int32, (heads, rows), 1)
        for i in range(own):
            span = slice(i * heads, (i + 1) * heads)
            total = part_refs[0][span, :]
            for ref in part_refs[1:]:
                total = total + ref[span, :]
            column = jnp.sum(jnp.where(lane == first + i, columns, 0.0), axis=1, keepdims=True)
            out_ref[span, :] = total * column
            summed = jnp.sum(total * query_ref[first + i].astype(F32), axis=1, keepdims=True)
            line = summed.T
            out_ref[size + i : size + i + 1, :] = jnp.concatenate(
                [line, jnp.zeros((1, width - heads), F32)], axis=1
            )
        if extra > own:
            out_ref[size + own :, :] = jnp.zeros((extra - own, width), F32)

    return vmem_call(
        body, "own_rows", pltpu.VMEM((size + extra, width), F32), (index_query, index_weight, *parts)
    )


def place_query(pieces, rows, heads):
    own = rows // len(pieces)
    size = own * heads
    width = pieces[0].shape[1]

    def body(*refs):
        piece_refs, (query_out, weight_out, sems) = refs[: len(pieces)], refs[len(pieces) :]
        z = lax.axis_index("keys")
        copies = []
        for r, ref in enumerate(piece_refs):
            at = pl.multiple_of((z ^ r) * size, size)
            copies.append(pltpu.make_async_copy(ref.at[:size], query_out.at[pl.ds(at, size)], sems.at[r]))
            copies[-1].start()
        for r, ref in enumerate(piece_refs):
            weight_out[pl.ds((z ^ r) * own, own), :] = ref[size : size + own, :heads]
        for copy in copies:
            copy.wait()

    query, weight = vmem_call(
        body,
        "place_query",
        (jax.ShapeDtypeStruct((rows * heads, width), F32), jax.ShapeDtypeStruct((rows, heads), F32)),
        pieces,
        [pltpu.SemaphoreType.DMA((len(pieces),))],
        out_specs=(any_spec, vmem_spec),
    )
    return query.reshape(rows, heads, width), weight


def place_keys(mine, others):
    chips = len(mine)
    chunk, width = mine[0].shape

    def body(*refs):
        out_ref, sems = refs[-2:]
        chip, core = head_place()
        copies = []
        for r in range(chips):
            for side in range(2):
                at = pl.multiple_of(((chip ^ r) * 2 + (core ^ side)) * chunk, chunk)
                n = side * chips + r
                copies.append(pltpu.make_async_copy(refs[n], out_ref.at[pl.ds(at, chunk)], sems.at[n]))
                copies[-1].start()
        for copy in copies:
            copy.wait()

    return vmem_call(
        body,
        "place_keys",
        jax.ShapeDtypeStruct((2 * chips * chunk, width), F32),
        (*mine, *others),
        [pltpu.SemaphoreType.DMA((2 * chips,))],
        out_specs=any_spec,
    )


def shards(main_query, latent_keys, index_query, index_keys, index_weight, query_pos, kl_weight):
    queries = main_query.shape[0]
    row_local, index_heads, _ = index_query.shape
    head_devices = lax.axis_size("heads")
    key_devices = lax.axis_size("keys")
    chips = head_devices // 2

    def to_keys(value, bits):
        return lax.ppermute(value, "keys", [(i, i ^ bits) for i in range(key_devices)])

    def to_heads(value, bits):
        return lax.ppermute(value, "heads", [(i, i ^ bits) for i in range(head_devices)])

    far_first = list(reversed(range(1, key_devices)))
    chips_far_first = list(reversed(range(1, chips)))

    probs, tops, stat = main_scores(query_pos[None, :], main_query.transpose(1, 2, 0), latent_keys.T)
    stats = [stat] + [to_keys(stat, bits) for bits in far_first]
    scores, index_lse, wiq = index_forward(
        query_pos, index_query, index_keys, index_weight, key_devices, stat
    )
    keep, send = head_sum(probs, tops, stats, queries, row_local)
    sums = add_stacks(keep, to_heads(send, 1))
    targets = [sums[0]] + [to_heads(sums[r], 2 * r) for r in chips_far_first]
    index_lse, _ = lax.optimization_barrier((index_lse, sums[0]))
    index_stats = [index_lse] + [to_keys(index_lse, bits) for bits in far_first]
    delta = deltas(scores, index_stats, targets, kl_weight[:, None], key_devices)

    slopes, arrived = {}, []
    for r in far_first + [0]:
        slopes[r], part = query_part(r, delta, index_query, index_keys)
        arrived.append(to_keys(part, r) if r else part)
    keep, send = key_part([slopes[r] for r in range(key_devices)], wiq, head_devices)
    sums = add_stacks(keep, to_heads(send, 1))
    key_own = add_all([sums[0]] + [to_heads(sums[r], 2 * r) for r in chips_far_first])
    query_own = own_rows(arrived, index_query, index_weight)
    pieces = [query_own] + [to_keys(query_own, r) for r in range(1, key_devices)]
    mine = [key_own] + [to_heads(key_own, 2 * r) for r in range(1, chips)]
    others = [to_heads(piece, 1) for piece in mine]
    key_grad = place_keys(mine, others)
    query_grad, weight_grad = place_query(pieces, row_local, index_heads)
    return query_grad, key_grad, weight_grad


def solution(mesh):
    placed = (
        P(None, "heads", None),
        P("keys", None),
        P("heads", None, None),
        P("keys", None),
        P("heads", None),
        P(),
        P("heads"),
    )
    return jax.shard_map(
        shards,
        mesh=mesh,
        in_specs=placed,
        out_specs=(P("heads", None, None), P("keys", None), P("heads", None)),
        check_vma=False,
    )
```

```python
import math

import jax
import jax.numpy as jnp
from jax import lax
from jax.experimental import pallas as pl
from jax.experimental.pallas import tpu as pltpu
from jax.sharding import PartitionSpec as P

H = 128

LOG2E = math.log2(math.e)
score_scale = 192.0 ** (-0.5) * LOG2E
masked_fill = -1e30

F32 = jnp.float32
BF16 = jnp.bfloat16
MIB = 1024 * 1024
SHORT = 0
LONG = 4 * 10**10

vmem_spec = pl.BlockSpec(memory_space=pltpu.VMEM)
smem_spec = pl.BlockSpec(memory_space=pltpu.SMEM)
any_spec = pl.BlockSpec(memory_space=pl.ANY)


def in_vmem(array):
    return pltpu.with_memory_space_constraint(array, pltpu.VMEM)


def in_hbm(array):
    return pltpu.with_memory_space_constraint(array, pltpu.HBM)


def vmem_call(
    body, name, outs, operands, scratch=(), out_specs=None, scalars=(), limit=12 * MIB, cost=0
):
    several = isinstance(outs, (tuple, list))
    if out_specs is None:
        out_specs = tuple(vmem_spec for _ in outs) if several else vmem_spec
    return pl.pallas_call(
        body,
        out_shape=outs,
        in_specs=[smem_spec] * len(scalars) + [vmem_spec] * len(operands),
        out_specs=out_specs,
        scratch_shapes=list(scratch),
        compiler_params=pltpu.CompilerParams(vmem_limit_bytes=limit),
        cost_estimate=pl.CostEstimate(flops=cost, bytes_accessed=0, transcendentals=0),
        name=name,
    )(*scalars, *[in_vmem(a) for a in operands])


def tile_of(extent, wanted):
    return wanted if extent % wanted == 0 else extent


def rows_of(ref, first, count):
    return ref[pl.ds(pl.multiple_of(first, count), count)]


def head_place():
    at = lax.axis_index("heads")
    return at // 2, at % 2


def index_forward(query_pos, kl, index_query, index_keys, index_weight, groups, after):
    rows, heads, width = index_query.shape
    keys = index_keys.shape[0]
    tile = tile_of(keys, 256)
    own = rows // groups

    def body(pos_ref, kl_ref, query_ref, keys_ref, weight_ref, _, score_ref, lse_ref, kl_out, wiq_ref, gate_ref):
        columns = weight_ref[...].T
        flat = query_ref[...].reshape(rows * heads, width)
        for row in range(rows):
            kl_out[row : row + 1, :] = jnp.full((1, 128), kl_ref[row], F32)
            piece = query_ref[row].astype(F32) * columns[:, row : row + 1]
            wiq_ref[row // own, :, (row % own) * heads : (row % own + 1) * heads] = piece.T.astype(BF16)
        first_key = lax.axis_index("keys") * keys
        first_row = lax.axis_index("heads") * rows
        for at in range(0, keys, tile):
            logits = lax.dot_general(
                flat, keys_ref[at : at + tile, :], (((1,), (1,)), ((), ())), preferred_element_type=F32
            )
            for g in range(groups):
                gate_ref[g, :, at : at + tile] = logits[g * own * heads : (g + 1) * own * heads, :].astype(BF16)
            index = first_key + at + lax.broadcasted_iota(jnp.int32, (1, tile), 1)
            for row in range(rows):
                active = jnp.maximum(logits[row * heads : (row + 1) * heads, :], 0.0)
                summed = jnp.sum(active * columns[:, row : row + 1], axis=0, keepdims=True)
                seen = index <= pos_ref[first_row + row]
                score_ref[row : row + 1, at : at + tile] = jnp.where(seen, summed * LOG2E, masked_fill)
        scores = score_ref[...]
        top = jnp.max(scores, axis=1, keepdims=True)
        total = jnp.sum(jnp.exp2(scores - top), axis=1, keepdims=True)
        lse_ref[...] = jnp.broadcast_to(top + jnp.log2(total), lse_ref.shape)

    return pl.pallas_call(
        body,
        out_shape=(
            pltpu.VMEM((rows, keys), F32),
            pltpu.VMEM((rows, 128), F32),
            pltpu.VMEM((rows, 128), F32),
            pltpu.VMEM((groups, width, own * heads), BF16),
            pltpu.VMEM((groups, own * heads, keys), BF16),
        ),
        in_specs=[smem_spec] * 2 + [vmem_spec] * 4,
        out_specs=(vmem_spec,) * 5,
        compiler_params=pltpu.CompilerParams(vmem_limit_bytes=16 * MIB),
        cost_estimate=pl.CostEstimate(flops=0, bytes_accessed=0, transcendentals=0),
        name="index_forward",
    )(query_pos, kl, *[in_vmem(a) for a in (index_query, index_keys, index_weight, after)])


def main_scores(pos, query_t, keys_t):
    head_local, feature, queries = query_t.shape
    keys = keys_t.shape[1]
    per = 256 // queries if queries < 256 and head_local % (256 // queries) == 0 else 1
    lanes = per * queries
    blocks = head_local // per
    tile = tile_of(keys, 128)
    tiles = keys // tile
    mask_at = -(-feature // 128) * 128
    depth = mask_at + -(-queries // 128) * 128

    def body(pos_ref, query_ref, keys_ref, prob_ref, top_ref, stat_ref, key_rows, weights):
        step = pl.program_id(0)

        @pl.when(step == 0)
        def _():
            chunk = tile_of(keys, 512)
            for at in range(0, keys, chunk):
                key_rows[at : at + chunk, :feature] = keys_ref[:, at : at + chunk].T
            if mask_at > feature:
                key_rows[:, feature:mask_at] = jnp.zeros((keys, mask_at - feature), BF16)
                weights[feature:mask_at, :] = jnp.zeros((mask_at - feature, lanes), BF16)
            index = lax.axis_index("keys") * keys + lax.broadcasted_iota(jnp.int32, (keys, queries), 0)
            hidden = jnp.where(index <= pos_ref[...], 0.0, masked_fill).astype(BF16)
            key_rows[:, mask_at : mask_at + queries] = hidden
            at_row = lax.broadcasted_iota(jnp.int32, (depth - mask_at, lanes), 0)
            at_lane = lax.broadcasted_iota(jnp.int32, (depth - mask_at, lanes), 1)
            weights[mask_at:, :] = jnp.where(at_row == at_lane % queries, 1.0, 0.0).astype(BF16)
            if depth > mask_at + queries:
                key_rows[:, mask_at + queries :] = jnp.zeros((keys, depth - mask_at - queries), BF16)

        for i in range(per):
            weights[:feature, i * queries : (i + 1) * queries] = query_ref[i]
        tops, totals = [], []
        for t in range(tiles):
            span = slice(t * tile, (t + 1) * tile)
            scores = jnp.dot(key_rows[span, :], weights[...], preferred_element_type=F32)
            top = jnp.max(scores, axis=0, keepdims=True)
            prob = jnp.exp2((scores - top) * score_scale)
            top = top * score_scale
            tops.append(top)
            totals.append(jnp.sum(prob, axis=0, keepdims=True))
            prob_ref[step, span, :] = prob.astype(prob_ref.dtype)
            top_ref[step, t : t + 1, :] = top
        best = tops[0]
        for top in tops[1:]:
            best = jnp.maximum(best, top)
        total = sum(s * jnp.exp2(top - best) for s, top in zip(totals, tops))
        stat_ref[pl.ds(step, 1), :] = best + jnp.log2(total)

    return pl.pallas_call(
        body,
        grid=(blocks,),
        out_shape=(
            pltpu.VMEM((blocks, keys, lanes), BF16),
            pltpu.VMEM((blocks, tiles, lanes), F32),
            pltpu.VMEM((blocks, lanes), F32),
        ),
        in_specs=[
            pl.BlockSpec((1, queries), lambda i: (0, 0)),
            pl.BlockSpec((per, feature, queries), lambda i: (i, 0, 0)),
            pl.BlockSpec((feature, keys), lambda i: (0, 0)),
        ],
        out_specs=(vmem_spec,) * 3,
        scratch_shapes=[pltpu.VMEM((keys, depth), BF16), pltpu.VMEM((depth, lanes), BF16)],
        compiler_params=pltpu.CompilerParams(vmem_limit_bytes=16 * MIB),
        name="main_scores",
    )(in_hbm(pos), in_hbm(query_t), in_hbm(keys_t))


def joined(stats):
    best = stats[0]
    for stat in stats[1:]:
        best = jnp.maximum(best, stat)
    return best + jnp.log2(sum(jnp.exp2(stat - best) for stat in stats))


def head_sum(probs, tops, stat, queries, row_local):
    blocks, keys, lanes = probs.shape
    tiles = tops.shape[1]
    tile = keys // tiles
    per = lanes // queries
    chips = queries // row_local // 2

    def body(prob_ref, top_ref, stat_ref, keep_ref, send_ref, summed):
        whole = stat_ref[...]
        factors = [jnp.exp2(top_ref[b] - whole[b : b + 1, :]) * (1.0 / H) for b in range(blocks)]
        for t in range(tiles):
            span = slice(t * tile, (t + 1) * tile)
            total = None
            for b in range(blocks):
                part = prob_ref[b, span, :].astype(F32) * factors[b][t : t + 1, :]
                for i in range(per):
                    piece = part[:, i * queries : (i + 1) * queries]
                    total = piece if total is None else total + piece
            summed[:, span] = total.T
        chip, core = head_place()
        for r in range(chips):
            first = (chip ^ r) * 2
            keep_ref[r] = rows_of(summed, (first + core) * row_local, row_local)
            send_ref[r] = rows_of(summed, (first + 1 - core) * row_local, row_local)

    half = pltpu.VMEM((chips, row_local, keys), F32)
    return vmem_call(
        body, "head_sum", (half, half), (probs, tops, stat), [pltpu.VMEM((queries, keys), F32)], cost=10**9
    )


def add_stacks(left, right):
    count = left.shape[0]

    def body(left_ref, right_ref, *outs):
        for r in range(count):
            outs[r][...] = left_ref[r] + right_ref[r]

    return vmem_call(
        body, "add_stacks", tuple(pltpu.VMEM(left.shape[1:], F32) for _ in range(count)), (left, right)
    )


def add_all(parts):
    def body(*refs):
        total = refs[0][...]
        for ref in refs[1:-1]:
            total = total + ref[...]
        refs[-1][...] = total

    return vmem_call(body, "add_all", pltpu.VMEM(parts[0].shape, F32), parts)


def stack_all(parts):
    def body(*refs):
        for r, ref in enumerate(refs[:-1]):
            refs[-1][r] = ref[...]

    return vmem_call(body, "stack_all", pltpu.VMEM((len(parts), *parts[0].shape), F32), parts)


def join_first(left, right, below):
    blocks, lanes = left.shape
    rows = below.shape[0]

    def body(left_ref, right_ref, below_ref, out_ref):
        out_ref[:blocks, :] = joined([left_ref[...], right_ref[...]])
        out_ref[blocks:, :] = jnp.concatenate([below_ref[...]] * (lanes // 128), axis=1)

    return vmem_call(body, "join_first", pltpu.VMEM((blocks + rows, lanes), F32), (left, right, below))


def join_more(left, right, blocks):
    count, lanes = left.shape

    def body(left_ref, right_ref, main_ref, index_ref):
        both = joined([left_ref[...], right_ref[...]])
        main_ref[...] = both[:blocks, :]
        index_ref[...] = both[blocks:, :128]

    outs = (pltpu.VMEM((blocks, lanes), F32), pltpu.VMEM((count - blocks, 128), F32))
    return vmem_call(body, "join_more", outs, (left, right))


def join_pair(left, right):
    def body(left_ref, right_ref, out_ref):
        out_ref[...] = joined([left_ref[...], right_ref[...]])

    return vmem_call(body, "join_pair", pltpu.VMEM(left.shape, F32), (left, right))


def deltas(scores, index_stats, targets, kl, groups):
    rows, keys = scores.shape
    own = rows // groups

    def body(score_ref, kl_ref, lse_ref, other_ref, *refs):
        target_refs, out_ref = refs[:-1], refs[-1]
        whole = joined([lse_ref[:, :1], other_ref[:, :1]])
        target = target_refs[0][...]
        for ref in target_refs[1:]:
            target = target + ref[...]
        delta = kl_ref[:, :1] * (jnp.exp2(score_ref[...] - whole) - target)
        for g in range(groups):
            out_ref[g] = delta[g * own : (g + 1) * own, :]

    return vmem_call(body, "deltas", pltpu.VMEM((groups, own, keys), F32), (scores, kl, *index_stats, *targets))


def query_part(r, delta, gate, index_keys):
    groups, own, keys = delta.shape
    size = gate.shape[1]
    heads = size // own
    width = index_keys.shape[1]

    def body(delta_ref, gate_ref, keys_ref, slope_ref, out_ref):
        group = lax.axis_index("keys") ^ r
        delta_rows = delta_ref[group]
        for row in range(own):
            line = jnp.broadcast_to(delta_rows[row : row + 1, :], (heads, keys)).astype(BF16)
            part = slice(row * heads, (row + 1) * heads)
            slope_ref[part, :] = jnp.where(gate_ref[group, part, :] > 0, line, jnp.zeros((), BF16))
        out_ref[...] = jnp.dot(slope_ref[...], keys_ref[...], preferred_element_type=F32)

    outs = (pltpu.VMEM((size, keys), BF16), pltpu.VMEM((size, width), F32))
    return vmem_call(body, "query_part", outs, (delta, gate, index_keys), cost=SHORT)


def key_part(slopes, wiq, head_devices):
    groups, width = wiq.shape[:2]
    keys = slopes[0].shape[1]
    chips = head_devices // 2
    chunk = keys // head_devices

    def body(wiq_ref, *refs):
        slope_refs, (keep_ref, send_ref) = refs[:groups], refs[groups:]
        z = lax.axis_index("keys")
        chip, core = head_place()
        for out_ref, side in ((send_ref, 1 - core), (keep_ref, core)):
            for n in range(chips):
                span = pl.ds(pl.multiple_of(((chip ^ n) * 2 + side) * chunk, chunk), chunk)
                summed = None
                for r in range(groups):
                    part = jnp.dot(wiq_ref[z ^ r], slope_refs[r][:, span], preferred_element_type=F32)
                    summed = part if summed is None else summed + part
                out_ref[n] = summed.T

    half = pltpu.VMEM((chips, chunk, width), F32)
    return vmem_call(body, "key_part", (half, half), (wiq, *slopes), cost=SHORT)


def own_rows(parts, index_query, index_weight):
    rows, heads, width = index_query.shape
    size = parts[0].shape[0]
    own = size // heads
    extra = -(-own // 8) * 8

    def body(query_ref, weight_ref, *refs):
        first = lax.axis_index("keys") * own
        part_refs, out_ref = refs[:-1], refs[-1]
        columns = weight_ref[...].T
        lane = lax.broadcasted_iota(jnp.int32, (heads, rows), 1)
        for i in range(own):
            span = slice(i * heads, (i + 1) * heads)
            total = part_refs[0][span, :]
            for ref in part_refs[1:]:
                total = total + ref[span, :]
            column = jnp.sum(jnp.where(lane == first + i, columns, 0.0), axis=1, keepdims=True)
            out_ref[span, :] = total * column
            summed = jnp.sum(total * query_ref[first + i].astype(F32), axis=1, keepdims=True)
            line = summed.T
            out_ref[size + i : size + i + 1, :] = jnp.concatenate(
                [line, jnp.zeros((1, width - heads), F32)], axis=1
            )
        if extra > own:
            out_ref[size + own :, :] = jnp.zeros((extra - own, width), F32)

    return vmem_call(
        body, "own_rows", pltpu.VMEM((size + extra, width), F32), (index_query, index_weight, *parts), cost=LONG
    )


def place_query(pieces, rows, heads):
    own = rows // len(pieces)
    size = own * heads
    width = pieces[0].shape[1]

    def body(*refs):
        piece_refs, (query_out, weight_out, sems) = refs[: len(pieces)], refs[len(pieces) :]
        z = lax.axis_index("keys")
        copies = []
        for r, ref in enumerate(piece_refs):
            at = pl.multiple_of((z ^ r) * size, size)
            copies.append(pltpu.make_async_copy(ref.at[:size], query_out.at[pl.ds(at, size)], sems.at[r]))
            copies[-1].start()
        for r, ref in enumerate(piece_refs):
            weight_out[pl.ds((z ^ r) * own, own), :] = ref[size : size + own, :heads]
        for copy in copies:
            copy.wait()

    query, weight = vmem_call(
        body,
        "place_query",
        (jax.ShapeDtypeStruct((rows * heads, width), F32), jax.ShapeDtypeStruct((rows, heads), F32)),
        pieces,
        [pltpu.SemaphoreType.DMA((len(pieces),))],
        out_specs=(any_spec, vmem_spec),
        cost=LONG,
    )
    return query.reshape(rows, heads, width), weight


def place_keys(mine, other):
    chips, chunk, width = mine.shape

    def body(mine_ref, other_ref, out_ref, sems):
        chip, core = head_place()
        copies = []
        for n, (ref, side) in enumerate(((mine_ref, core), (other_ref, 1 - core))):
            for r in range(chips):
                at = pl.multiple_of(((chip ^ r) * 2 + side) * chunk, chunk)
                copies.append(pltpu.make_async_copy(ref.at[r], out_ref.at[pl.ds(at, chunk)], sems.at[n, r]))
                copies[-1].start()
        for copy in copies:
            copy.wait()

    return vmem_call(
        body,
        "place_keys",
        jax.ShapeDtypeStruct((2 * chips * chunk, width), F32),
        (mine, other),
        [pltpu.SemaphoreType.DMA((2, chips))],
        out_specs=any_spec,
    )


def shards(main_query, latent_keys, index_query, index_keys, index_weight, query_pos, kl_weight):
    queries = main_query.shape[0]
    row_local, index_heads, _ = index_query.shape
    head_devices = lax.axis_size("heads")
    key_devices = lax.axis_size("keys")
    chips = head_devices // 2

    def to_keys(value, bits):
        return lax.ppermute(value, "keys", [(i, i ^ bits) for i in range(key_devices)])

    def to_heads(value, bits):
        return lax.ppermute(value, "heads", [(i, i ^ bits) for i in range(head_devices)])

    far_first = list(reversed(range(1, key_devices)))
    chips_far_first = list(reversed(range(1, chips)))

    probs, tops, stat = main_scores(query_pos[None, :], main_query.transpose(1, 2, 0), latent_keys.T)
    scores, index_lse, kl, wiq, gate = index_forward(
        query_pos, kl_weight, index_query, index_keys, index_weight, key_devices, stat
    )
    blocks = stat.shape[0]
    both = join_first(stat, to_keys(stat, 1), index_lse)
    bits = 2
    while bits < key_devices // 2:
        both = join_pair(both, to_keys(both, bits))
        bits *= 2
    stat, index_lse = join_more(both, to_keys(both, bits), blocks)
    keep, send = head_sum(probs, tops, stat, queries, row_local)
    index_lse, send = lax.optimization_barrier((index_lse, send))
    sums = add_stacks(keep, to_heads(send, 1))
    targets = [sums[0]] + [to_heads(sums[r], 2 * r) for r in chips_far_first]
    delta = deltas(scores, (index_lse, to_keys(index_lse, 1)), targets, kl, key_devices)

    slopes, arrived = {}, []
    for r in far_first + [0]:
        slopes[r], part = query_part(r, delta, gate, index_keys)
        arrived.append(to_keys(part, r) if r else part)
    keep, send = key_part([slopes[r] for r in range(key_devices)], wiq, head_devices)
    sums = add_stacks(keep, to_heads(send, 1))
    query_own = own_rows(arrived, index_query, index_weight)
    key_parts = [sums[0]] + [to_heads(sums[r], 2 * r) for r in chips_far_first]
    query_own, key_parts[0] = lax.optimization_barrier((query_own, key_parts[0]))
    key_own = add_all(key_parts)
    pieces = [query_own] + [to_keys(query_own, r) for r in range(1, key_devices)]
    mine, bits = [key_own], 2
    while bits < head_devices:
        mine = mine + [to_heads(piece, bits) for piece in mine]
        bits *= 2
    mine = stack_all(mine)
    key_grad = place_keys(mine, to_heads(mine, 1))
    query_grad, weight_grad = place_query(pieces, row_local, index_heads)
    return query_grad, key_grad, weight_grad


def solution(mesh):
    placed = (
        P(None, "heads", None),
        P("keys", None),
        P("heads", None, None),
        P("keys", None),
        P("heads", None),
        P(),
        P("heads"),
    )
    return jax.shard_map(
        shards,
        mesh=mesh,
        in_specs=placed,
        out_specs=(P("heads", None, None), P("keys", None), P("heads", None)),
        check_vma=False,
    )
```

```python
import math

import jax
import jax.numpy as jnp
from jax import lax
from jax.experimental import pallas as pl
from jax.experimental.pallas import tpu as pltpu
from jax.sharding import PartitionSpec as P

H = 128

LOG2E = math.log2(math.e)
score_scale = 192.0 ** (-0.5) * LOG2E
masked_fill = -1e30

F32 = jnp.float32
BF16 = jnp.bfloat16
MIB = 1024 * 1024
SHORT = 0
LONG = 4 * 10**10

vmem_spec = pl.BlockSpec(memory_space=pltpu.VMEM)
smem_spec = pl.BlockSpec(memory_space=pltpu.SMEM)
any_spec = pl.BlockSpec(memory_space=pl.ANY)


def in_vmem(array):
    return pltpu.with_memory_space_constraint(array, pltpu.VMEM)


def in_hbm(array):
    return pltpu.with_memory_space_constraint(array, pltpu.HBM)


def vmem_call(
    body, name, outs, operands, scratch=(), out_specs=None, scalars=(), limit=12 * MIB, cost=0
):
    several = isinstance(outs, (tuple, list))
    if out_specs is None:
        out_specs = tuple(vmem_spec for _ in outs) if several else vmem_spec
    return pl.pallas_call(
        body,
        out_shape=outs,
        in_specs=[smem_spec] * len(scalars) + [vmem_spec] * len(operands),
        out_specs=out_specs,
        scratch_shapes=list(scratch),
        compiler_params=pltpu.CompilerParams(vmem_limit_bytes=limit),
        cost_estimate=pl.CostEstimate(flops=cost, bytes_accessed=0, transcendentals=0),
        name=name,
    )(*scalars, *[in_vmem(a) for a in operands])


def tile_of(extent, wanted):
    return wanted if extent % wanted == 0 else extent


def rows_of(ref, first, count):
    return ref[pl.ds(pl.multiple_of(first, count), count)]


def head_place():
    at = lax.axis_index("heads")
    return at // 2, at % 2


def index_forward(query_pos, kl, index_query, index_keys, index_weight, groups, after):
    rows, heads, width = index_query.shape
    keys = index_keys.shape[0]
    tile = tile_of(keys, 256)
    own = rows // groups

    def body(pos_ref, kl_ref, query_ref, keys_ref, weight_ref, _, score_ref, lse_ref, kl_out, wiq_ref, gate_ref):
        columns = weight_ref[...].T
        flat = query_ref[...].reshape(rows * heads, width)
        for row in range(rows):
            kl_out[row : row + 1, :] = jnp.full((1, 128), kl_ref[row], F32)
            piece = query_ref[row].astype(F32) * columns[:, row : row + 1]
            wiq_ref[row // own, :, (row % own) * heads : (row % own + 1) * heads] = piece.T.astype(BF16)
        first_key = lax.axis_index("keys") * keys
        first_row = lax.axis_index("heads") * rows
        for at in range(0, keys, tile):
            logits = lax.dot_general(
                flat, keys_ref[at : at + tile, :], (((1,), (1,)), ((), ())), preferred_element_type=F32
            )
            for g in range(groups):
                gate_ref[g, :, at : at + tile] = logits[g * own * heads : (g + 1) * own * heads, :].astype(BF16)
            index = first_key + at + lax.broadcasted_iota(jnp.int32, (1, tile), 1)
            for row in range(rows):
                active = jnp.maximum(logits[row * heads : (row + 1) * heads, :], 0.0)
                summed = jnp.sum(active * columns[:, row : row + 1], axis=0, keepdims=True)
                seen = index <= pos_ref[first_row + row]
                score_ref[row : row + 1, at : at + tile] = jnp.where(seen, summed * LOG2E, masked_fill)
        scores = score_ref[...]
        top = jnp.max(scores, axis=1, keepdims=True)
        total = jnp.sum(jnp.exp2(scores - top), axis=1, keepdims=True)
        lse_ref[...] = jnp.broadcast_to(top + jnp.log2(total), lse_ref.shape)

    return pl.pallas_call(
        body,
        out_shape=(
            pltpu.VMEM((rows, keys), F32),
            pltpu.VMEM((rows, 128), F32),
            pltpu.VMEM((rows, 128), F32),
            pltpu.VMEM((groups, width, own * heads), BF16),
            pltpu.VMEM((groups, own * heads, keys), BF16),
        ),
        in_specs=[smem_spec] * 2 + [vmem_spec] * 4,
        out_specs=(vmem_spec,) * 5,
        compiler_params=pltpu.CompilerParams(vmem_limit_bytes=16 * MIB),
        cost_estimate=pl.CostEstimate(flops=0, bytes_accessed=0, transcendentals=0),
        name="index_forward",
    )(query_pos, kl, *[in_vmem(a) for a in (index_query, index_keys, index_weight, after)])


def main_scores(pos, query_t, keys_t):
    head_local, feature, queries = query_t.shape
    keys = keys_t.shape[1]
    per = 256 // queries if queries < 256 and head_local % (256 // queries) == 0 else 1
    lanes = per * queries
    blocks = head_local // per
    many = 2 if blocks % 2 == 0 else 1
    tile = tile_of(keys, 128)
    tiles = keys // tile
    mask_at = -(-feature // 128) * 128
    depth = mask_at + -(-queries // 128) * 128

    def body(pos_ref, query_ref, keys_ref, prob_ref, top_ref, stat_ref, key_rows, weights):
        step = pl.program_id(0)

        @pl.when(step == 0)
        def _():
            chunk = tile_of(keys, 512)
            for at in range(0, keys, chunk):
                key_rows[at : at + chunk, :feature] = keys_ref[:, at : at + chunk].T
            if mask_at > feature:
                key_rows[:, feature:mask_at] = jnp.zeros((keys, mask_at - feature), BF16)
                weights[:, feature:mask_at, :] = jnp.zeros((many, mask_at - feature, lanes), BF16)
            index = lax.axis_index("keys") * keys + lax.broadcasted_iota(jnp.int32, (keys, queries), 0)
            hidden = jnp.where(index <= pos_ref[...], 0.0, masked_fill).astype(BF16)
            key_rows[:, mask_at : mask_at + queries] = hidden
            at_row = lax.broadcasted_iota(jnp.int32, (depth - mask_at, lanes), 0)
            at_lane = lax.broadcasted_iota(jnp.int32, (depth - mask_at, lanes), 1)
            for k in range(many):
                weights[k, mask_at:, :] = jnp.where(at_row == at_lane % queries, 1.0, 0.0).astype(BF16)
            if depth > mask_at + queries:
                key_rows[:, mask_at + queries :] = jnp.zeros((keys, depth - mask_at - queries), BF16)

        for k in range(many):
            for i in range(per):
                weights[k, :feature, i * queries : (i + 1) * queries] = query_ref[k * per + i]
        for k in range(many):
            block = step * many + k
            tops, totals = [], []
            for t in range(tiles):
                span = slice(t * tile, (t + 1) * tile)
                scores = jnp.dot(key_rows[span, :], weights[k], preferred_element_type=F32)
                top = jnp.max(scores, axis=0, keepdims=True)
                prob = jnp.exp2((scores - top) * score_scale)
                top = top * score_scale
                tops.append(top)
                totals.append(jnp.sum(prob, axis=0, keepdims=True))
                prob_ref[block, span, :] = prob.astype(prob_ref.dtype)
                top_ref[block, t : t + 1, :] = top
            best = tops[0]
            for top in tops[1:]:
                best = jnp.maximum(best, top)
            total = sum(s * jnp.exp2(top - best) for s, top in zip(totals, tops))
            stat_ref[pl.ds(block, 1), :] = best + jnp.log2(total)

    return pl.pallas_call(
        body,
        grid=(blocks // many,),
        out_shape=(
            pltpu.VMEM((blocks, keys, lanes), F32),
            pltpu.VMEM((blocks, tiles, lanes), F32),
            pltpu.VMEM((blocks, lanes), F32),
        ),
        in_specs=[
            pl.BlockSpec((1, queries), lambda i: (0, 0)),
            pl.BlockSpec((many * per, feature, queries), lambda i: (i, 0, 0)),
            pl.BlockSpec((feature, keys), lambda i: (0, 0)),
        ],
        out_specs=(vmem_spec,) * 3,
        scratch_shapes=[pltpu.VMEM((keys, depth), BF16), pltpu.VMEM((many, depth, lanes), BF16)],
        compiler_params=pltpu.CompilerParams(vmem_limit_bytes=16 * MIB),
        name="main_scores",
    )(in_hbm(pos), in_hbm(query_t), in_hbm(keys_t))


def joined(stats):
    best = stats[0]
    for stat in stats[1:]:
        best = jnp.maximum(best, stat)
    return best + jnp.log2(sum(jnp.exp2(stat - best) for stat in stats))


def head_sum(probs, tops, stat, queries, row_local):
    blocks, keys, lanes = probs.shape
    tiles = tops.shape[1]
    tile = keys // tiles
    per = lanes // queries
    chips = queries // row_local // 2

    def body(prob_ref, top_ref, stat_ref, keep_ref, send_ref, summed):
        whole = stat_ref[...]
        factors = [jnp.exp2(top_ref[b] - whole[b : b + 1, :]) * (1.0 / H) for b in range(blocks)]
        for t in range(tiles):
            span = slice(t * tile, (t + 1) * tile)
            total = None
            for b in range(blocks):
                part = prob_ref[b, span, :].astype(F32) * factors[b][t : t + 1, :]
                for i in range(per):
                    piece = part[:, i * queries : (i + 1) * queries]
                    total = piece if total is None else total + piece
            summed[:, span] = total.T
        chip, core = head_place()
        for r in range(chips):
            first = (chip ^ r) * 2
            keep_ref[r] = rows_of(summed, (first + core) * row_local, row_local)
            send_ref[r] = rows_of(summed, (first + 1 - core) * row_local, row_local)

    half = pltpu.VMEM((chips, row_local, keys), F32)
    return vmem_call(
        body, "head_sum", (half, half), (probs, tops, stat), [pltpu.VMEM((queries, keys), F32)], cost=10**9
    )


def add_stacks(left, right):
    count = left.shape[0]

    def body(left_ref, right_ref, *outs):
        for r in range(count):
            outs[r][...] = left_ref[r] + right_ref[r]

    return vmem_call(
        body, "add_stacks", tuple(pltpu.VMEM(left.shape[1:], F32) for _ in range(count)), (left, right)
    )


def add_all(parts):
    def body(*refs):
        total = refs[0][...]
        for ref in refs[1:-1]:
            total = total + ref[...]
        refs[-1][...] = total

    return vmem_call(body, "add_all", pltpu.VMEM(parts[0].shape, F32), parts)


def stack_all(parts):
    def body(*refs):
        for r, ref in enumerate(refs[:-1]):
            refs[-1][r] = ref[...]

    return vmem_call(body, "stack_all", pltpu.VMEM((len(parts), *parts[0].shape), F32), parts)


def join_first(left, right, below):
    blocks, lanes = left.shape
    rows = below.shape[0]

    def body(left_ref, right_ref, below_ref, out_ref):
        out_ref[:blocks, :] = joined([left_ref[...], right_ref[...]])
        out_ref[blocks:, :] = jnp.concatenate([below_ref[...]] * (lanes // 128), axis=1)

    return vmem_call(body, "join_first", pltpu.VMEM((blocks + rows, lanes), F32), (left, right, below))


def join_more(left, right, blocks):
    count, lanes = left.shape

    def body(left_ref, right_ref, main_ref, index_ref):
        both = joined([left_ref[...], right_ref[...]])
        main_ref[...] = both[:blocks, :]
        index_ref[...] = both[blocks:, :128]

    outs = (pltpu.VMEM((blocks, lanes), F32), pltpu.VMEM((count - blocks, 128), F32))
    return vmem_call(body, "join_more", outs, (left, right))


def join_pair(left, right):
    def body(left_ref, right_ref, out_ref):
        out_ref[...] = joined([left_ref[...], right_ref[...]])

    return vmem_call(body, "join_pair", pltpu.VMEM(left.shape, F32), (left, right))


def gradients(scores, index_stats, targets, kl, gate, index_keys, wiq, head_devices):
    rows, keys = scores.shape
    groups, size = gate.shape[:2]
    own = rows // groups
    heads = size // own
    width = index_keys.shape[1]
    chips = head_devices // 2
    chunk = keys // head_devices

    def body(score_ref, kl_ref, lse_ref, other_ref, gate_ref, keys_ref, wiq_ref, *refs):
        target_refs, refs = refs[: len(targets)], refs[len(targets) :]
        query_outs, (keep_ref, send_ref, delta_ref, slope_ref, wiq_rows) = refs[:groups], refs[groups:]
        whole = joined([lse_ref[:, :1], other_ref[:, :1]])
        target = target_refs[0][...]
        for ref in target_refs[1:]:
            target = target + ref[...]
        delta = kl_ref[:, :1] * (jnp.exp2(score_ref[...] - whole) - target)
        for g in range(groups):
            delta_ref[g] = delta[g * own : (g + 1) * own, :]
        z = lax.axis_index("keys")
        chip, core = head_place()
        for r in range(groups):
            lines = delta_ref[z ^ r]
            for i in range(own):
                line = jnp.broadcast_to(lines[i : i + 1, :], (heads, keys)).astype(BF16)
                signs = gate_ref[z ^ r, i * heads : (i + 1) * heads, :]
                at = r * size + i * heads
                slope_ref[at : at + heads, :] = jnp.where(signs > 0, line, jnp.zeros((), BF16))
            wiq_rows[:, r * size : (r + 1) * size] = wiq_ref[z ^ r]
        part = jnp.dot(slope_ref[...], keys_ref[...], preferred_element_type=F32)
        for r in range(groups):
            query_outs[r][:size, :] = part[r * size : (r + 1) * size, :]
            query_outs[r][size:, :] = jnp.zeros((8, width), F32)
        for out_ref, side in ((send_ref, 1 - core), (keep_ref, core)):
            for n in range(chips):
                span = pl.ds(pl.multiple_of(((chip ^ n) * 2 + side) * chunk, chunk), chunk)
                out_ref[n] = jnp.dot(wiq_rows[...], slope_ref[:, span], preferred_element_type=F32).T

    half = pltpu.VMEM((chips, chunk, width), F32)
    outs = tuple(pltpu.VMEM((size + 8, width), F32) for _ in range(groups)) + (half, half)
    scratch = [
        pltpu.VMEM((groups, own, keys), F32),
        pltpu.VMEM((rows * heads, keys), BF16),
        pltpu.VMEM((width, rows * heads), BF16),
    ]
    operands = (scores, kl, *index_stats, gate, index_keys, wiq, *targets)
    return vmem_call(body, "gradients", outs, operands, scratch, limit=16 * MIB, cost=SHORT)


def own_rows(parts, index_query, index_weight):
    rows, heads, width = index_query.shape
    size = parts[0].shape[0] - 8
    own = size // heads
    extra = -(-own // 8) * 8

    def body(query_ref, weight_ref, *refs):
        first = lax.axis_index("keys") * own
        part_refs, out_ref = refs[:-1], refs[-1]
        columns = weight_ref[...].T
        lane = lax.broadcasted_iota(jnp.int32, (heads, rows), 1)
        for i in range(own):
            span = slice(i * heads, (i + 1) * heads)
            total = part_refs[0][span, :]
            for ref in part_refs[1:]:
                total = total + ref[span, :]
            column = jnp.sum(jnp.where(lane == first + i, columns, 0.0), axis=1, keepdims=True)
            out_ref[span, :] = total * column
            summed = jnp.sum(total * query_ref[first + i].astype(F32), axis=1, keepdims=True)
            line = summed.T
            out_ref[size + i : size + i + 1, :] = jnp.concatenate(
                [line, jnp.zeros((1, width - heads), F32)], axis=1
            )
        if extra > own:
            out_ref[size + own :, :] = jnp.zeros((extra - own, width), F32)

    return vmem_call(
        body, "own_rows", pltpu.VMEM((size + extra, width), F32), (index_query, index_weight, *parts), cost=LONG
    )


def place_query(pieces, rows, heads):
    own = rows // len(pieces)
    size = own * heads
    width = pieces[0].shape[1]

    def body(*refs):
        piece_refs, (query_out, weight_out, weights, sems) = refs[: len(pieces)], refs[len(pieces) :]
        z = lax.axis_index("keys")
        copies = []
        for r, ref in enumerate(piece_refs):
            at = pl.multiple_of((z ^ r) * size, size)
            copies.append(pltpu.make_async_copy(ref.at[:size], query_out.at[pl.ds(at, size)], sems.at[r]))
            copies[-1].start()
        for r, ref in enumerate(piece_refs):
            weights[pl.ds((z ^ r) * own, own), :] = ref[size : size + own, :heads]
        copies.append(pltpu.make_async_copy(weights, weight_out, sems.at[len(pieces)]))
        copies[-1].start()
        for copy in copies:
            copy.wait()

    query, weight = vmem_call(
        body,
        "place_query",
        (jax.ShapeDtypeStruct((rows * heads, width), F32), jax.ShapeDtypeStruct((rows, heads), F32)),
        pieces,
        [pltpu.VMEM((rows, heads), F32), pltpu.SemaphoreType.DMA((len(pieces) + 1,))],
        out_specs=(any_spec, any_spec),
        cost=LONG,
    )
    return query.reshape(rows, heads, width), weight


def place_keys(mine, other):
    chips, chunk, width = mine.shape

    def body(mine_ref, other_ref, out_ref, sems):
        chip, core = head_place()
        copies = []
        for n, (ref, side) in enumerate(((mine_ref, core), (other_ref, 1 - core))):
            for r in range(chips):
                at = pl.multiple_of(((chip ^ r) * 2 + side) * chunk, chunk)
                copies.append(pltpu.make_async_copy(ref.at[r], out_ref.at[pl.ds(at, chunk)], sems.at[n, r]))
                copies[-1].start()
        for copy in copies:
            copy.wait()

    return vmem_call(
        body,
        "place_keys",
        jax.ShapeDtypeStruct((2 * chips * chunk, width), F32),
        (mine, other),
        [pltpu.SemaphoreType.DMA((2, chips))],
        out_specs=any_spec,
    )


def shards(main_query, latent_keys, index_query, index_keys, index_weight, query_pos, kl_weight):
    queries = main_query.shape[0]
    row_local, index_heads, _ = index_query.shape
    head_devices = lax.axis_size("heads")
    key_devices = lax.axis_size("keys")
    chips = head_devices // 2

    def to_keys(value, bits):
        return lax.ppermute(value, "keys", [(i, i ^ bits) for i in range(key_devices)])

    def to_heads(value, bits):
        return lax.ppermute(value, "heads", [(i, i ^ bits) for i in range(head_devices)])

    far_first = list(reversed(range(1, key_devices)))
    chips_far_first = list(reversed(range(1, chips)))

    probs, tops, stat = main_scores(query_pos[None, :], main_query.transpose(1, 2, 0), latent_keys.T)
    scores, index_lse, kl, wiq, gate = index_forward(
        query_pos, kl_weight, index_query, index_keys, index_weight, key_devices, stat
    )
    blocks = stat.shape[0]
    both = join_first(stat, to_keys(stat, 1), index_lse)
    bits = 2
    while bits < key_devices // 2:
        both = join_pair(both, to_keys(both, bits))
        bits *= 2
    stat, index_lse = join_more(both, to_keys(both, bits), blocks)
    keep, send = head_sum(probs, tops, stat, queries, row_local)
    index_lse, send = lax.optimization_barrier((index_lse, send))
    sums = add_stacks(keep, to_heads(send, 1))
    targets = [sums[0]] + [to_heads(sums[r], 2 * r) for r in chips_far_first]
    index_stats = (index_lse, to_keys(index_lse, 1))
    *parts, keep, send = gradients(
        scores, index_stats, targets, kl, gate, index_keys, wiq, head_devices
    )
    arrived = [to_keys(parts[r], r) for r in far_first] + [parts[0]]
    query_own = own_rows(arrived, index_query, index_weight)
    sums = add_stacks(keep, to_heads(send, 1))
    key_parts = [sums[0]] + [to_heads(sums[r], 2 * r) for r in chips_far_first]
    query_own, key_parts[0] = lax.optimization_barrier((query_own, key_parts[0]))
    key_own = add_all(key_parts)
    pieces = [query_own] + [to_keys(query_own, r) for r in range(1, key_devices)]
    mine, bits = [key_own], 2
    while bits < head_devices:
        mine = mine + [to_heads(piece, bits) for piece in mine]
        bits *= 2
    mine = stack_all(mine)
    key_grad = place_keys(mine, to_heads(mine, 1))
    query_grad, weight_grad = place_query(pieces, row_local, index_heads)
    return query_grad, key_grad, weight_grad


def solution(mesh):
    placed = (
        P(None, "heads", None),
        P("keys", None),
        P("heads", None, None),
        P("keys", None),
        P("heads", None),
        P(),
        P("heads"),
    )
    return jax.shard_map(
        shards,
        mesh=mesh,
        in_specs=placed,
        out_specs=(P("heads", None, None), P("keys", None), P("heads", None)),
        check_vma=False,
    )
```

```python
import math

import jax
import jax.numpy as jnp
from jax import lax
from jax.experimental import pallas as pl
from jax.experimental.pallas import tpu as pltpu
from jax.sharding import PartitionSpec as P

H = 128

LOG2E = math.log2(math.e)
score_scale = 192.0 ** (-0.5) * LOG2E
masked_fill = -1e30

F32 = jnp.float32
BF16 = jnp.bfloat16
MIB = 1024 * 1024
SHORT = 0
LONG = 4 * 10**10

vmem_spec = pl.BlockSpec(memory_space=pltpu.VMEM)
smem_spec = pl.BlockSpec(memory_space=pltpu.SMEM)
any_spec = pl.BlockSpec(memory_space=pl.ANY)


def in_vmem(array):
    return pltpu.with_memory_space_constraint(array, pltpu.VMEM)


def in_hbm(array):
    return pltpu.with_memory_space_constraint(array, pltpu.HBM)


def vmem_call(
    body, name, outs, operands, scratch=(), out_specs=None, scalars=(), limit=12 * MIB, cost=0
):
    several = isinstance(outs, (tuple, list))
    if out_specs is None:
        out_specs = tuple(vmem_spec for _ in outs) if several else vmem_spec
    return pl.pallas_call(
        body,
        out_shape=outs,
        in_specs=[smem_spec] * len(scalars) + [vmem_spec] * len(operands),
        out_specs=out_specs,
        scratch_shapes=list(scratch),
        compiler_params=pltpu.CompilerParams(vmem_limit_bytes=limit),
        cost_estimate=pl.CostEstimate(flops=cost, bytes_accessed=0, transcendentals=0),
        name=name,
    )(*scalars, *[in_vmem(a) for a in operands])


def tile_of(extent, wanted):
    return wanted if extent % wanted == 0 else extent


def rows_of(ref, first, count):
    return ref[pl.ds(pl.multiple_of(first, count), count)]


def head_place():
    at = lax.axis_index("heads")
    return at // 2, at % 2


def weighted_columns(query_ref, columns, rows, heads):
    for row in range(rows):
        piece = query_ref[row * heads : (row + 1) * heads, :].astype(F32) * columns[:, row : row + 1]
        yield row, piece.T.astype(BF16)


def index_forward(query_pos, index_query, index_keys, index_weight, after):
    rows, heads, width = index_query.shape
    keys = index_keys.shape[0]
    tile = tile_of(keys, 256)

    def body(pos_ref, query_ref, keys_ref, weight_ref, _, score_ref, lse_ref, pack_ref):
        columns = weight_ref[...].T
        flat = query_ref[...].reshape(rows * heads, width)
        pack_ref[: rows * heads, :] = flat.astype(F32)
        pack_ref[rows * heads :, :] = jnp.concatenate(
            [weight_ref[...], jnp.zeros((rows, width - heads), F32)], axis=1
        )
        first_key = lax.axis_index("keys") * keys
        first_row = lax.axis_index("heads") * rows
        for at in range(0, keys, tile):
            logits = lax.dot_general(
                flat, keys_ref[at : at + tile, :], (((1,), (1,)), ((), ())), preferred_element_type=F32
            )
            index = first_key + at + lax.broadcasted_iota(jnp.int32, (1, tile), 1)
            for row in range(rows):
                active = jnp.maximum(logits[row * heads : (row + 1) * heads, :], 0.0)
                summed = jnp.sum(active * columns[:, row : row + 1], axis=0, keepdims=True)
                seen = index <= pos_ref[first_row + row]
                score_ref[row : row + 1, at : at + tile] = jnp.where(seen, summed * LOG2E, masked_fill)
        scores = score_ref[...]
        top = jnp.max(scores, axis=1, keepdims=True)
        total = jnp.sum(jnp.exp2(scores - top), axis=1, keepdims=True)
        lse_ref[...] = jnp.broadcast_to(top + jnp.log2(total), lse_ref.shape)

    outs = (
        pltpu.VMEM((rows, keys), F32),
        pltpu.VMEM((rows, 128), F32),
        pltpu.VMEM((rows * heads + rows, width), F32),
    )
    operands = (index_query, index_keys, index_weight, after)
    return vmem_call(body, "index_forward", outs, operands, scalars=(query_pos,), limit=16 * MIB)


def index_signs(kl, index_query, index_keys, index_weight, groups):
    rows, heads, width = index_query.shape
    keys = index_keys.shape[0]
    tile = tile_of(keys, 256)
    own = rows // groups
    size = own * heads

    def body(kl_ref, query_ref, keys_ref, weight_ref, gate_ref, wiq_ref, kl_out):
        for row in range(rows):
            kl_out[row : row + 1, :] = jnp.full((1, 128), kl_ref[row], F32)
        flat = query_ref[...].reshape(rows * heads, width)
        for row, piece in weighted_columns(flat, weight_ref[...].T, rows, heads):
            wiq_ref[row // own, :, (row % own) * heads : (row % own + 1) * heads] = piece
        for at in range(0, keys, tile):
            logits = lax.dot_general(
                flat, keys_ref[at : at + tile, :], (((1,), (1,)), ((), ())), preferred_element_type=F32
            )
            for g in range(groups):
                gate_ref[g, :, at : at + tile] = logits[g * size : (g + 1) * size, :].astype(BF16)

    outs = (
        pltpu.VMEM((groups, size, keys), BF16),
        pltpu.VMEM((groups, width, size), BF16),
        pltpu.VMEM((rows, 128), F32),
    )
    operands = (index_query, index_keys, index_weight)
    return vmem_call(body, "index_signs", outs, operands, scalars=(kl,), limit=16 * MIB)


def other_signs(pack, index_keys, rows):
    keys, width = index_keys.shape
    heads = pack.shape[0] // rows - 1
    half = keys // 2
    tile = tile_of(half, 256)

    def body(pack_ref, keys_ref, gate_ref, wiq_ref):
        flat = pack_ref[: rows * heads, :].astype(BF16)
        columns = pack_ref[rows * heads :, :].T[:heads, :]
        for row, piece in weighted_columns(flat, columns, rows, heads):
            wiq_ref[:, row * heads : (row + 1) * heads] = piece
        _, core = head_place()
        for at in range(0, half, tile):
            span = pl.ds(pl.multiple_of(core * half + at, tile), tile)
            gate_ref[:, at : at + tile] = lax.dot_general(
                flat, keys_ref[span, :], (((1,), (1,)), ((), ())), preferred_element_type=F32
            ).astype(BF16)

    outs = (pltpu.VMEM((rows * heads, half), BF16), pltpu.VMEM((width, rows * heads), BF16))
    return vmem_call(body, "other_signs", outs, (pack, index_keys), limit=16 * MIB)


def main_scores(pos, query_t, keys_t):
    head_local, feature, queries = query_t.shape
    keys = keys_t.shape[1]
    per = 256 // queries if queries < 256 and head_local % (256 // queries) == 0 else 1
    lanes = per * queries
    blocks = head_local // per
    many = 2 if blocks % 2 == 0 else 1
    tile = tile_of(keys, 128)
    tiles = keys // tile
    mask_at = -(-feature // 128) * 128
    depth = mask_at + -(-queries // 128) * 128

    def body(pos_ref, query_ref, keys_ref, prob_ref, top_ref, stat_ref, key_rows, weights):
        step = pl.program_id(0)

        @pl.when(step == 0)
        def _():
            chunk = tile_of(keys, 512)
            for at in range(0, keys, chunk):
                key_rows[at : at + chunk, :feature] = keys_ref[:, at : at + chunk].T
            if mask_at > feature:
                key_rows[:, feature:mask_at] = jnp.zeros((keys, mask_at - feature), BF16)
                weights[:, feature:mask_at, :] = jnp.zeros((many, mask_at - feature, lanes), BF16)
            index = lax.axis_index("keys") * keys + lax.broadcasted_iota(jnp.int32, (keys, queries), 0)
            hidden = jnp.where(index <= pos_ref[...], 0.0, masked_fill).astype(BF16)
            key_rows[:, mask_at : mask_at + queries] = hidden
            at_row = lax.broadcasted_iota(jnp.int32, (depth - mask_at, lanes), 0)
            at_lane = lax.broadcasted_iota(jnp.int32, (depth - mask_at, lanes), 1)
            for k in range(many):
                weights[k, mask_at:, :] = jnp.where(at_row == at_lane % queries, 1.0, 0.0).astype(BF16)
            if depth > mask_at + queries:
                key_rows[:, mask_at + queries :] = jnp.zeros((keys, depth - mask_at - queries), BF16)

        for k in range(many):
            for i in range(per):
                weights[k, :feature, i * queries : (i + 1) * queries] = query_ref[k * per + i]
        for k in range(many):
            block = step * many + k
            tops, totals = [], []
            for t in range(tiles):
                span = slice(t * tile, (t + 1) * tile)
                scores = jnp.dot(key_rows[span, :], weights[k], preferred_element_type=F32)
                top = jnp.max(scores, axis=0, keepdims=True)
                prob = jnp.exp2((scores - top) * score_scale)
                top = top * score_scale
                tops.append(top)
                totals.append(jnp.sum(prob, axis=0, keepdims=True))
                prob_ref[block, span, :] = prob.astype(prob_ref.dtype)
                top_ref[block, t : t + 1, :] = top
            best = tops[0]
            for top in tops[1:]:
                best = jnp.maximum(best, top)
            total = sum(s * jnp.exp2(top - best) for s, top in zip(totals, tops))
            stat_ref[pl.ds(block, 1), :] = best + jnp.log2(total)

    return pl.pallas_call(
        body,
        grid=(blocks // many,),
        out_shape=(
            pltpu.VMEM((blocks, keys, lanes), F32),
            pltpu.VMEM((blocks, tiles, lanes), F32),
            pltpu.VMEM((blocks, lanes), F32),
        ),
        in_specs=[
            pl.BlockSpec((1, queries), lambda i: (0, 0)),
            pl.BlockSpec((many * per, feature, queries), lambda i: (i, 0, 0)),
            pl.BlockSpec((feature, keys), lambda i: (0, 0)),
        ],
        out_specs=(vmem_spec,) * 3,
        scratch_shapes=[pltpu.VMEM((keys, depth), BF16), pltpu.VMEM((many, depth, lanes), BF16)],
        compiler_params=pltpu.CompilerParams(vmem_limit_bytes=16 * MIB),
        name="main_scores",
    )(in_hbm(pos), in_hbm(query_t), in_hbm(keys_t))


def joined(stats):
    best = stats[0]
    for stat in stats[1:]:
        best = jnp.maximum(best, stat)
    return best + jnp.log2(sum(jnp.exp2(stat - best) for stat in stats))


def head_sum(probs, tops, stat, queries, row_local):
    blocks, keys, lanes = probs.shape
    tiles = tops.shape[1]
    tile = keys // tiles
    per = lanes // queries
    chips = queries // row_local // 2

    def body(prob_ref, top_ref, stat_ref, keep_ref, send_ref, summed):
        whole = stat_ref[...]
        factors = [jnp.exp2(top_ref[b] - whole[b : b + 1, :]) * (1.0 / H) for b in range(blocks)]
        for t in range(tiles):
            span = slice(t * tile, (t + 1) * tile)
            total = None
            for b in range(blocks):
                part = prob_ref[b, span, :].astype(F32) * factors[b][t : t + 1, :]
                for i in range(per):
                    piece = part[:, i * queries : (i + 1) * queries]
                    total = piece if total is None else total + piece
            summed[:, span] = total.T
        chip, core = head_place()
        for r in range(chips):
            first = (chip ^ r) * 2
            keep_ref[r] = rows_of(summed, (first + core) * row_local, row_local)
            send_ref[r] = rows_of(summed, (first + 1 - core) * row_local, row_local)

    half = pltpu.VMEM((chips, row_local, keys), F32)
    return vmem_call(
        body, "head_sum", (half, half), (probs, tops, stat), [pltpu.VMEM((queries, keys), F32)], cost=10**9
    )


def add_stacks(left, right):
    count = left.shape[0]

    def body(left_ref, right_ref, *outs):
        for r in range(count):
            outs[r][...] = left_ref[r] + right_ref[r]

    return vmem_call(
        body, "add_stacks", tuple(pltpu.VMEM(left.shape[1:], F32) for _ in range(count)), (left, right)
    )


def add_all(parts):
    def body(*refs):
        total = refs[0][...]
        for ref in refs[1:-1]:
            total = total + ref[...]
        refs[-1][...] = total

    return vmem_call(body, "add_all", pltpu.VMEM(parts[0].shape, F32), parts)


def stack_all(parts):
    def body(*refs):
        for r, ref in enumerate(refs[:-1]):
            refs[-1][r] = ref[...]

    return vmem_call(body, "stack_all", pltpu.VMEM((len(parts), *parts[0].shape), F32), parts)


def join_first(left, right, below):
    blocks, lanes = left.shape
    rows = below.shape[0]

    def body(left_ref, right_ref, below_ref, out_ref):
        out_ref[:blocks, :] = joined([left_ref[...], right_ref[...]])
        out_ref[blocks:, :] = jnp.concatenate([below_ref[...]] * (lanes // 128), axis=1)

    return vmem_call(body, "join_first", pltpu.VMEM((blocks + rows, lanes), F32), (left, right, below))


def join_more(left, right, blocks):
    count, lanes = left.shape

    def body(left_ref, right_ref, main_ref, index_ref):
        both = joined([left_ref[...], right_ref[...]])
        main_ref[...] = both[:blocks, :]
        index_ref[...] = both[blocks:, :128]

    outs = (pltpu.VMEM((blocks, lanes), F32), pltpu.VMEM((count - blocks, 128), F32))
    return vmem_call(body, "join_more", outs, (left, right))


def join_pair(left, right):
    def body(left_ref, right_ref, out_ref):
        out_ref[...] = joined([left_ref[...], right_ref[...]])

    return vmem_call(body, "join_pair", pltpu.VMEM(left.shape, F32), (left, right))


def query_part(scores, index_stats, targets, kl, gate, index_keys):
    rows, keys = scores.shape
    groups, size = gate.shape[:2]
    own = rows // groups
    heads = size // own
    width = index_keys.shape[1]
    half = keys // 2

    def body(score_ref, kl_ref, lse_ref, other_ref, gate_ref, keys_ref, *refs):
        target_refs, refs = refs[: len(targets)], refs[len(targets) :]
        keep_ref, send_ref, slope_ref, across_ref, delta_ref = refs
        whole = joined([lse_ref[:, :1], other_ref[:, :1]])
        target = target_refs[0][...]
        for ref in target_refs[1:]:
            target = target + ref[...]
        delta = kl_ref[:, :1] * (jnp.exp2(score_ref[...] - whole) - target)
        for g in range(groups):
            delta_ref[g] = delta[g * own : (g + 1) * own, :]
        z = lax.axis_index("keys")
        _, core = head_place()
        across_ref[...] = jnp.where(core == 0, delta[:, half:], delta[:, :half])
        for r in range(groups):
            lines = delta_ref[z ^ r]
            for i in range(own):
                line = jnp.broadcast_to(lines[i : i + 1, :], (heads, keys)).astype(BF16)
                signs = gate_ref[z ^ r, i * heads : (i + 1) * heads, :]
                at = r * size + i * heads
                slope_ref[at : at + heads, :] = jnp.where(signs > 0, line, jnp.zeros((), BF16))
        part = jnp.dot(slope_ref[...], keys_ref[...], preferred_element_type=F32)
        for r in range(groups):
            out_ref = send_ref if r % 2 else keep_ref
            out_ref[r // 2] = part[r * size : (r + 1) * size, :]

    side = pltpu.VMEM((groups // 2, size, width), F32)
    outs = (side, side, pltpu.VMEM((rows * heads, keys), BF16), pltpu.VMEM((rows, half), F32))
    scratch = [pltpu.VMEM((groups, own, keys), F32)]
    operands = (scores, kl, *index_stats, gate, index_keys, *targets)
    return vmem_call(body, "query_part", outs, operands, scratch, limit=16 * MIB)


def key_part(slopes, wiq, other_delta, other_gate, other_wiq, chips):
    groups, width, size = wiq.shape
    rows, half = other_delta.shape
    count = other_gate.shape[0]
    heads = count // rows
    chunk = half // chips

    def body(slope_ref, wiq_ref, delta_ref, gate_ref, other_ref, *refs):
        outs, (wiq_rows, other_slopes) = refs[:chips], refs[chips:]
        z = lax.axis_index("keys")
        for r in range(groups):
            wiq_rows[:, r * size : (r + 1) * size] = wiq_ref[z ^ r]
        for row in range(rows):
            span = slice(row * heads, (row + 1) * heads)
            line = jnp.broadcast_to(delta_ref[row : row + 1, :], (heads, half)).astype(BF16)
            other_slopes[span, :] = jnp.where(gate_ref[span, :] > 0, line, jnp.zeros((), BF16))
        chip, core = head_place()
        for n, out_ref in enumerate(outs):
            at = pl.multiple_of((chip ^ n) * chunk, chunk)
            here = pl.ds(pl.multiple_of(core * half + at, chunk), chunk)
            total = jnp.dot(wiq_rows[...], slope_ref[:, here], preferred_element_type=F32)
            total += jnp.dot(other_ref[...], other_slopes[:, pl.ds(at, chunk)], preferred_element_type=F32)
            out_ref[...] = total.T

    outs = tuple(pltpu.VMEM((chunk, width), F32) for _ in range(chips))
    scratch = [pltpu.VMEM((width, count), BF16), pltpu.VMEM((count, half), BF16)]
    operands = (slopes, wiq, other_delta, other_gate, other_wiq)
    return vmem_call(body, "key_part", outs, operands, scratch, limit=16 * MIB)


def add_halve(left, right):
    count = left.shape[0]

    def body(left_ref, right_ref, even_ref, odd_ref):
        for n in range(count):
            (odd_ref if n % 2 else even_ref)[n // 2] = left_ref[n] + right_ref[n]

    side = pltpu.VMEM((count // 2, *left.shape[1:]), F32)
    return vmem_call(body, "add_halve", (side, side), (left, right))


def own_rows(left, right, index_query, index_weight):
    rows, heads, width = index_query.shape
    size = left.shape[1]
    own = size // heads
    extra = -(-own // 8) * 8

    def body(query_ref, weight_ref, left_ref, right_ref, out_ref):
        first = lax.axis_index("keys") * own
        columns = weight_ref[...].T
        lane = lax.broadcasted_iota(jnp.int32, (heads, rows), 1)
        for i in range(own):
            span = slice(i * heads, (i + 1) * heads)
            total = left_ref[0, span, :] + right_ref[0, span, :]
            column = jnp.sum(jnp.where(lane == first + i, columns, 0.0), axis=1, keepdims=True)
            out_ref[span, :] = total * column
            summed = jnp.sum(total * query_ref[first + i].astype(F32), axis=1, keepdims=True)
            out_ref[size + i : size + i + 1, :] = jnp.concatenate(
                [summed.T, jnp.zeros((1, width - heads), F32)], axis=1
            )
        if extra > own:
            out_ref[size + own :, :] = jnp.zeros((extra - own, width), F32)

    out = pltpu.VMEM((size + extra, width), F32)
    return vmem_call(body, "own_rows", out, (index_query, index_weight, left, right), cost=LONG)


def place_query(pieces, rows, heads):
    own = rows // len(pieces)
    size = own * heads
    width = pieces[0].shape[1]
    order = list(pieces)

    def body(*refs):
        piece_refs, (query_out, weight_out, weights, sems) = refs[: len(pieces)], refs[len(pieces) :]
        z = lax.axis_index("keys")
        copies = []
        for r, ref in zip(order, piece_refs):
            at = pl.multiple_of((z ^ r) * size, size)
            copies.append(pltpu.make_async_copy(ref.at[:size], query_out.at[pl.ds(at, size)], sems.at[r]))
            copies[-1].start()
        for r, ref in zip(order, piece_refs):
            weights[pl.ds((z ^ r) * own, own), :] = ref[size : size + own, :heads]
        copies.append(pltpu.make_async_copy(weights, weight_out, sems.at[len(pieces)]))
        copies[-1].start()
        for copy in copies:
            copy.wait()

    query, weight = vmem_call(
        body,
        "place_query",
        (jax.ShapeDtypeStruct((rows * heads, width), F32), jax.ShapeDtypeStruct((rows, heads), F32)),
        list(pieces.values()),
        [pltpu.VMEM((rows, heads), F32), pltpu.SemaphoreType.DMA((len(pieces) + 1,))],
        out_specs=(any_spec, any_spec),
        cost=LONG,
    )
    return query.reshape(rows, heads, width), weight


def place_keys(mine, other):
    chips, chunk, width = mine.shape

    def body(mine_ref, other_ref, out_ref, sems):
        chip, core = head_place()
        copies = []
        for n, (ref, side) in enumerate(((mine_ref, core), (other_ref, 1 - core))):
            for r in range(chips):
                at = pl.multiple_of(side * (chips * chunk) + (chip ^ r) * chunk, chunk)
                copies.append(pltpu.make_async_copy(ref.at[r], out_ref.at[pl.ds(at, chunk)], sems.at[n, r]))
                copies[-1].start()
        for copy in copies:
            copy.wait()

    return vmem_call(
        body,
        "place_keys",
        jax.ShapeDtypeStruct((2 * chips * chunk, width), F32),
        (mine, other),
        [pltpu.SemaphoreType.DMA((2, chips))],
        out_specs=any_spec,
    )


def shards(main_query, latent_keys, index_query, index_keys, index_weight, query_pos, kl_weight):
    queries = main_query.shape[0]
    row_local, index_heads, _ = index_query.shape
    head_devices = lax.axis_size("heads")
    key_devices = lax.axis_size("keys")
    chips = head_devices // 2

    def to_keys(value, bits):
        return lax.ppermute(value, "keys", [(i, i ^ bits) for i in range(key_devices)])

    def to_heads(value, bits):
        return lax.ppermute(value, "heads", [(i, i ^ bits) for i in range(head_devices)])

    chip_order = list(reversed(range(1, chips)))
    key_order = [key_devices - 1] + list(range(1, key_devices - 1))

    probs, tops, stat = main_scores(query_pos[None, :], main_query.transpose(1, 2, 0), latent_keys.T)
    scores, index_lse, pack = index_forward(query_pos, index_query, index_keys, index_weight, stat)
    blocks = stat.shape[0]
    both = join_first(stat, to_keys(stat, 1), index_lse)
    bits = 2
    while bits < key_devices // 2:
        both = join_pair(both, to_keys(both, bits))
        bits *= 2
    stat, index_lse = join_more(both, to_keys(both, bits), blocks)
    keep, send = head_sum(probs, tops, stat, queries, row_local)
    index_lse, send, index_query, pack = lax.optimization_barrier((index_lse, send, index_query, pack))
    sums = add_stacks(keep, to_heads(send, 1))
    targets = [sums[0]] + [to_heads(sums[r], 2 * r) for r in chip_order]
    gate, wiq, kl = index_signs(kl_weight, index_query, index_keys, index_weight, key_devices)
    other_gate, other_wiq = other_signs(to_heads(pack, 1), index_keys, row_local)
    index_stats = (index_lse, to_keys(index_lse, 1))
    other_gate, gate = lax.optimization_barrier((other_gate, gate))
    even, odd, slopes, across = query_part(scores, index_stats, targets, kl, gate, index_keys)

    bits, other_odd = 1, to_keys(odd, 1)
    parts = key_part(slopes, wiq, to_heads(across, 1), other_gate, other_wiq, chips)
    key_own = add_all([parts[0]] + [to_heads(parts[r], 2 * r) for r in chip_order])
    while bits < key_devices // 2:
        even, odd = add_halve(even, other_odd)
        bits *= 2
        other_odd = to_keys(odd, bits)
    even, key_own = lax.optimization_barrier((even, key_own))
    query_own = own_rows(even, other_odd, index_query, index_weight)
    pieces = {0: query_own, **{r: to_keys(query_own, r) for r in key_order}}
    mine, bits = [key_own], 2
    while bits < head_devices:
        mine = mine + [to_heads(piece, bits) for piece in mine]
        bits *= 2
    mine = stack_all(mine)
    key_grad = place_keys(mine, to_heads(mine, 1))
    query_grad, weight_grad = place_query(pieces, row_local, index_heads)
    return query_grad, key_grad, weight_grad


def solution(mesh):
    placed = (
        P(None, "heads", None),
        P("keys", None),
        P("heads", None, None),
        P("keys", None),
        P("heads", None),
        P(),
        P("heads"),
    )
    return jax.shard_map(
        shards,
        mesh=mesh,
        in_specs=placed,
        out_specs=(P("heads", None, None), P("keys", None), P("heads", None)),
        check_vma=False,
    )
```

```python
import math

import jax
import jax.numpy as jnp
from jax import lax
from jax.experimental import pallas as pl
from jax.experimental.pallas import tpu as pltpu
from jax.sharding import PartitionSpec as P

H = 128

LOG2E = math.log2(math.e)
score_scale = 192.0 ** (-0.5) * LOG2E
masked_fill = -1e30

F32 = jnp.float32
BF16 = jnp.bfloat16
MIB = 1024 * 1024
SHORT = 0
LONG = 4 * 10**10

vmem_spec = pl.BlockSpec(memory_space=pltpu.VMEM)
smem_spec = pl.BlockSpec(memory_space=pltpu.SMEM)
any_spec = pl.BlockSpec(memory_space=pl.ANY)


def in_vmem(array):
    return pltpu.with_memory_space_constraint(array, pltpu.VMEM)


def in_hbm(array):
    return pltpu.with_memory_space_constraint(array, pltpu.HBM)


def vmem_call(
    body, name, outs, operands, scratch=(), out_specs=None, scalars=(), limit=12 * MIB, cost=0
):
    several = isinstance(outs, (tuple, list))
    if out_specs is None:
        out_specs = tuple(vmem_spec for _ in outs) if several else vmem_spec
    return pl.pallas_call(
        body,
        out_shape=outs,
        in_specs=[smem_spec] * len(scalars) + [vmem_spec] * len(operands),
        out_specs=out_specs,
        scratch_shapes=list(scratch),
        compiler_params=pltpu.CompilerParams(vmem_limit_bytes=limit),
        cost_estimate=pl.CostEstimate(flops=cost, bytes_accessed=0, transcendentals=0),
        name=name,
    )(*scalars, *[in_vmem(a) for a in operands])


def tile_of(extent, wanted):
    return wanted if extent % wanted == 0 else extent


def rows_of(ref, first, count):
    return ref[pl.ds(pl.multiple_of(first, count), count)]


def head_place():
    at = lax.axis_index("heads")
    return at // 2, at % 2


def weighted_columns(query_ref, columns, rows, heads):
    for row in range(rows):
        piece = query_ref[row * heads : (row + 1) * heads, :].astype(F32) * columns[:, row : row + 1]
        yield row, piece.T.astype(BF16)


def index_forward(query_pos, index_query, index_keys, index_weight, after):
    rows, heads, width = index_query.shape
    keys = index_keys.shape[0]
    tile = tile_of(keys, 256)

    def body(pos_ref, query_ref, keys_ref, weight_ref, _, score_ref, lse_ref, pack_ref):
        columns = weight_ref[...].T
        flat = query_ref[...].reshape(rows * heads, width)
        pack_ref[: rows * heads, :] = flat.astype(F32)
        pack_ref[rows * heads :, :] = jnp.concatenate(
            [weight_ref[...], jnp.zeros((rows, width - heads), F32)], axis=1
        )
        first_key = lax.axis_index("keys") * keys
        first_row = lax.axis_index("heads") * rows
        for at in range(0, keys, tile):
            logits = lax.dot_general(
                flat, keys_ref[at : at + tile, :], (((1,), (1,)), ((), ())), preferred_element_type=F32
            )
            index = first_key + at + lax.broadcasted_iota(jnp.int32, (1, tile), 1)
            for row in range(rows):
                active = jnp.maximum(logits[row * heads : (row + 1) * heads, :], 0.0)
                summed = jnp.sum(active * columns[:, row : row + 1], axis=0, keepdims=True)
                seen = index <= pos_ref[first_row + row]
                score_ref[row : row + 1, at : at + tile] = jnp.where(seen, summed * LOG2E, masked_fill)
        scores = score_ref[...]
        top = jnp.max(scores, axis=1, keepdims=True)
        total = jnp.sum(jnp.exp2(scores - top), axis=1, keepdims=True)
        lse_ref[...] = jnp.broadcast_to(top + jnp.log2(total), lse_ref.shape)

    outs = (
        pltpu.VMEM((rows, keys), F32),
        pltpu.VMEM((rows, 128), F32),
        pltpu.VMEM((rows * heads + rows, width), F32),
    )
    operands = (index_query, index_keys, index_weight, after)
    return vmem_call(body, "index_forward", outs, operands, scalars=(query_pos,), limit=16 * MIB)


def index_signs(kl, index_query, index_keys, index_weight, groups):
    rows, heads, width = index_query.shape
    keys = index_keys.shape[0]
    tile = tile_of(keys, 256)
    own = rows // groups
    size = own * heads

    def body(kl_ref, query_ref, keys_ref, weight_ref, gate_ref, wiq_ref, kl_out):
        for row in range(rows):
            kl_out[row : row + 1, :] = jnp.full((1, 128), kl_ref[row], F32)
        flat = query_ref[...].reshape(rows * heads, width)
        for row, piece in weighted_columns(flat, weight_ref[...].T, rows, heads):
            wiq_ref[row // own, :, (row % own) * heads : (row % own + 1) * heads] = piece
        for at in range(0, keys, tile):
            logits = lax.dot_general(
                flat, keys_ref[at : at + tile, :], (((1,), (1,)), ((), ())), preferred_element_type=F32
            )
            for g in range(groups):
                gate_ref[g, :, at : at + tile] = logits[g * size : (g + 1) * size, :].astype(BF16)

    outs = (
        pltpu.VMEM((groups, size, keys), BF16),
        pltpu.VMEM((groups, width, size), BF16),
        pltpu.VMEM((rows, 128), F32),
    )
    operands = (index_query, index_keys, index_weight)
    return vmem_call(body, "index_signs", outs, operands, scalars=(kl,), limit=16 * MIB)


def other_signs(pack, index_keys, rows):
    keys, width = index_keys.shape
    heads = pack.shape[0] // rows - 1
    half = keys // 2
    tile = tile_of(half, 256)

    def body(pack_ref, keys_ref, gate_ref, wiq_ref):
        flat = pack_ref[: rows * heads, :].astype(BF16)
        columns = pack_ref[rows * heads :, :].T[:heads, :]
        for row, piece in weighted_columns(flat, columns, rows, heads):
            wiq_ref[:, row * heads : (row + 1) * heads] = piece
        _, core = head_place()
        for at in range(0, half, tile):
            span = pl.ds(pl.multiple_of(core * half + at, tile), tile)
            gate_ref[:, at : at + tile] = lax.dot_general(
                flat, keys_ref[span, :], (((1,), (1,)), ((), ())), preferred_element_type=F32
            ).astype(BF16)

    outs = (pltpu.VMEM((rows * heads, half), BF16), pltpu.VMEM((width, rows * heads), BF16))
    return vmem_call(body, "other_signs", outs, (pack, index_keys), limit=16 * MIB)


def main_scores(pos, query_t, keys_t):
    head_local, feature, queries = query_t.shape
    keys = keys_t.shape[1]
    per = 256 // queries if queries < 256 and head_local % (256 // queries) == 0 else 1
    lanes = per * queries
    blocks = head_local // per
    many = 2 if blocks % 2 == 0 else 1
    tile = tile_of(keys, 128)
    tiles = keys // tile
    mask_at = -(-feature // 128) * 128
    depth = mask_at + -(-queries // 128) * 128

    def body(pos_ref, query_ref, keys_ref, prob_ref, top_ref, stat_ref, key_rows, weights):
        step = pl.program_id(0)

        @pl.when(step == 0)
        def _():
            chunk = tile_of(keys, 512)
            for at in range(0, keys, chunk):
                key_rows[at : at + chunk, :feature] = keys_ref[:, at : at + chunk].T
            if mask_at > feature:
                key_rows[:, feature:mask_at] = jnp.zeros((keys, mask_at - feature), BF16)
                weights[:, feature:mask_at, :] = jnp.zeros((many, mask_at - feature, lanes), BF16)
            index = lax.axis_index("keys") * keys + lax.broadcasted_iota(jnp.int32, (keys, queries), 0)
            hidden = jnp.where(index <= pos_ref[...], 0.0, masked_fill).astype(BF16)
            key_rows[:, mask_at : mask_at + queries] = hidden
            at_row = lax.broadcasted_iota(jnp.int32, (depth - mask_at, lanes), 0)
            at_lane = lax.broadcasted_iota(jnp.int32, (depth - mask_at, lanes), 1)
            for k in range(many):
                weights[k, mask_at:, :] = jnp.where(at_row == at_lane % queries, 1.0, 0.0).astype(BF16)
            if depth > mask_at + queries:
                key_rows[:, mask_at + queries :] = jnp.zeros((keys, depth - mask_at - queries), BF16)

        for k in range(many):
            for i in range(per):
                weights[k, :feature, i * queries : (i + 1) * queries] = query_ref[k * per + i]
        for k in range(many):
            block = step * many + k
            tops, totals = [], []
            for t in range(tiles):
                span = slice(t * tile, (t + 1) * tile)
                scores = jnp.dot(key_rows[span, :], weights[k], preferred_element_type=F32)
                top = jnp.max(scores, axis=0, keepdims=True)
                prob = jnp.exp2((scores - top) * score_scale)
                top = top * score_scale
                tops.append(top)
                totals.append(jnp.sum(prob, axis=0, keepdims=True))
                prob_ref[block, span, :] = prob.astype(prob_ref.dtype)
                top_ref[block, t : t + 1, :] = top
            best = tops[0]
            for top in tops[1:]:
                best = jnp.maximum(best, top)
            total = sum(s * jnp.exp2(top - best) for s, top in zip(totals, tops))
            stat_ref[pl.ds(block, 1), :] = best + jnp.log2(total)

    return pl.pallas_call(
        body,
        grid=(blocks // many,),
        out_shape=(
            pltpu.VMEM((blocks, keys, lanes), F32),
            pltpu.VMEM((blocks, tiles, lanes), F32),
            pltpu.VMEM((blocks, lanes), F32),
        ),
        in_specs=[
            pl.BlockSpec((1, queries), lambda i: (0, 0)),
            pl.BlockSpec((many * per, feature, queries), lambda i: (i, 0, 0)),
            pl.BlockSpec((feature, keys), lambda i: (0, 0)),
        ],
        out_specs=(vmem_spec,) * 3,
        scratch_shapes=[pltpu.VMEM((keys, depth), BF16), pltpu.VMEM((many, depth, lanes), BF16)],
        compiler_params=pltpu.CompilerParams(vmem_limit_bytes=16 * MIB),
        name="main_scores",
    )(in_hbm(pos), in_hbm(query_t), in_hbm(keys_t))


def joined(stats):
    best = stats[0]
    for stat in stats[1:]:
        best = jnp.maximum(best, stat)
    return best + jnp.log2(sum(jnp.exp2(stat - best) for stat in stats))


def head_sum(probs, tops, stat, queries, row_local):
    blocks, keys, lanes = probs.shape
    tiles = tops.shape[1]
    tile = keys // tiles
    per = lanes // queries
    chips = queries // row_local // 2

    def body(prob_ref, top_ref, stat_ref, keep_ref, send_ref, summed):
        whole = stat_ref[...]
        factors = [jnp.exp2(top_ref[b] - whole[b : b + 1, :]) * (1.0 / H) for b in range(blocks)]
        for t in range(tiles):
            span = slice(t * tile, (t + 1) * tile)
            total = None
            for b in range(blocks):
                part = prob_ref[b, span, :].astype(F32) * factors[b][t : t + 1, :]
                for i in range(per):
                    piece = part[:, i * queries : (i + 1) * queries]
                    total = piece if total is None else total + piece
            summed[:, span] = total.T
        chip, core = head_place()
        for r in range(chips):
            first = (chip ^ r) * 2
            keep_ref[r] = rows_of(summed, (first + core) * row_local, row_local)
            send_ref[r] = rows_of(summed, (first + 1 - core) * row_local, row_local)

    half = pltpu.VMEM((chips, row_local, keys), F32)
    return vmem_call(
        body, "head_sum", (half, half), (probs, tops, stat), [pltpu.VMEM((queries, keys), F32)], cost=10**9
    )


def add_stacks(left, right):
    count = left.shape[0]

    def body(left_ref, right_ref, *outs):
        for r in range(count):
            outs[r][...] = left_ref[r] + right_ref[r]

    return vmem_call(
        body, "add_stacks", tuple(pltpu.VMEM(left.shape[1:], F32) for _ in range(count)), (left, right)
    )


def add_all(parts):
    def body(*refs):
        total = refs[0][...]
        for ref in refs[1:-1]:
            total = total + ref[...]
        refs[-1][...] = total

    return vmem_call(body, "add_all", pltpu.VMEM(parts[0].shape, F32), parts)


def stack_all(parts):
    def body(*refs):
        for r, ref in enumerate(refs[:-1]):
            refs[-1][r] = ref[...]

    return vmem_call(body, "stack_all", pltpu.VMEM((len(parts), *parts[0].shape), F32), parts)


def join_first(left, right, below):
    blocks, lanes = left.shape
    rows = below.shape[0]

    def body(left_ref, right_ref, below_ref, out_ref):
        out_ref[:blocks, :] = joined([left_ref[...], right_ref[...]])
        out_ref[blocks:, :] = jnp.concatenate([below_ref[...]] * (lanes // 128), axis=1)

    return vmem_call(body, "join_first", pltpu.VMEM((blocks + rows, lanes), F32), (left, right, below))


def join_more(left, right, blocks):
    count, lanes = left.shape

    def body(left_ref, right_ref, main_ref, index_ref):
        both = joined([left_ref[...], right_ref[...]])
        main_ref[...] = both[:blocks, :]
        index_ref[...] = both[blocks:, :128]

    outs = (pltpu.VMEM((blocks, lanes), F32), pltpu.VMEM((count - blocks, 128), F32))
    return vmem_call(body, "join_more", outs, (left, right))


def join_pair(left, right):
    def body(left_ref, right_ref, out_ref):
        out_ref[...] = joined([left_ref[...], right_ref[...]])

    return vmem_call(body, "join_pair", pltpu.VMEM(left.shape, F32), (left, right))


def group_order(groups):
    return [*range(1, groups, 2), *range(0, groups, 2)]


def fill_slopes(delta_ref, gate_ref, slope_ref, order, z):
    own, keys = delta_ref.shape[1:]
    size = gate_ref.shape[1]
    heads = size // own
    for n, r in enumerate(order):
        lines = delta_ref[z ^ r]
        for i in range(own):
            line = jnp.broadcast_to(lines[i : i + 1, :], (heads, keys)).astype(BF16)
            signs = gate_ref[z ^ r, i * heads : (i + 1) * heads, :]
            at = n * size + i * heads
            slope_ref[at : at + heads, :] = jnp.where(signs > 0, line, jnp.zeros((), BF16))


def query_part(scores, index_stats, targets, kl, gate, index_keys):
    rows, keys = scores.shape
    groups, size = gate.shape[:2]
    own = rows // groups
    width = index_keys.shape[1]
    half = keys // 2
    order = group_order(groups)[: groups // 2]
    many = len(order)

    def body(score_ref, kl_ref, lse_ref, other_ref, gate_ref, keys_ref, *refs):
        target_refs, (send_ref, slope_ref, delta_ref, across_ref) = refs[: len(targets)], refs[len(targets) :]
        whole = joined([lse_ref[:, :1], other_ref[:, :1]])
        target = target_refs[0][...]
        for ref in target_refs[1:]:
            target = target + ref[...]
        delta = kl_ref[:, :1] * (jnp.exp2(score_ref[...] - whole) - target)
        for g in range(groups):
            delta_ref[g] = delta[g * own : (g + 1) * own, :]
        _, core = head_place()
        across_ref[...] = jnp.where(core == 0, delta[:, half:], delta[:, :half])
        fill_slopes(delta_ref, gate_ref, slope_ref, order, lax.axis_index("keys"))
        part = jnp.dot(slope_ref[...], keys_ref[...], preferred_element_type=F32)
        send_ref[...] = part.reshape(many, size, width)

    outs = (
        pltpu.VMEM((many, size, width), F32),
        pltpu.VMEM((many * size, keys), BF16),
        pltpu.VMEM((groups, own, keys), F32),
        pltpu.VMEM((rows, half), F32),
    )
    operands = (scores, kl, *index_stats, gate, index_keys, *targets)
    return vmem_call(body, "query_part", outs, operands, limit=16 * MIB)


def query_rest(delta, gate, index_keys):
    groups, size, keys = gate.shape
    width = index_keys.shape[1]
    order = group_order(groups)[groups // 2 :]
    many = len(order)

    def body(delta_ref, gate_ref, keys_ref, keep_ref, slope_ref):
        fill_slopes(delta_ref, gate_ref, slope_ref, order, lax.axis_index("keys"))
        part = jnp.dot(slope_ref[...], keys_ref[...], preferred_element_type=F32)
        keep_ref[...] = part.reshape(many, size, width)

    outs = (pltpu.VMEM((many, size, width), F32), pltpu.VMEM((many * size, keys), BF16))
    return vmem_call(body, "query_rest", outs, (delta, gate, index_keys), limit=16 * MIB)


def key_part(slopes, wiq, other_delta, other_gate, other_wiq, chips):
    groups, width, size = wiq.shape
    rows, half = other_delta.shape
    count = other_gate.shape[0]
    heads = count // rows
    chunk = half // chips
    first = slopes[0].shape[0]

    def body(odd_ref, even_ref, wiq_ref, delta_ref, gate_ref, other_ref, *refs):
        outs, (wiq_rows, other_slopes) = refs[:chips], refs[chips:]
        z = lax.axis_index("keys")
        for n, r in enumerate(group_order(groups)):
            wiq_rows[:, n * size : (n + 1) * size] = wiq_ref[z ^ r]
        for row in range(rows):
            span = slice(row * heads, (row + 1) * heads)
            line = jnp.broadcast_to(delta_ref[row : row + 1, :], (heads, half)).astype(BF16)
            other_slopes[span, :] = jnp.where(gate_ref[span, :] > 0, line, jnp.zeros((), BF16))
        chip, core = head_place()
        for n, out_ref in enumerate(outs):
            at = pl.multiple_of((chip ^ n) * chunk, chunk)
            here = pl.ds(pl.multiple_of(core * half + at, chunk), chunk)
            total = jnp.dot(wiq_rows[:, :first], odd_ref[:, here], preferred_element_type=F32)
            total += jnp.dot(wiq_rows[:, first:], even_ref[:, here], preferred_element_type=F32)
            total += jnp.dot(other_ref[...], other_slopes[:, pl.ds(at, chunk)], preferred_element_type=F32)
            out_ref[...] = total.T

    outs = tuple(pltpu.VMEM((chunk, width), F32) for _ in range(chips))
    scratch = [pltpu.VMEM((width, count), BF16), pltpu.VMEM((count, half), BF16)]
    operands = (*slopes, wiq, other_delta, other_gate, other_wiq)
    return vmem_call(body, "key_part", outs, operands, scratch, limit=16 * MIB)


def add_halve(left, right):
    count = left.shape[0]

    def body(left_ref, right_ref, even_ref, odd_ref):
        for n in range(count):
            (odd_ref if n % 2 else even_ref)[n // 2] = left_ref[n] + right_ref[n]

    side = pltpu.VMEM((count // 2, *left.shape[1:]), F32)
    return vmem_call(body, "add_halve", (side, side), (left, right))


def own_rows(left, right, index_query, index_weight):
    rows, heads, width = index_query.shape
    size = left.shape[1]
    own = size // heads
    extra = -(-own // 8) * 8

    def body(query_ref, weight_ref, left_ref, right_ref, out_ref):
        first = lax.axis_index("keys") * own
        columns = weight_ref[...].T
        lane = lax.broadcasted_iota(jnp.int32, (heads, rows), 1)
        for i in range(own):
            span = slice(i * heads, (i + 1) * heads)
            total = left_ref[0, span, :] + right_ref[0, span, :]
            column = jnp.sum(jnp.where(lane == first + i, columns, 0.0), axis=1, keepdims=True)
            out_ref[span, :] = total * column
            summed = jnp.sum(total * query_ref[first + i].astype(F32), axis=1, keepdims=True)
            out_ref[size + i : size + i + 1, :] = jnp.concatenate(
                [summed.T, jnp.zeros((1, width - heads), F32)], axis=1
            )
        if extra > own:
            out_ref[size + own :, :] = jnp.zeros((extra - own, width), F32)

    out = pltpu.VMEM((size + extra, width), F32)
    return vmem_call(body, "own_rows", out, (index_query, index_weight, left, right), cost=LONG)


def gather_weights(pieces, rows, heads):
    own = rows // len(pieces)
    size = own * heads
    order = list(pieces)

    def body(*refs):
        z = lax.axis_index("keys")
        for r, ref in zip(order, refs):
            refs[-1][pl.ds((z ^ r) * own, own), :] = ref[size : size + own, :heads]

    out = pltpu.VMEM((rows, heads), F32)
    return vmem_call(body, "gather_weights", out, list(pieces.values()), cost=LONG)


def place_all(pieces, weights, mine, other):
    rows, heads = weights.shape
    own = rows // len(pieces)
    size = own * heads
    order = list(pieces)
    count = len(order)
    chips, chunk, width = mine.shape

    def body(weight_ref, mine_ref, other_ref, *refs):
        piece_refs, (query_out, key_out, weight_out, sems) = refs[:count], refs[count:]
        z = lax.axis_index("keys")
        chip, core = head_place()
        pairs = [(weight_ref, weight_out)]
        for r, ref in zip(order, piece_refs):
            at = pl.multiple_of((z ^ r) * size, size)
            pairs.append((ref.at[:size], query_out.at[pl.ds(at, size)]))
        for ref, side in ((mine_ref, core), (other_ref, 1 - core)):
            for r in range(chips):
                at = pl.multiple_of(side * (chips * chunk) + (chip ^ r) * chunk, chunk)
                pairs.append((ref.at[r], key_out.at[pl.ds(at, chunk)]))
        copies = [pltpu.make_async_copy(*pair, sems.at[n]) for n, pair in enumerate(pairs)]
        for copy in copies:
            copy.start()
        for copy in copies:
            copy.wait()

    query, key, weight = vmem_call(
        body,
        "place_all",
        (
            jax.ShapeDtypeStruct((rows * heads, width), F32),
            jax.ShapeDtypeStruct((2 * chips * chunk, width), F32),
            jax.ShapeDtypeStruct((rows, heads), F32),
        ),
        (weights, mine, other, *pieces.values()),
        [pltpu.SemaphoreType.DMA((1 + count + 2 * chips,))],
        out_specs=(any_spec,) * 3,
    )
    return query.reshape(rows, heads, width), key, weight


def shards(main_query, latent_keys, index_query, index_keys, index_weight, query_pos, kl_weight):
    queries = main_query.shape[0]
    row_local, index_heads, _ = index_query.shape
    head_devices = lax.axis_size("heads")
    key_devices = lax.axis_size("keys")
    chips = head_devices // 2

    def to_keys(value, bits):
        return lax.ppermute(value, "keys", [(i, i ^ bits) for i in range(key_devices)])

    def to_heads(value, bits):
        return lax.ppermute(value, "heads", [(i, i ^ bits) for i in range(head_devices)])

    chip_order = list(reversed(range(1, chips)))
    key_order = [key_devices - 1] + list(range(1, key_devices - 1))

    probs, tops, stat = main_scores(query_pos[None, :], main_query.transpose(1, 2, 0), latent_keys.T)
    scores, index_lse, pack = index_forward(query_pos, index_query, index_keys, index_weight, stat)
    blocks = stat.shape[0]
    both = join_first(stat, to_keys(stat, 1), index_lse)
    bits = 2
    while bits < key_devices // 2:
        both = join_pair(both, to_keys(both, bits))
        bits *= 2
    stat, index_lse = join_more(both, to_keys(both, bits), blocks)
    keep, send = head_sum(probs, tops, stat, queries, row_local)
    index_lse, send, index_query, pack = lax.optimization_barrier((index_lse, send, index_query, pack))
    sums = add_stacks(keep, to_heads(send, 1))
    targets = [sums[0]] + [to_heads(sums[r], 2 * r) for r in chip_order]
    gate, wiq, kl = index_signs(kl_weight, index_query, index_keys, index_weight, key_devices)
    other_gate, other_wiq = other_signs(to_heads(pack, 1), index_keys, row_local)
    index_stats = (index_lse, to_keys(index_lse, 1))
    other_gate, gate = lax.optimization_barrier((other_gate, gate))
    odd, odd_slopes, delta, across = query_part(scores, index_stats, targets, kl, gate, index_keys)
    even, even_slopes = query_rest(delta, gate, index_keys)
    slopes = (odd_slopes, even_slopes)

    bits, other_odd = 1, to_keys(odd, 1)
    parts = key_part(slopes, wiq, to_heads(across, 1), other_gate, other_wiq, chips)
    key_own = add_all([parts[0]] + [to_heads(parts[r], 2 * r) for r in chip_order])
    while bits < key_devices // 2:
        even, odd = add_halve(even, other_odd)
        bits *= 2
        other_odd = to_keys(odd, bits)
    even, key_own = lax.optimization_barrier((even, key_own))
    query_own = own_rows(even, other_odd, index_query, index_weight)
    pieces = {0: query_own, **{r: to_keys(query_own, r) for r in key_order}}
    mine = {r: to_heads(key_own, 2 * r) for r in range(1, chips)}
    mine = [key_own] + [mine[r] for r in range(1, chips)]
    mine = stack_all(mine)
    weights = gather_weights(pieces, row_local, index_heads)
    return place_all(pieces, weights, mine, to_heads(mine, 1))


def solution(mesh):
    placed = (
        P(None, "heads", None),
        P("keys", None),
        P("heads", None, None),
        P("keys", None),
        P("heads", None),
        P(),
        P("heads"),
    )
    return jax.shard_map(
        shards,
        mesh=mesh,
        in_specs=placed,
        out_specs=(P("heads", None, None), P("keys", None), P("heads", None)),
        check_vma=False,
    )
```

```python
import math

import jax
import jax.numpy as jnp
from jax import lax
from jax.experimental import pallas as pl
from jax.experimental.pallas import tpu as pltpu
from jax.sharding import PartitionSpec as P

H = 128

LOG2E = math.log2(math.e)
score_scale = 192.0 ** (-0.5) * LOG2E
masked_fill = -1e30

F32 = jnp.float32
BF16 = jnp.bfloat16
MIB = 1024 * 1024
LONG = 4 * 10**10

vmem_spec = pl.BlockSpec(memory_space=pltpu.VMEM)
smem_spec = pl.BlockSpec(memory_space=pltpu.SMEM)
any_spec = pl.BlockSpec(memory_space=pl.ANY)


def in_vmem(array):
    return pltpu.with_memory_space_constraint(array, pltpu.VMEM)


def in_hbm(array):
    return pltpu.with_memory_space_constraint(array, pltpu.HBM)


def vmem_call(
    body, name, outs, operands, scratch=(), out_specs=None, scalars=(), limit=12 * MIB, cost=0
):
    several = isinstance(outs, (tuple, list))
    if out_specs is None:
        out_specs = tuple(vmem_spec for _ in outs) if several else vmem_spec
    return pl.pallas_call(
        body,
        out_shape=outs,
        in_specs=[smem_spec] * len(scalars) + [vmem_spec] * len(operands),
        out_specs=out_specs,
        scratch_shapes=list(scratch),
        compiler_params=pltpu.CompilerParams(vmem_limit_bytes=limit),
        cost_estimate=pl.CostEstimate(flops=cost, bytes_accessed=0, transcendentals=0),
        name=name,
    )(*scalars, *[in_vmem(a) for a in operands])


def tile_of(extent, wanted):
    return wanted if extent % wanted == 0 else extent


def rows_of(ref, first, count):
    return ref[pl.ds(pl.multiple_of(first, count), count)]


def head_place():
    at = lax.axis_index("heads")
    return at // 2, at % 2


def weighted_columns(query_ref, columns, rows, heads):
    for row in range(rows):
        piece = query_ref[row * heads : (row + 1) * heads, :].astype(F32) * columns[:, row : row + 1]
        yield row, piece.T.astype(BF16)


def index_forward(query_pos, index_query, index_keys, index_weight, after):
    rows, heads, width = index_query.shape
    keys = index_keys.shape[0]
    tile = tile_of(keys, 256)

    def body(pos_ref, query_ref, keys_ref, weight_ref, _, score_ref, lse_ref, pack_ref):
        columns = weight_ref[...].T
        flat = query_ref[...].reshape(rows * heads, width)
        pack_ref[: rows * heads, :] = flat.astype(F32)
        pack_ref[rows * heads :, :] = jnp.concatenate(
            [weight_ref[...], jnp.zeros((rows, width - heads), F32)], axis=1
        )
        first_key = lax.axis_index("keys") * keys
        first_row = lax.axis_index("heads") * rows
        for at in range(0, keys, tile):
            logits = lax.dot_general(
                flat, keys_ref[at : at + tile, :], (((1,), (1,)), ((), ())), preferred_element_type=F32
            )
            index = first_key + at + lax.broadcasted_iota(jnp.int32, (1, tile), 1)
            for row in range(rows):
                active = jnp.maximum(logits[row * heads : (row + 1) * heads, :], 0.0)
                summed = jnp.sum(active * columns[:, row : row + 1], axis=0, keepdims=True)
                seen = index <= pos_ref[first_row + row]
                score_ref[row : row + 1, at : at + tile] = jnp.where(seen, summed * LOG2E, masked_fill)
        scores = score_ref[...]
        top = jnp.max(scores, axis=1, keepdims=True)
        total = jnp.sum(jnp.exp2(scores - top), axis=1, keepdims=True)
        lse_ref[...] = jnp.broadcast_to(top + jnp.log2(total), lse_ref.shape)

    outs = (
        pltpu.VMEM((rows, keys), F32),
        pltpu.VMEM((rows, 128), F32),
        pltpu.VMEM((rows * heads + rows, width), F32),
    )
    operands = (index_query, index_keys, index_weight, after)
    return vmem_call(body, "index_forward", outs, operands, scalars=(query_pos,), limit=16 * MIB)


def index_signs(kl, index_query, index_keys, index_weight, groups):
    rows, heads, width = index_query.shape
    keys = index_keys.shape[0]
    tile = tile_of(keys, 256)
    own = rows // groups
    size = own * heads

    def body(kl_ref, query_ref, keys_ref, weight_ref, gate_ref, wiq_ref, kl_out):
        for row in range(rows):
            kl_out[row : row + 1, :] = jnp.full((1, 128), kl_ref[row], F32)
        flat = query_ref[...].reshape(rows * heads, width)
        for row, piece in weighted_columns(flat, weight_ref[...].T, rows, heads):
            wiq_ref[row // own, :, (row % own) * heads : (row % own + 1) * heads] = piece
        for at in range(0, keys, tile):
            logits = lax.dot_general(
                flat, keys_ref[at : at + tile, :], (((1,), (1,)), ((), ())), preferred_element_type=F32
            )
            for g in range(groups):
                gate_ref[g, :, at : at + tile] = logits[g * size : (g + 1) * size, :].astype(BF16)

    outs = (
        pltpu.VMEM((groups, size, keys), BF16),
        pltpu.VMEM((groups, width, size), BF16),
        pltpu.VMEM((rows, 128), F32),
    )
    operands = (index_query, index_keys, index_weight)
    return vmem_call(body, "index_signs", outs, operands, scalars=(kl,), limit=16 * MIB)


def other_signs(pack, index_keys, rows):
    keys, width = index_keys.shape
    heads = pack.shape[0] // rows - 1
    half = keys // 2
    tile = tile_of(half, 256)

    def body(pack_ref, keys_ref, gate_ref, wiq_ref):
        flat = pack_ref[: rows * heads, :].astype(BF16)
        columns = pack_ref[rows * heads :, :].T[:heads, :]
        for row, piece in weighted_columns(flat, columns, rows, heads):
            wiq_ref[:, row * heads : (row + 1) * heads] = piece
        _, core = head_place()
        for at in range(0, half, tile):
            span = pl.ds(pl.multiple_of(core * half + at, tile), tile)
            gate_ref[:, at : at + tile] = lax.dot_general(
                flat, keys_ref[span, :], (((1,), (1,)), ((), ())), preferred_element_type=F32
            ).astype(BF16)

    outs = (pltpu.VMEM((rows * heads, half), BF16), pltpu.VMEM((width, rows * heads), BF16))
    return vmem_call(body, "other_signs", outs, (pack, index_keys), limit=16 * MIB)


def main_scores(pos, query_t, keys_t):
    head_local, feature, queries = query_t.shape
    keys = keys_t.shape[1]
    per = 256 // queries if queries < 256 and head_local % (256 // queries) == 0 else 1
    lanes = per * queries
    blocks = head_local // per
    many = 4 if blocks % 4 == 0 else 1
    tile = tile_of(keys, 128)
    tiles = keys // tile
    mask_at = -(-feature // 128) * 128
    depth = mask_at + -(-queries // 128) * 128

    def body(pos_ref, query_ref, keys_ref, prob_ref, top_ref, stat_ref, key_rows, weights):
        step = pl.program_id(0)

        @pl.when(step == 0)
        def _():
            chunk = tile_of(keys, 512)
            for at in range(0, keys, chunk):
                key_rows[at : at + chunk, :feature] = keys_ref[:, at : at + chunk].T
            if mask_at > feature:
                key_rows[:, feature:mask_at] = jnp.zeros((keys, mask_at - feature), BF16)
                weights[:, feature:mask_at, :] = jnp.zeros((many, mask_at - feature, lanes), BF16)
            index = lax.axis_index("keys") * keys + lax.broadcasted_iota(jnp.int32, (keys, queries), 0)
            hidden = jnp.where(index <= pos_ref[...], 0.0, masked_fill).astype(BF16)
            key_rows[:, mask_at : mask_at + queries] = hidden
            at_row = lax.broadcasted_iota(jnp.int32, (depth - mask_at, lanes), 0)
            at_lane = lax.broadcasted_iota(jnp.int32, (depth - mask_at, lanes), 1)
            for k in range(many):
                weights[k, mask_at:, :] = jnp.where(at_row == at_lane % queries, 1.0, 0.0).astype(BF16)
            if depth > mask_at + queries:
                key_rows[:, mask_at + queries :] = jnp.zeros((keys, depth - mask_at - queries), BF16)

        for k in range(many):
            for i in range(per):
                weights[k, :feature, i * queries : (i + 1) * queries] = query_ref[k * per + i]
        for k in range(many):
            block = step * many + k
            tops, totals = [], []
            for t in range(tiles):
                span = slice(t * tile, (t + 1) * tile)
                scores = jnp.dot(key_rows[span, :], weights[k], preferred_element_type=F32)
                top = jnp.max(scores, axis=0, keepdims=True)
                prob = jnp.exp2((scores - top) * score_scale)
                top = top * score_scale
                tops.append(top)
                totals.append(jnp.sum(prob, axis=0, keepdims=True))
                prob_ref[block, span, :] = prob.astype(prob_ref.dtype)
                top_ref[block, t : t + 1, :] = top
            best = tops[0]
            for top in tops[1:]:
                best = jnp.maximum(best, top)
            total = sum(s * jnp.exp2(top - best) for s, top in zip(totals, tops))
            stat_ref[pl.ds(block, 1), :] = best + jnp.log2(total)

    return pl.pallas_call(
        body,
        grid=(blocks // many,),
        out_shape=(
            pltpu.VMEM((blocks, keys, lanes), F32),
            pltpu.VMEM((blocks, tiles, lanes), F32),
            pltpu.VMEM((blocks, lanes), F32),
        ),
        in_specs=[
            pl.BlockSpec((1, queries), lambda i: (0, 0)),
            pl.BlockSpec((many * per, feature, queries), lambda i: (i, 0, 0)),
            pl.BlockSpec((feature, keys), lambda i: (0, 0)),
        ],
        out_specs=(vmem_spec,) * 3,
        scratch_shapes=[pltpu.VMEM((keys, depth), BF16), pltpu.VMEM((many, depth, lanes), BF16)],
        compiler_params=pltpu.CompilerParams(vmem_limit_bytes=16 * MIB),
        name="main_scores",
    )(in_hbm(pos), in_hbm(query_t), in_hbm(keys_t))


def joined(stats):
    best = stats[0]
    for stat in stats[1:]:
        best = jnp.maximum(best, stat)
    return best + jnp.log2(sum(jnp.exp2(stat - best) for stat in stats))


def head_sum(probs, tops, stat, queries, row_local):
    blocks, keys, lanes = probs.shape
    tiles = tops.shape[1]
    tile = keys // tiles
    per = lanes // queries
    chips = queries // row_local // 2

    def body(prob_ref, top_ref, stat_ref, keep_ref, send_ref, summed):
        whole = stat_ref[...]
        factors = [jnp.exp2(top_ref[b] - whole[b : b + 1, :]) * (1.0 / H) for b in range(blocks)]
        for t in range(tiles):
            span = slice(t * tile, (t + 1) * tile)
            total = None
            for b in range(blocks):
                part = prob_ref[b, span, :].astype(F32) * factors[b][t : t + 1, :]
                for i in range(per):
                    piece = part[:, i * queries : (i + 1) * queries]
                    total = piece if total is None else total + piece
            summed[:, span] = total.T
        chip, core = head_place()
        for r in range(chips):
            first = (chip ^ r) * 2
            keep_ref[r] = rows_of(summed, (first + core) * row_local, row_local)
            send_ref[r] = rows_of(summed, (first + 1 - core) * row_local, row_local)

    half = pltpu.VMEM((chips, row_local, keys), F32)
    return vmem_call(
        body, "head_sum", (half, half), (probs, tops, stat), [pltpu.VMEM((queries, keys), F32)], cost=10**9
    )


def add_stacks(left, right):
    count = left.shape[0]

    def body(left_ref, right_ref, *outs):
        for r in range(count):
            outs[r][...] = left_ref[r] + right_ref[r]

    return vmem_call(
        body, "add_stacks", tuple(pltpu.VMEM(left.shape[1:], F32) for _ in range(count)), (left, right)
    )


def add_all(parts):
    count, width = parts[0].shape

    def body(*refs):
        total = refs[0][...]
        for ref in refs[1:-2]:
            total = total + ref[...]
        refs[-2][...] = total
        refs[-1][:count, :] = total
        refs[-1][count:, :] = jnp.zeros((16, width), F32)

    outs = (pltpu.VMEM((count, width), F32), pltpu.VMEM((count + 16, width), F32))
    return vmem_call(body, "add_all", outs, parts)


def stack_chips(parts):
    chunk, width = parts[0].shape

    def body(*refs):
        chip, _ = head_place()
        for r, ref in enumerate(refs[:-1]):
            refs[-1][pl.ds(pl.multiple_of((chip ^ r) * chunk, chunk), chunk), :] = ref[:chunk, :]

    return vmem_call(body, "stack_chips", pltpu.VMEM((len(parts) * chunk, width), F32), parts)


def join_first(left, right, below):
    blocks, lanes = left.shape
    rows = below.shape[0]

    def body(left_ref, right_ref, below_ref, out_ref):
        out_ref[:blocks, :] = joined([left_ref[...], right_ref[...]])
        out_ref[blocks:, :] = jnp.concatenate([below_ref[...]] * (lanes // 128), axis=1)

    return vmem_call(body, "join_first", pltpu.VMEM((blocks + rows, lanes), F32), (left, right, below))


def join_more(left, right, blocks):
    count, lanes = left.shape

    def body(left_ref, right_ref, main_ref, index_ref):
        both = joined([left_ref[...], right_ref[...]])
        main_ref[...] = both[:blocks, :]
        index_ref[...] = both[blocks:, :128]

    outs = (pltpu.VMEM((blocks, lanes), F32), pltpu.VMEM((count - blocks, 128), F32))
    return vmem_call(body, "join_more", outs, (left, right))


def join_pair(left, right):
    def body(left_ref, right_ref, out_ref):
        out_ref[...] = joined([left_ref[...], right_ref[...]])

    return vmem_call(body, "join_pair", pltpu.VMEM(left.shape, F32), (left, right))


def group_order(groups):
    return [*range(1, groups, 2), *range(0, groups, 2)]


def fill_slopes(delta_ref, gate_ref, slope_ref, order, z):
    own, keys = delta_ref.shape[1:]
    size = gate_ref.shape[1]
    heads = size // own
    for n, r in enumerate(order):
        lines = delta_ref[z ^ r]
        for i in range(own):
            line = jnp.broadcast_to(lines[i : i + 1, :], (heads, keys)).astype(BF16)
            signs = gate_ref[z ^ r, i * heads : (i + 1) * heads, :]
            at = n * size + i * heads
            slope_ref[at : at + heads, :] = jnp.where(signs > 0, line, jnp.zeros((), BF16))


def query_part(scores, index_stats, targets, kl, gate, index_keys):
    rows, keys = scores.shape
    groups, size = gate.shape[:2]
    own = rows // groups
    width = index_keys.shape[1]
    half = keys // 2
    order = group_order(groups)[: groups // 2]
    many = len(order)

    def body(score_ref, kl_ref, lse_ref, other_ref, gate_ref, keys_ref, *refs):
        target_refs, (send_ref, slope_ref, delta_ref, across_ref) = refs[: len(targets)], refs[len(targets) :]
        whole = joined([lse_ref[:, :1], other_ref[:, :1]])
        target = target_refs[0][...]
        for ref in target_refs[1:]:
            target = target + ref[...]
        delta = kl_ref[:, :1] * (jnp.exp2(score_ref[...] - whole) - target)
        for g in range(groups):
            delta_ref[g] = delta[g * own : (g + 1) * own, :]
        _, core = head_place()
        across_ref[...] = jnp.where(core == 0, delta[:, half:], delta[:, :half])
        fill_slopes(delta_ref, gate_ref, slope_ref, order, lax.axis_index("keys"))
        part = jnp.dot(slope_ref[...], keys_ref[...], preferred_element_type=F32)
        send_ref[...] = part.reshape(many, size, width)

    outs = (
        pltpu.VMEM((many, size, width), F32),
        pltpu.VMEM((many * size, keys), BF16),
        pltpu.VMEM((groups, own, keys), F32),
        pltpu.VMEM((rows, half), F32),
    )
    operands = (scores, kl, *index_stats, gate, index_keys, *targets)
    return vmem_call(body, "query_part", outs, operands, limit=16 * MIB)


def query_rest(delta, gate, index_keys):
    groups, size, keys = gate.shape
    width = index_keys.shape[1]
    order = group_order(groups)[groups // 2 :]
    many = len(order)

    def body(delta_ref, gate_ref, keys_ref, keep_ref, slope_ref):
        fill_slopes(delta_ref, gate_ref, slope_ref, order, lax.axis_index("keys"))
        part = jnp.dot(slope_ref[...], keys_ref[...], preferred_element_type=F32)
        keep_ref[...] = part.reshape(many, size, width)

    outs = (pltpu.VMEM((many, size, width), F32), pltpu.VMEM((many * size, keys), BF16))
    return vmem_call(body, "query_rest", outs, (delta, gate, index_keys), limit=16 * MIB)


def key_part(slopes, wiq, other_delta, other_gate, other_wiq, chips):
    groups, width, size = wiq.shape
    rows, half = other_delta.shape
    count = other_gate.shape[0]
    heads = count // rows
    chunk = half // chips
    first = slopes[0].shape[0]

    def body(odd_ref, even_ref, wiq_ref, delta_ref, gate_ref, other_ref, *refs):
        outs, (wiq_rows, other_slopes) = refs[:chips], refs[chips:]
        z = lax.axis_index("keys")
        for n, r in enumerate(group_order(groups)):
            wiq_rows[:, n * size : (n + 1) * size] = wiq_ref[z ^ r]
        for row in range(rows):
            span = slice(row * heads, (row + 1) * heads)
            line = jnp.broadcast_to(delta_ref[row : row + 1, :], (heads, half)).astype(BF16)
            other_slopes[span, :] = jnp.where(gate_ref[span, :] > 0, line, jnp.zeros((), BF16))
        chip, core = head_place()
        for n, out_ref in enumerate(outs):
            at = pl.multiple_of((chip ^ n) * chunk, chunk)
            here = pl.ds(pl.multiple_of(core * half + at, chunk), chunk)
            total = jnp.dot(wiq_rows[:, :first], odd_ref[:, here], preferred_element_type=F32)
            total += jnp.dot(wiq_rows[:, first:], even_ref[:, here], preferred_element_type=F32)
            total += jnp.dot(other_ref[...], other_slopes[:, pl.ds(at, chunk)], preferred_element_type=F32)
            out_ref[...] = total.T

    outs = tuple(pltpu.VMEM((chunk, width), F32) for _ in range(chips))
    scratch = [pltpu.VMEM((width, count), BF16), pltpu.VMEM((count, half), BF16)]
    operands = (*slopes, wiq, other_delta, other_gate, other_wiq)
    return vmem_call(body, "key_part", outs, operands, scratch, limit=16 * MIB)


def add_halve(left, right):
    count = left.shape[0]

    def body(left_ref, right_ref, even_ref, odd_ref):
        for n in range(count):
            (odd_ref if n % 2 else even_ref)[n // 2] = left_ref[n] + right_ref[n]

    side = pltpu.VMEM((count // 2, *left.shape[1:]), F32)
    return vmem_call(body, "add_halve", (side, side), (left, right))


def own_rows(left, right, index_query, index_weight):
    rows, heads, width = index_query.shape
    size = left.shape[1]
    own = size // heads
    extra = -(-own // 8) * 8

    def body(query_ref, weight_ref, left_ref, right_ref, out_ref):
        first = lax.axis_index("keys") * own
        columns = weight_ref[...].T
        lane = lax.broadcasted_iota(jnp.int32, (heads, rows), 1)
        for i in range(own):
            span = slice(i * heads, (i + 1) * heads)
            total = left_ref[0, span, :] + right_ref[0, span, :]
            column = jnp.sum(jnp.where(lane == first + i, columns, 0.0), axis=1, keepdims=True)
            out_ref[span, :] = total * column
            summed = jnp.sum(total * query_ref[first + i].astype(F32), axis=1, keepdims=True)
            out_ref[size + i : size + i + 1, :] = jnp.concatenate(
                [summed.T, jnp.zeros((1, width - heads), F32)], axis=1
            )
        if extra > own:
            out_ref[size + own :, :] = jnp.zeros((extra - own, width), F32)

    out = pltpu.VMEM((size + extra, width), F32)
    return vmem_call(body, "own_rows", out, (index_query, index_weight, left, right), cost=LONG)


def gather_weights(pieces, rows, heads):
    own = rows // len(pieces)
    size = own * heads
    order = list(pieces)

    def body(*refs):
        z = lax.axis_index("keys")
        for r, ref in zip(order, refs):
            refs[-1][pl.ds((z ^ r) * own, own), :] = ref[size : size + own, :heads]

    out = pltpu.VMEM((rows, heads), F32)
    return vmem_call(body, "gather_weights", out, list(pieces.values()), cost=LONG)


def place_all(pieces, weights, mine, other):
    rows, heads = weights.shape
    size = rows // len(pieces) * heads
    order = list(pieces)
    count = len(order)
    half, width = mine.shape

    def body(weight_ref, mine_ref, other_ref, *refs):
        piece_refs, (query_out, key_out, weight_out, sems) = refs[:count], refs[count:]
        z = lax.axis_index("keys")
        _, core = head_place()
        pairs = [(weight_ref, weight_out)]
        for r, ref in zip(order, piece_refs):
            at = pl.multiple_of((z ^ r) * size, size)
            pairs.append((ref.at[:size], query_out.at[pl.ds(at, size)]))
        for ref, side in ((mine_ref, core), (other_ref, 1 - core)):
            pairs.append((ref, key_out.at[pl.ds(pl.multiple_of(side * half, half), half)]))
        copies = [pltpu.make_async_copy(*pair, sems.at[n]) for n, pair in enumerate(pairs)]
        for copy in copies:
            copy.start()
        for copy in copies:
            copy.wait()

    query, key, weight = vmem_call(
        body,
        "place_all",
        (
            jax.ShapeDtypeStruct((rows * heads, width), F32),
            jax.ShapeDtypeStruct((2 * half, width), F32),
            jax.ShapeDtypeStruct((rows, heads), F32),
        ),
        (weights, mine, other, *pieces.values()),
        [pltpu.SemaphoreType.DMA((3 + count,))],
        out_specs=(any_spec,) * 3,
    )
    return query.reshape(rows, heads, width), key, weight


def shards(main_query, latent_keys, index_query, index_keys, index_weight, query_pos, kl_weight):
    queries = main_query.shape[0]
    row_local, index_heads, _ = index_query.shape
    head_devices = lax.axis_size("heads")
    key_devices = lax.axis_size("keys")
    chips = head_devices // 2

    def to_keys(value, bits):
        return lax.ppermute(value, "keys", [(i, i ^ bits) for i in range(key_devices)])

    def to_heads(value, bits):
        return lax.ppermute(value, "heads", [(i, i ^ bits) for i in range(head_devices)])

    chip_order = list(reversed(range(1, chips)))
    key_order = [key_devices - 1] + list(range(1, key_devices - 1))

    probs, tops, stat = main_scores(query_pos[None, :], main_query.transpose(1, 2, 0), latent_keys.T)
    scores, index_lse, pack = index_forward(query_pos, index_query, index_keys, index_weight, stat)
    blocks = stat.shape[0]
    both = join_first(stat, to_keys(stat, 1), index_lse)
    bits = 2
    while bits < key_devices // 2:
        both = join_pair(both, to_keys(both, bits))
        bits *= 2
    stat, index_lse = join_more(both, to_keys(both, bits), blocks)
    keep, send = head_sum(probs, tops, stat, queries, row_local)
    index_lse, send, index_query, pack = lax.optimization_barrier((index_lse, send, index_query, pack))
    sums = add_stacks(keep, to_heads(send, 1))
    targets = [sums[0]] + [to_heads(sums[r], 2 * r) for r in chip_order]
    gate, wiq, kl = index_signs(kl_weight, index_query, index_keys, index_weight, key_devices)
    other_gate, other_wiq = other_signs(to_heads(pack, 1), index_keys, row_local)
    index_stats = (index_lse, to_keys(index_lse, 1))
    other_gate, gate = lax.optimization_barrier((other_gate, gate))
    odd, odd_slopes, delta, across = query_part(scores, index_stats, targets, kl, gate, index_keys)
    even, even_slopes = query_rest(delta, gate, index_keys)
    slopes = (odd_slopes, even_slopes)

    bits, other_odd = 1, to_keys(odd, 1)
    parts = key_part(slopes, wiq, to_heads(across, 1), other_gate, other_wiq, chips)
    key_own, key_wide = add_all([parts[0]] + [to_heads(parts[r], 2 * r) for r in chip_order])
    while bits < key_devices // 2:
        even, odd = add_halve(even, other_odd)
        bits *= 2
        other_odd = to_keys(odd, bits)
    even, key_own = lax.optimization_barrier((even, key_own))
    query_own = own_rows(even, other_odd, index_query, index_weight)
    pieces = {0: query_own, **{r: to_keys(query_own, r) for r in key_order}}
    mine = {r: to_heads(key_own if r == chips - 1 else key_wide, 2 * r) for r in range(1, chips)}
    mine = [key_own] + [mine[r] for r in range(1, chips)]
    mine = stack_chips(mine)
    weights = gather_weights(pieces, row_local, index_heads)
    return place_all(pieces, weights, mine, to_heads(mine, 1))


def solution(mesh):
    placed = (
        P(None, "heads", None),
        P("keys", None),
        P("heads", None, None),
        P("keys", None),
        P("heads", None),
        P(),
        P("heads"),
    )
    return jax.shard_map(
        shards,
        mesh=mesh,
        in_specs=placed,
        out_specs=(P("heads", None, None), P("keys", None), P("heads", None)),
        check_vma=False,
    )
```

```python
import math

import jax
import jax.numpy as jnp
from jax import lax
from jax.experimental import pallas as pl
from jax.experimental.pallas import tpu as pltpu
from jax.sharding import PartitionSpec as P

H = 128

LOG2E = math.log2(math.e)
score_scale = 192.0 ** (-0.5) * LOG2E
masked_fill = -1e30

F32 = jnp.float32
BF16 = jnp.bfloat16
MIB = 1024 * 1024
LONG = 4 * 10**10

vmem_spec = pl.BlockSpec(memory_space=pltpu.VMEM)
smem_spec = pl.BlockSpec(memory_space=pltpu.SMEM)
any_spec = pl.BlockSpec(memory_space=pl.ANY)


def in_vmem(array):
    return pltpu.with_memory_space_constraint(array, pltpu.VMEM)


def in_hbm(array):
    return pltpu.with_memory_space_constraint(array, pltpu.HBM)


def vmem_call(
    body, name, outs, operands, scratch=(), out_specs=None, scalars=(), limit=12 * MIB, cost=0
):
    several = isinstance(outs, (tuple, list))
    if out_specs is None:
        out_specs = tuple(vmem_spec for _ in outs) if several else vmem_spec
    return pl.pallas_call(
        body,
        out_shape=outs,
        in_specs=[smem_spec] * len(scalars) + [vmem_spec] * len(operands),
        out_specs=out_specs,
        scratch_shapes=list(scratch),
        compiler_params=pltpu.CompilerParams(vmem_limit_bytes=limit),
        cost_estimate=pl.CostEstimate(flops=cost, bytes_accessed=0, transcendentals=0),
        name=name,
    )(*scalars, *[in_vmem(a) for a in operands])


def tile_of(extent, wanted):
    return wanted if extent % wanted == 0 else extent


def rows_of(ref, first, count):
    return ref[pl.ds(pl.multiple_of(first, count), count)]


def head_place():
    at = lax.axis_index("heads")
    return at // 2, at % 2


def weighted_columns(query_ref, columns, rows, heads):
    for row in range(rows):
        piece = query_ref[row * heads : (row + 1) * heads, :].astype(F32) * columns[:, row : row + 1]
        yield row, piece.T.astype(BF16)


def index_forward(query_pos, index_query, index_keys, index_weight, after):
    rows, heads, width = index_query.shape
    keys = index_keys.shape[0]
    tile = tile_of(keys, 256)

    def body(pos_ref, query_ref, keys_ref, weight_ref, _, score_ref, lse_ref, pack_ref):
        columns = weight_ref[...].T
        flat = query_ref[...].reshape(rows * heads, width)
        pack_ref[: rows * heads, :] = flat.astype(F32)
        pack_ref[rows * heads :, :] = jnp.concatenate(
            [weight_ref[...], jnp.zeros((rows, width - heads), F32)], axis=1
        )
        first_key = lax.axis_index("keys") * keys
        first_row = lax.axis_index("heads") * rows
        for at in range(0, keys, tile):
            logits = lax.dot_general(
                flat, keys_ref[at : at + tile, :], (((1,), (1,)), ((), ())), preferred_element_type=F32
            )
            index = first_key + at + lax.broadcasted_iota(jnp.int32, (1, tile), 1)
            for row in range(rows):
                active = jnp.maximum(logits[row * heads : (row + 1) * heads, :], 0.0)
                summed = jnp.sum(active * columns[:, row : row + 1], axis=0, keepdims=True)
                seen = index <= pos_ref[first_row + row]
                score_ref[row : row + 1, at : at + tile] = jnp.where(seen, summed * LOG2E, masked_fill)
        scores = score_ref[...]
        top = jnp.max(scores, axis=1, keepdims=True)
        total = jnp.sum(jnp.exp2(scores - top), axis=1, keepdims=True)
        lse_ref[...] = jnp.broadcast_to(top + jnp.log2(total), lse_ref.shape)

    outs = (
        pltpu.VMEM((rows, keys), F32),
        pltpu.VMEM((rows, 128), F32),
        pltpu.VMEM((rows * heads + rows, width), F32),
    )
    operands = (index_query, index_keys, index_weight, after)
    return vmem_call(body, "index_forward", outs, operands, scalars=(query_pos,), limit=16 * MIB)


def index_signs(kl, index_query, index_keys, index_weight, groups):
    rows, heads, width = index_query.shape
    keys = index_keys.shape[0]
    tile = tile_of(keys, 256)
    own = rows // groups
    size = own * heads

    def body(kl_ref, query_ref, keys_ref, weight_ref, gate_ref, wiq_ref, kl_out):
        for row in range(rows):
            kl_out[row : row + 1, :] = jnp.full((1, 128), kl_ref[row], F32)
        flat = query_ref[...].reshape(rows * heads, width)
        for row, piece in weighted_columns(flat, weight_ref[...].T, rows, heads):
            wiq_ref[row // own, :, (row % own) * heads : (row % own + 1) * heads] = piece
        for at in range(0, keys, tile):
            logits = lax.dot_general(
                flat, keys_ref[at : at + tile, :], (((1,), (1,)), ((), ())), preferred_element_type=F32
            )
            for g in range(groups):
                gate_ref[g, :, at : at + tile] = logits[g * size : (g + 1) * size, :].astype(BF16)

    outs = (
        pltpu.VMEM((groups, size, keys), BF16),
        pltpu.VMEM((groups, width, size), BF16),
        pltpu.VMEM((rows, 128), F32),
    )
    operands = (index_query, index_keys, index_weight)
    return vmem_call(body, "index_signs", outs, operands, scalars=(kl,), limit=16 * MIB)


def other_signs(pack, index_keys, rows):
    keys, width = index_keys.shape
    heads = pack.shape[0] // rows - 1
    half = keys // 2
    tile = tile_of(half, 256)

    def body(pack_ref, keys_ref, gate_ref, wiq_ref):
        flat = pack_ref[: rows * heads, :].astype(BF16)
        columns = pack_ref[rows * heads :, :].T[:heads, :]
        for row, piece in weighted_columns(flat, columns, rows, heads):
            wiq_ref[:, row * heads : (row + 1) * heads] = piece
        _, core = head_place()
        for at in range(0, half, tile):
            span = pl.ds(pl.multiple_of(core * half + at, tile), tile)
            gate_ref[:, at : at + tile] = lax.dot_general(
                flat, keys_ref[span, :], (((1,), (1,)), ((), ())), preferred_element_type=F32
            ).astype(BF16)

    outs = (pltpu.VMEM((rows * heads, half), BF16), pltpu.VMEM((width, rows * heads), BF16))
    return vmem_call(body, "other_signs", outs, (pack, index_keys), limit=16 * MIB)


def main_scores(pos, query_t, keys_t):
    head_local, feature, queries = query_t.shape
    keys = keys_t.shape[1]
    per = 256 // queries if queries < 256 and head_local % (256 // queries) == 0 else 1
    lanes = per * queries
    blocks = head_local // per
    many = 4 if blocks % 4 == 0 else 1
    tile = tile_of(keys, 128)
    tiles = keys // tile
    mask_at = -(-feature // 128) * 128
    depth = mask_at + -(-queries // 128) * 128

    def body(pos_ref, query_ref, keys_ref, prob_ref, top_ref, stat_ref, key_rows, weights):
        step = pl.program_id(0)

        @pl.when(step == 0)
        def _():
            chunk = tile_of(keys, 512)
            for at in range(0, keys, chunk):
                key_rows[at : at + chunk, :feature] = keys_ref[:, at : at + chunk].T
            if mask_at > feature:
                key_rows[:, feature:mask_at] = jnp.zeros((keys, mask_at - feature), BF16)
                weights[:, feature:mask_at, :] = jnp.zeros((many, mask_at - feature, lanes), BF16)
            index = lax.axis_index("keys") * keys + lax.broadcasted_iota(jnp.int32, (keys, queries), 0)
            hidden = jnp.where(index <= pos_ref[...], 0.0, masked_fill).astype(BF16)
            key_rows[:, mask_at : mask_at + queries] = hidden
            at_row = lax.broadcasted_iota(jnp.int32, (depth - mask_at, lanes), 0)
            at_lane = lax.broadcasted_iota(jnp.int32, (depth - mask_at, lanes), 1)
            for k in range(many):
                weights[k, mask_at:, :] = jnp.where(at_row == at_lane % queries, 1.0, 0.0).astype(BF16)
            if depth > mask_at + queries:
                key_rows[:, mask_at + queries :] = jnp.zeros((keys, depth - mask_at - queries), BF16)

        for k in range(many):
            for i in range(per):
                weights[k, :feature, i * queries : (i + 1) * queries] = query_ref[k * per + i]
        for k in range(many):
            block = step * many + k
            tops, totals = [], []
            for t in range(tiles):
                span = slice(t * tile, (t + 1) * tile)
                scores = jnp.dot(key_rows[span, :], weights[k], preferred_element_type=F32)
                top = jnp.max(scores, axis=0, keepdims=True)
                prob = jnp.exp2((scores - top) * score_scale)
                top = top * score_scale
                tops.append(top)
                totals.append(jnp.sum(prob, axis=0, keepdims=True))
                prob_ref[block, span, :] = prob.astype(prob_ref.dtype)
                top_ref[block, t : t + 1, :] = top
            best = tops[0]
            for top in tops[1:]:
                best = jnp.maximum(best, top)
            total = sum(s * jnp.exp2(top - best) for s, top in zip(totals, tops))
            stat_ref[pl.ds(block, 1), :] = best + jnp.log2(total)

    return pl.pallas_call(
        body,
        grid=(blocks // many,),
        out_shape=(
            pltpu.VMEM((blocks, keys, lanes), F32),
            pltpu.VMEM((blocks, tiles, lanes), F32),
            pltpu.VMEM((blocks, lanes), F32),
        ),
        in_specs=[
            pl.BlockSpec((1, queries), lambda i: (0, 0)),
            pl.BlockSpec((many * per, feature, queries), lambda i: (i, 0, 0)),
            pl.BlockSpec((feature, keys), lambda i: (0, 0)),
        ],
        out_specs=(vmem_spec,) * 3,
        scratch_shapes=[pltpu.VMEM((keys, depth), BF16), pltpu.VMEM((many, depth, lanes), BF16)],
        compiler_params=pltpu.CompilerParams(vmem_limit_bytes=16 * MIB),
        name="main_scores",
    )(in_hbm(pos), in_hbm(query_t), in_hbm(keys_t))


def joined(stats):
    best = stats[0]
    for stat in stats[1:]:
        best = jnp.maximum(best, stat)
    return best + jnp.log2(sum(jnp.exp2(stat - best) for stat in stats))


def head_sum(probs, tops, stat, queries, row_local):
    blocks, keys, lanes = probs.shape
    tiles = tops.shape[1]
    tile = keys // tiles
    per = lanes // queries
    chips = queries // row_local // 2

    def body(prob_ref, top_ref, stat_ref, keep_ref, send_ref, summed):
        whole = stat_ref[...]
        factors = [jnp.exp2(top_ref[b] - whole[b : b + 1, :]) * (1.0 / H) for b in range(blocks)]
        for t in range(tiles):
            span = slice(t * tile, (t + 1) * tile)
            total = None
            for b in range(blocks):
                part = prob_ref[b, span, :].astype(F32) * factors[b][t : t + 1, :]
                for i in range(per):
                    piece = part[:, i * queries : (i + 1) * queries]
                    total = piece if total is None else total + piece
            summed[:, span] = total.T
        chip, core = head_place()
        for r in range(chips):
            first = (chip ^ r) * 2
            keep_ref[r] = rows_of(summed, (first + core) * row_local, row_local)
            send_ref[r] = rows_of(summed, (first + 1 - core) * row_local, row_local)

    half = pltpu.VMEM((chips, row_local, keys), F32)
    return vmem_call(
        body, "head_sum", (half, half), (probs, tops, stat), [pltpu.VMEM((queries, keys), F32)], cost=10**9
    )


def add_stacks(left, right):
    count = left.shape[0]

    def body(left_ref, right_ref, *outs):
        for r in range(count):
            outs[r][...] = left_ref[r] + right_ref[r]

    return vmem_call(
        body, "add_stacks", tuple(pltpu.VMEM(left.shape[1:], F32) for _ in range(count)), (left, right)
    )


def add_all(parts):
    count, width = parts[0].shape

    def body(*refs):
        total = refs[0][...]
        for ref in refs[1:-2]:
            total = total + ref[...]
        refs[-2][...] = total
        refs[-1][:count, :] = total
        refs[-1][count:, :] = jnp.zeros((16, width), F32)

    outs = (pltpu.VMEM((count, width), F32), pltpu.VMEM((count + 16, width), F32))
    return vmem_call(body, "add_all", outs, parts)


def stack_chips(parts):
    chunk, width = parts[0].shape

    def body(*refs):
        chip, _ = head_place()
        for r, ref in enumerate(refs[:-1]):
            refs[-1][pl.ds(pl.multiple_of((chip ^ r) * chunk, chunk), chunk), :] = ref[:chunk, :]

    return vmem_call(body, "stack_chips", pltpu.VMEM((len(parts) * chunk, width), F32), parts)


def join_first(left, right, below):
    blocks, lanes = left.shape
    rows = below.shape[0]

    def body(left_ref, right_ref, below_ref, out_ref):
        out_ref[:blocks, :] = joined([left_ref[...], right_ref[...]])
        out_ref[blocks:, :] = jnp.concatenate([below_ref[...]] * (lanes // 128), axis=1)

    return vmem_call(body, "join_first", pltpu.VMEM((blocks + rows, lanes), F32), (left, right, below))


def join_more(left, right, blocks):
    count, lanes = left.shape

    def body(left_ref, right_ref, main_ref, index_ref):
        both = joined([left_ref[...], right_ref[...]])
        main_ref[...] = both[:blocks, :]
        index_ref[...] = both[blocks:, :128]

    outs = (pltpu.VMEM((blocks, lanes), F32), pltpu.VMEM((count - blocks, 128), F32))
    return vmem_call(body, "join_more", outs, (left, right))


def join_pair(left, right):
    def body(left_ref, right_ref, out_ref):
        out_ref[...] = joined([left_ref[...], right_ref[...]])

    return vmem_call(body, "join_pair", pltpu.VMEM(left.shape, F32), (left, right))


def group_order(groups):
    return [*range(1, groups, 2), *range(0, groups, 2)]


def fill_slopes(delta_ref, gate_ref, slope_ref, order, z):
    own, keys = delta_ref.shape[1:]
    size = gate_ref.shape[1]
    heads = size // own
    for n, r in enumerate(order):
        lines = delta_ref[z ^ r]
        for i in range(own):
            line = jnp.broadcast_to(lines[i : i + 1, :], (heads, keys)).astype(BF16)
            signs = gate_ref[z ^ r, i * heads : (i + 1) * heads, :]
            at = n * size + i * heads
            slope_ref[at : at + heads, :] = jnp.where(signs > 0, line, jnp.zeros((), BF16))


def prepare(scores, index_stats, kl, index_query, index_weight, groups):
    rows, heads, width = index_query.shape
    own = rows // groups

    def body(score_ref, lse_ref, other_ref, kl_ref, query_ref, weight_ref, base_ref, column_ref, row_ref):
        whole = joined([lse_ref[:, :1], other_ref[:, :1]])
        base_ref[...] = kl_ref[:, :1] * jnp.exp2(score_ref[...] - whole)
        first = lax.axis_index("keys") * own
        columns = weight_ref[...].T
        lane = lax.broadcasted_iota(jnp.int32, (heads, rows), 1)
        for i in range(own):
            span = slice(i * heads, (i + 1) * heads)
            column = jnp.sum(jnp.where(lane == first + i, columns, 0.0), axis=1, keepdims=True)
            column_ref[span, :] = jnp.broadcast_to(column, (heads, width))
            row_ref[span, :] = query_ref[first + i].astype(F32)

    side = pltpu.VMEM((own * heads, width), F32)
    operands = (scores, *index_stats, kl, index_query, index_weight)
    return vmem_call(body, "prepare", (pltpu.VMEM(scores.shape, F32), side, side), operands)


def query_part(base, targets, kl, gate, index_keys):
    rows, keys = base.shape
    groups, size = gate.shape[:2]
    own = rows // groups
    width = index_keys.shape[1]
    half = keys // 2
    order = group_order(groups)[: groups // 2]
    many = len(order)

    def body(base_ref, kl_ref, gate_ref, keys_ref, *refs):
        target_refs, (send_ref, slope_ref, delta_ref, across_ref) = refs[: len(targets)], refs[len(targets) :]
        target = target_refs[0][...]
        for ref in target_refs[1:]:
            target = target + ref[...]
        delta = base_ref[...] - kl_ref[:, :1] * target
        for g in range(groups):
            delta_ref[g] = delta[g * own : (g + 1) * own, :]
        _, core = head_place()
        across_ref[...] = jnp.where(core == 0, delta[:, half:], delta[:, :half])
        fill_slopes(delta_ref, gate_ref, slope_ref, order, lax.axis_index("keys"))
        part = jnp.dot(slope_ref[...], keys_ref[...], preferred_element_type=F32)
        send_ref[...] = part.reshape(many, size, width)

    outs = (
        pltpu.VMEM((many, size, width), F32),
        pltpu.VMEM((many * size, keys), BF16),
        pltpu.VMEM((groups, own, keys), F32),
        pltpu.VMEM((rows, half), F32),
    )
    operands = (base, kl, gate, index_keys, *targets)
    return vmem_call(body, "query_part", outs, operands, limit=16 * MIB)


def query_rest(delta, gate, index_keys):
    groups, size, keys = gate.shape
    width = index_keys.shape[1]
    order = group_order(groups)[groups // 2 :]
    many = len(order)

    def body(delta_ref, gate_ref, keys_ref, keep_ref, slope_ref):
        fill_slopes(delta_ref, gate_ref, slope_ref, order, lax.axis_index("keys"))
        part = jnp.dot(slope_ref[...], keys_ref[...], preferred_element_type=F32)
        keep_ref[...] = part.reshape(many, size, width)

    outs = (pltpu.VMEM((many, size, width), F32), pltpu.VMEM((many * size, keys), BF16))
    return vmem_call(body, "query_rest", outs, (delta, gate, index_keys), limit=16 * MIB)


def key_part(slopes, wiq, other_delta, other_gate, other_wiq, chips):
    groups, width, size = wiq.shape
    rows, half = other_delta.shape
    count = other_gate.shape[0]
    heads = count // rows
    chunk = half // chips
    first = slopes[0].shape[0]

    def body(odd_ref, even_ref, wiq_ref, delta_ref, gate_ref, other_ref, *refs):
        outs, (wiq_rows, other_slopes) = refs[:chips], refs[chips:]
        z = lax.axis_index("keys")
        for n, r in enumerate(group_order(groups)):
            wiq_rows[:, n * size : (n + 1) * size] = wiq_ref[z ^ r]
        for row in range(rows):
            span = slice(row * heads, (row + 1) * heads)
            line = jnp.broadcast_to(delta_ref[row : row + 1, :], (heads, half)).astype(BF16)
            other_slopes[span, :] = jnp.where(gate_ref[span, :] > 0, line, jnp.zeros((), BF16))
        chip, core = head_place()
        for n, out_ref in enumerate(outs):
            at = pl.multiple_of((chip ^ n) * chunk, chunk)
            here = pl.ds(pl.multiple_of(core * half + at, chunk), chunk)
            total = jnp.dot(wiq_rows[:, :first], odd_ref[:, here], preferred_element_type=F32)
            total += jnp.dot(wiq_rows[:, first:], even_ref[:, here], preferred_element_type=F32)
            total += jnp.dot(other_ref[...], other_slopes[:, pl.ds(at, chunk)], preferred_element_type=F32)
            out_ref[...] = total.T

    outs = tuple(pltpu.VMEM((chunk, width), F32) for _ in range(chips))
    scratch = [pltpu.VMEM((width, count), BF16), pltpu.VMEM((count, half), BF16)]
    operands = (*slopes, wiq, other_delta, other_gate, other_wiq)
    return vmem_call(body, "key_part", outs, operands, scratch, limit=16 * MIB)


def add_halve(left, right):
    count = left.shape[0]

    def body(left_ref, right_ref, even_ref, odd_ref):
        for n in range(count):
            (odd_ref if n % 2 else even_ref)[n // 2] = left_ref[n] + right_ref[n]

    side = pltpu.VMEM((count // 2, *left.shape[1:]), F32)
    return vmem_call(body, "add_halve", (side, side), (left, right))


def own_rows(left, right, column, row, heads):
    size, width = column.shape
    own = size // heads
    extra = -(-own // 8) * 8

    def body(left_ref, right_ref, column_ref, row_ref, out_ref):
        total = left_ref[0] + right_ref[0]
        out_ref[:size, :] = total * column_ref[...]
        summed = jnp.sum(total * row_ref[...], axis=1, keepdims=True)
        for i in range(own):
            out_ref[size + i : size + i + 1, :] = jnp.concatenate(
                [summed[i * heads : (i + 1) * heads, :].T, jnp.zeros((1, width - heads), F32)], axis=1
            )
        if extra > own:
            out_ref[size + own :, :] = jnp.zeros((extra - own, width), F32)

    out = pltpu.VMEM((size + extra, width), F32)
    return vmem_call(body, "own_rows", out, (left, right, column, row), cost=LONG)


def gather_weights(pieces, rows, heads):
    own = rows // len(pieces)
    size = own * heads
    order = list(pieces)

    def body(*refs):
        z = lax.axis_index("keys")
        for r, ref in zip(order, refs):
            refs[-1][pl.ds((z ^ r) * own, own), :] = ref[size : size + own, :heads]

    out = pltpu.VMEM((rows, heads), F32)
    return vmem_call(body, "gather_weights", out, list(pieces.values()), cost=LONG)


def place_all(pieces, weights, mine, other):
    rows, heads = weights.shape
    size = rows // len(pieces) * heads
    order = list(pieces)
    count = len(order)
    half, width = mine.shape

    def body(weight_ref, mine_ref, other_ref, *refs):
        piece_refs, (query_out, key_out, weight_out, sems) = refs[:count], refs[count:]
        z = lax.axis_index("keys")
        _, core = head_place()
        pairs = [(weight_ref, weight_out)]
        for r, ref in zip(order, piece_refs):
            at = pl.multiple_of((z ^ r) * size, size)
            pairs.append((ref.at[:size], query_out.at[pl.ds(at, size)]))
        for ref, side in ((mine_ref, core), (other_ref, 1 - core)):
            pairs.append((ref, key_out.at[pl.ds(pl.multiple_of(side * half, half), half)]))
        copies = [pltpu.make_async_copy(*pair, sems.at[n]) for n, pair in enumerate(pairs)]
        for copy in copies:
            copy.start()
        for copy in copies:
            copy.wait()

    query, key, weight = vmem_call(
        body,
        "place_all",
        (
            jax.ShapeDtypeStruct((rows * heads, width), F32),
            jax.ShapeDtypeStruct((2 * half, width), F32),
            jax.ShapeDtypeStruct((rows, heads), F32),
        ),
        (weights, mine, other, *pieces.values()),
        [pltpu.SemaphoreType.DMA((3 + count,))],
        out_specs=(any_spec,) * 3,
    )
    return query.reshape(rows, heads, width), key, weight


def shards(main_query, latent_keys, index_query, index_keys, index_weight, query_pos, kl_weight):
    queries = main_query.shape[0]
    row_local, index_heads, _ = index_query.shape
    head_devices = lax.axis_size("heads")
    key_devices = lax.axis_size("keys")
    chips = head_devices // 2

    def to_keys(value, bits):
        return lax.ppermute(value, "keys", [(i, i ^ bits) for i in range(key_devices)])

    def to_heads(value, bits):
        return lax.ppermute(value, "heads", [(i, i ^ bits) for i in range(head_devices)])

    chip_order = list(reversed(range(1, chips)))
    key_order = [key_devices - 1] + list(range(1, key_devices - 1))

    probs, tops, stat = main_scores(query_pos[None, :], main_query.transpose(1, 2, 0), latent_keys.T)
    scores, index_lse, pack = index_forward(query_pos, index_query, index_keys, index_weight, stat)
    blocks = stat.shape[0]
    both = join_first(stat, to_keys(stat, 1), index_lse)
    both, signs_query = lax.optimization_barrier((both, index_query))
    bits = 2
    while bits < key_devices // 2:
        both = join_pair(both, to_keys(both, bits))
        bits *= 2
    gate, wiq, kl = index_signs(kl_weight, signs_query, index_keys, index_weight, key_devices)
    stat, index_lse = join_more(both, to_keys(both, bits), blocks)
    stat, gate = lax.optimization_barrier((stat, gate))
    keep, send = head_sum(probs, tops, stat, queries, row_local)
    index_lse, send, index_query, pack = lax.optimization_barrier((index_lse, send, index_query, pack))
    sums = add_stacks(keep, to_heads(send, 1))
    targets = [sums[0]] + [to_heads(sums[r], 2 * r) for r in chip_order]
    other_gate, other_wiq = other_signs(to_heads(pack, 1), index_keys, row_local)
    index_stats = (index_lse, to_keys(index_lse, 1))
    other_gate, gate = lax.optimization_barrier((other_gate, gate))
    base, own_column, own_query = prepare(scores, index_stats, kl, index_query, index_weight, key_devices)
    odd, odd_slopes, delta, across = query_part(base, targets, kl, gate, index_keys)
    even, even_slopes = query_rest(delta, gate, index_keys)
    slopes = (odd_slopes, even_slopes)

    bits, other_odd = 1, to_keys(odd, 1)
    parts = key_part(slopes, wiq, to_heads(across, 1), other_gate, other_wiq, chips)
    key_own, key_wide = add_all([parts[0]] + [to_heads(parts[r], 2 * r) for r in [*range(2, chips), 1]])
    while bits < key_devices // 2:
        even, odd = add_halve(even, other_odd)
        bits *= 2
        other_odd = to_keys(odd, bits)
    even, key_own = lax.optimization_barrier((even, key_own))
    query_own = own_rows(even, other_odd, own_column, own_query, index_heads)
    pieces = {0: query_own, **{r: to_keys(query_own, r) for r in key_order}}
    mine = {r: to_heads(key_own if r == chips - 1 else key_wide, 2 * r) for r in range(1, chips)}
    mine = [key_own] + [mine[r] for r in range(1, chips)]
    mine = stack_chips(mine)
    weights = gather_weights(pieces, row_local, index_heads)
    return place_all(pieces, weights, mine, to_heads(mine, 1))


def solution(mesh):
    placed = (
        P(None, "heads", None),
        P("keys", None),
        P("heads", None, None),
        P("keys", None),
        P("heads", None),
        P(),
        P("heads"),
    )
    return jax.shard_map(
        shards,
        mesh=mesh,
        in_specs=placed,
        out_specs=(P("heads", None, None), P("keys", None), P("heads", None)),
        check_vma=False,
    )
```

```python
import math

import jax
import jax.numpy as jnp
from jax import lax
from jax.experimental import pallas as pl
from jax.experimental.pallas import tpu as pltpu
from jax.sharding import PartitionSpec as P

H = 128

LOG2E = math.log2(math.e)
score_scale = 192.0 ** (-0.5) * LOG2E
masked_fill = -1e30

F32 = jnp.float32
BF16 = jnp.bfloat16
MIB = 1024 * 1024
LONG = 4 * 10**10

vmem_spec = pl.BlockSpec(memory_space=pltpu.VMEM)
smem_spec = pl.BlockSpec(memory_space=pltpu.SMEM)
any_spec = pl.BlockSpec(memory_space=pl.ANY)


def in_vmem(array):
    return pltpu.with_memory_space_constraint(array, pltpu.VMEM)


def in_hbm(array):
    return pltpu.with_memory_space_constraint(array, pltpu.HBM)


def vmem_call(
    body, name, outs, operands, scratch=(), out_specs=None, scalars=(), limit=12 * MIB, cost=0
):
    several = isinstance(outs, (tuple, list))
    if out_specs is None:
        out_specs = tuple(vmem_spec for _ in outs) if several else vmem_spec
    return pl.pallas_call(
        body,
        out_shape=outs,
        in_specs=[smem_spec] * len(scalars) + [vmem_spec] * len(operands),
        out_specs=out_specs,
        scratch_shapes=list(scratch),
        compiler_params=pltpu.CompilerParams(vmem_limit_bytes=limit),
        cost_estimate=pl.CostEstimate(flops=cost, bytes_accessed=0, transcendentals=0),
        name=name,
    )(*scalars, *[in_vmem(a) for a in operands])


def tile_of(extent, wanted):
    return wanted if extent % wanted == 0 else extent


def rows_of(ref, first, count):
    return ref[pl.ds(pl.multiple_of(first, count), count)]


def head_place():
    at = lax.axis_index("heads")
    return at // 2, at % 2


def weighted_columns(query_ref, columns, rows, heads):
    for row in range(rows):
        piece = query_ref[row * heads : (row + 1) * heads, :].astype(F32) * columns[:, row : row + 1]
        yield row, piece.T.astype(BF16)


def index_forward(query_pos, index_query, index_keys, index_weight, after):
    rows, heads, width = index_query.shape
    keys = index_keys.shape[0]
    tile = tile_of(keys, 256)

    def body(pos_ref, query_ref, keys_ref, weight_ref, _, score_ref, lse_ref, pack_ref):
        columns = weight_ref[...].T
        flat = query_ref[...].reshape(rows * heads, width)
        pack_ref[: rows * heads, :] = flat.astype(F32)
        pack_ref[rows * heads :, :] = jnp.concatenate(
            [weight_ref[...], jnp.zeros((rows, width - heads), F32)], axis=1
        )
        first_key = lax.axis_index("keys") * keys
        first_row = lax.axis_index("heads") * rows
        for at in range(0, keys, tile):
            logits = lax.dot_general(
                flat, keys_ref[at : at + tile, :], (((1,), (1,)), ((), ())), preferred_element_type=F32
            )
            index = first_key + at + lax.broadcasted_iota(jnp.int32, (1, tile), 1)
            for row in range(rows):
                active = jnp.maximum(logits[row * heads : (row + 1) * heads, :], 0.0)
                summed = jnp.sum(active * columns[:, row : row + 1], axis=0, keepdims=True)
                seen = index <= pos_ref[first_row + row]
                score_ref[row : row + 1, at : at + tile] = jnp.where(seen, summed * LOG2E, masked_fill)
        scores = score_ref[...]
        top = jnp.max(scores, axis=1, keepdims=True)
        total = jnp.sum(jnp.exp2(scores - top), axis=1, keepdims=True)
        lse_ref[...] = jnp.broadcast_to(top + jnp.log2(total), lse_ref.shape)

    outs = (
        pltpu.VMEM((rows, keys), F32),
        pltpu.VMEM((rows, 128), F32),
        pltpu.VMEM((rows * heads + rows, width), F32),
    )
    operands = (index_query, index_keys, index_weight, after)
    return vmem_call(body, "index_forward", outs, operands, scalars=(query_pos,), limit=16 * MIB)


def index_signs(kl, index_query, index_keys, index_weight, groups):
    rows, heads, width = index_query.shape
    keys = index_keys.shape[0]
    tile = tile_of(keys, 256)
    own = rows // groups
    size = own * heads

    def body(kl_ref, query_ref, keys_ref, weight_ref, gate_ref, wiq_ref, kl_out):
        for row in range(rows):
            kl_out[row : row + 1, :] = jnp.full((1, 128), kl_ref[row], F32)
        flat = query_ref[...].reshape(rows * heads, width)
        for row, piece in weighted_columns(flat, weight_ref[...].T, rows, heads):
            wiq_ref[row // own, :, (row % own) * heads : (row % own + 1) * heads] = piece
        for at in range(0, keys, tile):
            logits = lax.dot_general(
                flat, keys_ref[at : at + tile, :], (((1,), (1,)), ((), ())), preferred_element_type=F32
            )
            for g in range(groups):
                gate_ref[g, :, at : at + tile] = logits[g * size : (g + 1) * size, :].astype(BF16)

    outs = (
        pltpu.VMEM((groups, size, keys), BF16),
        pltpu.VMEM((groups, width, size), BF16),
        pltpu.VMEM((rows, 128), F32),
    )
    operands = (index_query, index_keys, index_weight)
    return vmem_call(body, "index_signs", outs, operands, scalars=(kl,), limit=16 * MIB)


def other_signs(pack, index_keys, rows):
    keys, width = index_keys.shape
    heads = pack.shape[0] // rows - 1
    half = keys // 2
    tile = tile_of(half, 256)

    def body(pack_ref, keys_ref, gate_ref, wiq_ref):
        flat = pack_ref[: rows * heads, :].astype(BF16)
        columns = pack_ref[rows * heads :, :].T[:heads, :]
        for row, piece in weighted_columns(flat, columns, rows, heads):
            wiq_ref[:, row * heads : (row + 1) * heads] = piece
        _, core = head_place()
        for at in range(0, half, tile):
            span = pl.ds(pl.multiple_of(core * half + at, tile), tile)
            gate_ref[:, at : at + tile] = lax.dot_general(
                flat, keys_ref[span, :], (((1,), (1,)), ((), ())), preferred_element_type=F32
            ).astype(BF16)

    outs = (pltpu.VMEM((rows * heads, half), BF16), pltpu.VMEM((width, rows * heads), BF16))
    return vmem_call(body, "other_signs", outs, (pack, index_keys), limit=16 * MIB)


def main_scores(pos, query_t, keys_t):
    head_local, feature, queries = query_t.shape
    keys = keys_t.shape[1]
    per = 256 // queries if queries < 256 and head_local % (256 // queries) == 0 else 1
    lanes = per * queries
    blocks = head_local // per
    many = 4 if blocks % 4 == 0 else 1
    tile = tile_of(keys, 128)
    tiles = keys // tile
    mask_at = -(-feature // 128) * 128
    depth = mask_at + -(-queries // 128) * 128

    def body(pos_ref, query_ref, keys_ref, prob_ref, top_ref, stat_ref, key_rows, weights):
        step = pl.program_id(0)

        @pl.when(step == 0)
        def _():
            chunk = tile_of(keys, 512)
            for at in range(0, keys, chunk):
                key_rows[at : at + chunk, :feature] = keys_ref[:, at : at + chunk].T
            if mask_at > feature:
                key_rows[:, feature:mask_at] = jnp.zeros((keys, mask_at - feature), BF16)
                weights[:, feature:mask_at, :] = jnp.zeros((many, mask_at - feature, lanes), BF16)
            index = lax.axis_index("keys") * keys + lax.broadcasted_iota(jnp.int32, (keys, queries), 0)
            hidden = jnp.where(index <= pos_ref[...], 0.0, masked_fill).astype(BF16)
            key_rows[:, mask_at : mask_at + queries] = hidden
            at_row = lax.broadcasted_iota(jnp.int32, (depth - mask_at, lanes), 0)
            at_lane = lax.broadcasted_iota(jnp.int32, (depth - mask_at, lanes), 1)
            for k in range(many):
                weights[k, mask_at:, :] = jnp.where(at_row == at_lane % queries, 1.0, 0.0).astype(BF16)
            if depth > mask_at + queries:
                key_rows[:, mask_at + queries :] = jnp.zeros((keys, depth - mask_at - queries), BF16)

        for k in range(many):
            for i in range(per):
                weights[k, :feature, i * queries : (i + 1) * queries] = query_ref[k * per + i]
        for k in range(many):
            block = step * many + k
            tops, totals = [], []
            for t in range(tiles):
                span = slice(t * tile, (t + 1) * tile)
                scores = jnp.dot(key_rows[span, :], weights[k], preferred_element_type=F32)
                top = jnp.max(scores, axis=0, keepdims=True)
                prob = jnp.exp2((scores - top) * score_scale)
                top = top * score_scale
                tops.append(top)
                totals.append(jnp.sum(prob, axis=0, keepdims=True))
                prob_ref[block, span, :] = prob.astype(prob_ref.dtype)
                top_ref[block, t : t + 1, :] = top
            best = tops[0]
            for top in tops[1:]:
                best = jnp.maximum(best, top)
            total = sum(s * jnp.exp2(top - best) for s, top in zip(totals, tops))
            stat_ref[pl.ds(block, 1), :] = best + jnp.log2(total)

    return pl.pallas_call(
        body,
        grid=(blocks // many,),
        out_shape=(
            pltpu.VMEM((blocks, keys, lanes), F32),
            pltpu.VMEM((blocks, tiles, lanes), F32),
            pltpu.VMEM((blocks, lanes), F32),
        ),
        in_specs=[
            pl.BlockSpec((1, queries), lambda i: (0, 0)),
            pl.BlockSpec((many * per, feature, queries), lambda i: (i, 0, 0)),
            pl.BlockSpec((feature, keys), lambda i: (0, 0)),
        ],
        out_specs=(vmem_spec,) * 3,
        scratch_shapes=[pltpu.VMEM((keys, depth), BF16), pltpu.VMEM((many, depth, lanes), BF16)],
        compiler_params=pltpu.CompilerParams(vmem_limit_bytes=16 * MIB),
        name="main_scores",
    )(in_hbm(pos), in_hbm(query_t), in_hbm(keys_t))


def joined(stats):
    best = stats[0]
    for stat in stats[1:]:
        best = jnp.maximum(best, stat)
    return best + jnp.log2(sum(jnp.exp2(stat - best) for stat in stats))


def head_sum(probs, tops, stat, queries, row_local):
    blocks, keys, lanes = probs.shape
    tiles = tops.shape[1]
    tile = keys // tiles
    per = lanes // queries
    chips = queries // row_local // 2

    def body(prob_ref, top_ref, stat_ref, keep_ref, send_ref, summed):
        whole = stat_ref[...]
        factors = [jnp.exp2(top_ref[b] - whole[b : b + 1, :]) * (1.0 / H) for b in range(blocks)]
        for t in range(tiles):
            span = slice(t * tile, (t + 1) * tile)
            total = None
            for b in range(blocks):
                part = prob_ref[b, span, :].astype(F32) * factors[b][t : t + 1, :]
                for i in range(per):
                    piece = part[:, i * queries : (i + 1) * queries]
                    total = piece if total is None else total + piece
            summed[:, span] = total.T
        chip, core = head_place()
        for r in range(chips):
            first = (chip ^ r) * 2
            keep_ref[r] = rows_of(summed, (first + core) * row_local, row_local)
            send_ref[r] = rows_of(summed, (first + 1 - core) * row_local, row_local)

    half = pltpu.VMEM((chips, row_local, keys), F32)
    return vmem_call(
        body, "head_sum", (half, half), (probs, tops, stat), [pltpu.VMEM((queries, keys), F32)], cost=10**9
    )


def add_stacks(left, right):
    count = left.shape[0]

    def body(left_ref, right_ref, *outs):
        for r in range(count):
            outs[r][...] = left_ref[r] + right_ref[r]

    return vmem_call(
        body, "add_stacks", tuple(pltpu.VMEM(left.shape[1:], F32) for _ in range(count)), (left, right)
    )


def add_all(parts):
    count, width = parts[0].shape

    def body(*refs):
        total = refs[0][...]
        for ref in refs[1:-2]:
            total = total + ref[...]
        refs[-2][...] = total
        refs[-1][:count, :] = total
        refs[-1][count:, :] = jnp.zeros((16, width), F32)

    outs = (pltpu.VMEM((count, width), F32), pltpu.VMEM((count + 16, width), F32))
    return vmem_call(body, "add_all", outs, parts)


def stack_chips(parts):
    chunk, width = parts[0].shape

    def body(*refs):
        chip, _ = head_place()
        for r, ref in enumerate(refs[:-1]):
            refs[-1][pl.ds(pl.multiple_of((chip ^ r) * chunk, chunk), chunk), :] = ref[:chunk, :]

    return vmem_call(body, "stack_chips", pltpu.VMEM((len(parts) * chunk, width), F32), parts)


def join_first(left, right, below):
    blocks, lanes = left.shape
    rows = below.shape[0]

    def body(left_ref, right_ref, below_ref, out_ref):
        out_ref[:blocks, :] = joined([left_ref[...], right_ref[...]])
        out_ref[blocks:, :] = jnp.concatenate([below_ref[...]] * (lanes // 128), axis=1)

    return vmem_call(body, "join_first", pltpu.VMEM((blocks + rows, lanes), F32), (left, right, below))


def join_more(left, right, blocks):
    count, lanes = left.shape

    def body(left_ref, right_ref, main_ref, index_ref):
        both = joined([left_ref[...], right_ref[...]])
        main_ref[...] = both[:blocks, :]
        index_ref[...] = both[blocks:, :128]

    outs = (pltpu.VMEM((blocks, lanes), F32), pltpu.VMEM((count - blocks, 128), F32))
    return vmem_call(body, "join_more", outs, (left, right))


def join_pair(left, right):
    def body(left_ref, right_ref, out_ref):
        out_ref[...] = joined([left_ref[...], right_ref[...]])

    return vmem_call(body, "join_pair", pltpu.VMEM(left.shape, F32), (left, right))


def group_order(groups):
    return [*range(1, groups, 2), *range(0, groups, 2)]


def fill_slopes(delta_ref, gate_ref, slope_ref, order, z):
    own, keys = delta_ref.shape[1:]
    size = gate_ref.shape[1]
    heads = size // own
    for n, r in enumerate(order):
        lines = delta_ref[z ^ r]
        for i in range(own):
            line = jnp.broadcast_to(lines[i : i + 1, :], (heads, keys)).astype(BF16)
            signs = gate_ref[z ^ r, i * heads : (i + 1) * heads, :]
            at = n * size + i * heads
            slope_ref[at : at + heads, :] = jnp.where(signs > 0, line, jnp.zeros((), BF16))


def prepare(scores, index_stats, kl, index_query, index_weight, groups):
    rows, heads, width = index_query.shape
    own = rows // groups

    def body(score_ref, lse_ref, other_ref, kl_ref, query_ref, weight_ref, base_ref, column_ref, row_ref):
        whole = joined([lse_ref[:, :1], other_ref[:, :1]])
        base_ref[...] = kl_ref[:, :1] * jnp.exp2(score_ref[...] - whole)
        first = lax.axis_index("keys") * own
        columns = weight_ref[...].T
        lane = lax.broadcasted_iota(jnp.int32, (heads, rows), 1)
        for i in range(own):
            span = slice(i * heads, (i + 1) * heads)
            column = jnp.sum(jnp.where(lane == first + i, columns, 0.0), axis=1, keepdims=True)
            column_ref[span, :] = jnp.broadcast_to(column, (heads, width))
            row_ref[span, :] = query_ref[first + i].astype(F32)

    side = pltpu.VMEM((own * heads, width), F32)
    operands = (scores, *index_stats, kl, index_query, index_weight)
    return vmem_call(body, "prepare", (pltpu.VMEM(scores.shape, F32), side, side), operands)


def query_part(base, targets, kl, gate, index_keys):
    rows, keys = base.shape
    groups, size = gate.shape[:2]
    own = rows // groups
    width = index_keys.shape[1]
    half = keys // 2
    order = group_order(groups)[: groups // 2]
    many = len(order)

    def body(base_ref, kl_ref, gate_ref, keys_ref, *refs):
        target_refs, (send_ref, slope_ref, delta_ref, across_ref) = refs[: len(targets)], refs[len(targets) :]
        target = target_refs[0][...]
        for ref in target_refs[1:]:
            target = target + ref[...]
        delta = base_ref[...] - kl_ref[:, :1] * target
        for g in range(groups):
            delta_ref[g] = delta[g * own : (g + 1) * own, :]
        _, core = head_place()
        across_ref[...] = jnp.where(core == 0, delta[:, half:], delta[:, :half])
        fill_slopes(delta_ref, gate_ref, slope_ref, order, lax.axis_index("keys"))
        part = jnp.dot(slope_ref[...], keys_ref[...], preferred_element_type=F32)
        send_ref[...] = part.reshape(many, size, width)

    outs = (
        pltpu.VMEM((many, size, width), F32),
        pltpu.VMEM((many * size, keys), BF16),
        pltpu.VMEM((groups, own, keys), F32),
        pltpu.VMEM((rows, half), F32),
    )
    operands = (base, kl, gate, index_keys, *targets)
    return vmem_call(body, "query_part", outs, operands, limit=16 * MIB)


def query_rest(delta, gate, index_keys):
    groups, size, keys = gate.shape
    width = index_keys.shape[1]
    order = group_order(groups)[groups // 2 :]
    many = len(order)

    def body(delta_ref, gate_ref, keys_ref, keep_ref, slope_ref):
        fill_slopes(delta_ref, gate_ref, slope_ref, order, lax.axis_index("keys"))
        part = jnp.dot(slope_ref[...], keys_ref[...], preferred_element_type=F32)
        keep_ref[...] = part.reshape(many, size, width)

    outs = (pltpu.VMEM((many, size, width), F32), pltpu.VMEM((many * size, keys), BF16))
    return vmem_call(body, "query_rest", outs, (delta, gate, index_keys), limit=16 * MIB)


def key_part(slopes, wiq, other_delta, other_gate, other_wiq, chips):
    groups, width, size = wiq.shape
    rows, half = other_delta.shape
    count = other_gate.shape[0]
    heads = count // rows
    chunk = half // chips
    first = slopes[0].shape[0]

    def body(odd_ref, even_ref, wiq_ref, delta_ref, gate_ref, other_ref, *refs):
        outs, (wiq_rows, other_slopes) = refs[:chips], refs[chips:]
        z = lax.axis_index("keys")
        for n, r in enumerate(group_order(groups)):
            wiq_rows[:, n * size : (n + 1) * size] = wiq_ref[z ^ r]
        for row in range(rows):
            span = slice(row * heads, (row + 1) * heads)
            line = jnp.broadcast_to(delta_ref[row : row + 1, :], (heads, half)).astype(BF16)
            other_slopes[span, :] = jnp.where(gate_ref[span, :] > 0, line, jnp.zeros((), BF16))
        chip, core = head_place()
        for n, out_ref in enumerate(outs):
            at = pl.multiple_of((chip ^ n) * chunk, chunk)
            here = pl.ds(pl.multiple_of(core * half + at, chunk), chunk)
            total = jnp.dot(wiq_rows[:, :first], odd_ref[:, here], preferred_element_type=F32)
            total += jnp.dot(wiq_rows[:, first:], even_ref[:, here], preferred_element_type=F32)
            total += jnp.dot(other_ref[...], other_slopes[:, pl.ds(at, chunk)], preferred_element_type=F32)
            out_ref[...] = total.T

    outs = tuple(pltpu.VMEM((chunk, width), F32) for _ in range(chips))
    scratch = [pltpu.VMEM((width, count), BF16), pltpu.VMEM((count, half), BF16)]
    operands = (*slopes, wiq, other_delta, other_gate, other_wiq)
    return vmem_call(body, "key_part", outs, operands, scratch, limit=16 * MIB)


def add_halve(left, right):
    count = left.shape[0]

    def body(left_ref, right_ref, even_ref, odd_ref):
        for n in range(count):
            (odd_ref if n % 2 else even_ref)[n // 2] = left_ref[n] + right_ref[n]

    side = pltpu.VMEM((count // 2, *left.shape[1:]), F32)
    return vmem_call(body, "add_halve", (side, side), (left, right))


def own_rows(left, right, column, row, heads):
    size, width = column.shape
    own = size // heads
    extra = -(-own // 8) * 8

    def body(left_ref, right_ref, column_ref, row_ref, out_ref):
        total = left_ref[0] + right_ref[0]
        out_ref[:size, :] = total * column_ref[...]
        summed = jnp.sum(total * row_ref[...], axis=1, keepdims=True)
        for i in range(own):
            out_ref[size + i : size + i + 1, :] = jnp.concatenate(
                [summed[i * heads : (i + 1) * heads, :].T, jnp.zeros((1, width - heads), F32)], axis=1
            )
        if extra > own:
            out_ref[size + own :, :] = jnp.zeros((extra - own, width), F32)

    out = pltpu.VMEM((size + extra, width), F32)
    return vmem_call(body, "own_rows", out, (left, right, column, row), cost=LONG)


def gather_weights(pieces, rows, heads):
    own = rows // len(pieces)
    size = own * heads
    order = list(pieces)

    def body(*refs):
        z = lax.axis_index("keys")
        for r, ref in zip(order, refs):
            refs[-1][pl.ds((z ^ r) * own, own), :] = ref[size : size + own, :heads]

    out = pltpu.VMEM((rows, heads), F32)
    return vmem_call(body, "gather_weights", out, list(pieces.values()), cost=LONG)


def place_all(pieces, weights, mine, other):
    rows, heads = weights.shape
    size = rows // len(pieces) * heads
    order = list(pieces)
    count = len(order)
    half, width = mine.shape

    def body(weight_ref, mine_ref, other_ref, *refs):
        piece_refs, (query_out, key_out, weight_out, sems) = refs[:count], refs[count:]
        z = lax.axis_index("keys")
        _, core = head_place()
        pairs = [(weight_ref, weight_out)]
        for r, ref in zip(order, piece_refs):
            at = pl.multiple_of((z ^ r) * size, size)
            pairs.append((ref.at[:size], query_out.at[pl.ds(at, size)]))
        for ref, side in ((mine_ref, core), (other_ref, 1 - core)):
            pairs.append((ref, key_out.at[pl.ds(pl.multiple_of(side * half, half), half)]))
        copies = [pltpu.make_async_copy(*pair, sems.at[n]) for n, pair in enumerate(pairs)]
        for copy in copies:
            copy.start()
        for copy in copies:
            copy.wait()

    query, key, weight = vmem_call(
        body,
        "place_all",
        (
            jax.ShapeDtypeStruct((rows * heads, width), F32),
            jax.ShapeDtypeStruct((2 * half, width), F32),
            jax.ShapeDtypeStruct((rows, heads), F32),
        ),
        (weights, mine, other, *pieces.values()),
        [pltpu.SemaphoreType.DMA((3 + count,))],
        out_specs=(any_spec,) * 3,
    )
    return query.reshape(rows, heads, width), key, weight


def shards(main_query, latent_keys, index_query, index_keys, index_weight, query_pos, kl_weight):
    queries = main_query.shape[0]
    row_local, index_heads, _ = index_query.shape
    head_devices = lax.axis_size("heads")
    key_devices = lax.axis_size("keys")
    chips = head_devices // 2

    def to_keys(value, bits):
        return lax.ppermute(value, "keys", [(i, i ^ bits) for i in range(key_devices)])

    def to_heads(value, bits):
        return lax.ppermute(value, "heads", [(i, i ^ bits) for i in range(head_devices)])

    chip_order = list(reversed(range(1, chips)))
    key_order = [key_devices - 1] + list(range(1, key_devices - 1))

    probs, tops, stat = main_scores(query_pos[None, :], main_query.transpose(1, 2, 0), latent_keys.T)
    scores, index_lse, pack = index_forward(query_pos, index_query, index_keys, index_weight, stat)
    blocks = stat.shape[0]
    both = join_first(stat, to_keys(stat, 1), index_lse)
    bits = 2
    while bits < key_devices // 2:
        both = join_pair(both, to_keys(both, bits))
        bits *= 2
    stat, index_lse = join_more(both, to_keys(both, bits), blocks)
    keep, send = head_sum(probs, tops, stat, queries, row_local)
    index_lse, send, index_query, pack = lax.optimization_barrier((index_lse, send, index_query, pack))
    sums = add_stacks(keep, to_heads(send, 1))
    targets = [sums[0]] + [to_heads(sums[r], 2 * r) for r in chip_order]
    gate, wiq, kl = index_signs(kl_weight, index_query, index_keys, index_weight, key_devices)
    other_gate, other_wiq = other_signs(to_heads(pack, 1), index_keys, row_local)
    index_stats = (index_lse, to_keys(index_lse, 1))
    other_gate, gate = lax.optimization_barrier((other_gate, gate))
    base, own_column, own_query = prepare(scores, index_stats, kl, index_query, index_weight, key_devices)
    odd, odd_slopes, delta, across = query_part(base, targets, kl, gate, index_keys)
    even, even_slopes = query_rest(delta, gate, index_keys)
    slopes = (odd_slopes, even_slopes)

    bits, other_odd = 1, to_keys(odd, 1)
    parts = key_part(slopes, wiq, to_heads(across, 1), other_gate, other_wiq, chips)
    key_own, key_wide = add_all([parts[0]] + [to_heads(parts[r], 2 * r) for r in [*range(2, chips), 1]])
    while bits < key_devices // 2:
        even, odd = add_halve(even, other_odd)
        bits *= 2
        other_odd = to_keys(odd, bits)
    even, key_own = lax.optimization_barrier((even, key_own))
    query_own = own_rows(even, other_odd, own_column, own_query, index_heads)
    pieces = {0: query_own, **{r: to_keys(query_own, r) for r in key_order}}
    mine = {r: to_heads(key_own if r == chips - 1 else key_wide, 2 * r) for r in range(1, chips)}
    mine = [key_own] + [mine[r] for r in range(1, chips)]
    mine = stack_chips(mine)
    weights = gather_weights(pieces, row_local, index_heads)
    return place_all(pieces, weights, mine, to_heads(mine, 1))


def solution(mesh):
    placed = (
        P(None, "heads", None),
        P("keys", None),
        P("heads", None, None),
        P("keys", None),
        P("heads", None),
        P(),
        P("heads"),
    )
    return jax.shard_map(
        shards,
        mesh=mesh,
        in_specs=placed,
        out_specs=(P("heads", None, None), P("keys", None), P("heads", None)),
        check_vma=False,
    )
```
